32 devices in a mesh: freq: 4 (over z), brow: 2 (over x), bcol: 4 (over y, core).
Axes of the slice: x: 2, y: 2, z: 4, core: 2. Of those that a mesh axis runs over, the one named last changes fastest.
Arguments:
- voltages: bfloat16 [2, 1024, 94208], P(None, ('brow', 'bcol', 'freq')), may hold values from -6 to 6
- fir_taps: float32 [16, 4096], replicated, may hold values from -1.5 to 1.5
Outputs:
- visibilities: float32 [2, 128, 1024, 2, 4, 128], P(None, 'freq', 'brow', None, 'bcol')
The draws below stay inside these ranges and needn't reach their ends.
All inputs are finite; a program needn't handle non-finite values.
Results may differ from the reference program's by a relative error of at most 0.0036.
Values may be sent and summed in bfloat16 or wider, within the bound.
No kernel may reach another device: no remote copies, remote signals or barrier semaphores. Data moves between devices by JAX's collectives and lax.ppermute only.
A program may use at most 192 MiB of HBM per device.

```python
import jax
import jax.numpy as jnp
from jax import lax

CHANNELS = 4096
RADIX = 64
TAPS = 16
AVG = 32
FRAMES = 8
STREAMS = 1024
SAMPLES = 94208
COARSE = 128
BLOCK = 128
N_BROW = 2
N_BCOL = 4


def level_of(key, dims, shards, smallest, top_value):
    factor_of, own = 1.0, jax.random.fold_in(key, 6)
    for position, shards_of in shards:
        steps = jnp.exp(jax.random.uniform(jax.random.fold_in(own, position), (shards_of,), jnp.float32, smallest / len(shards), top_value / len(shards)))
        factor_of = factor_of * jnp.repeat(steps, dims[position] // shards_of).reshape([-1 if axis == position else 1 for axis in range(len(dims))])
    return factor_of


def scatter_about(rng, shape, deviation, bound, pieces=(), held_as=jnp.bfloat16):
    result = deviation * jax.random.normal(rng, shape, jnp.float32)
    if pieces:
        result = result * level_of(rng, shape, pieces, -0.22, 0.18)
    return jnp.clip(result, -bound, bound).astype(held_as)


def setup_inputs(seed: int = 0) -> dict:
    key_list = jax.random.split(jax.random.key(seed), 3)
    return {
        "voltages": scatter_about(key_list[0], (2, STREAMS, SAMPLES), 1.0, 6.0, ((1, 32),)),
        "fir_taps": scatter_about(key_list[1], (TAPS, CHANNELS), 0.25, 1.5, (), jnp.float32),
    }


def channelize(block, fir_taps):
    width = block.shape[1]
    frames = block.astype(jnp.float32).reshape(2, width, FRAMES + TAPS - 1, CHANNELS)
    filtered = jnp.zeros((2, width, FRAMES, CHANNELS), jnp.float32)
    for tap in range(TAPS):
        filtered = filtered + fir_taps[tap] * frames[:, :, tap:tap + FRAMES, :]
    spectrum = jnp.fft.fft(filtered[0] + 1j * filtered[1], axis=-1) / RADIX
    parts = jnp.stack([jnp.real(spectrum), jnp.imag(spectrum)])
    return jnp.transpose(parts, (0, 1, 3, 2)).astype(jnp.bfloat16)


def reference(voltages, fir_taps):
    blocks = voltages.reshape(2, STREAMS // 64, 64, SAMPLES).transpose(1, 0, 2, 3)
    spectra = lax.map(lambda block: channelize(block, fir_taps), blocks)
    spectra = spectra.transpose(1, 0, 2, 3, 4).reshape(2, STREAMS, COARSE, AVG * FRAMES)
    scale = 1.0 / (FRAMES * AVG)

    def coarse_channel(index):
        block = lax.dynamic_index_in_dim(spectra, index, 2, keepdims=False)
        left = jnp.concatenate([block[0], block[1]], axis=1)
        flipped = jnp.concatenate([-block[1], block[0]], axis=1)
        real_part = jnp.dot(left, left.T, preferred_element_type=jnp.float32)
        imag_part = jnp.dot(left, flipped.T, preferred_element_type=jnp.float32)
        return jnp.stack([real_part, imag_part]) * scale

    vis = lax.map(coarse_channel, jnp.arange(COARSE, dtype=jnp.int32))
    vis = vis.transpose(1, 0, 2, 3)
    return vis.reshape(2, COARSE, STREAMS, N_BROW, N_BCOL, BLOCK)
```

```python
import functools
import math

import jax
import jax.numpy as jnp
import numpy as np
from jax import lax
from jax.experimental import pallas as pl
from jax.experimental.pallas import tpu as pltpu
from jax.sharding import PartitionSpec as P

CHANNELS = 4096
TAPS = 16
AVG = 32
FRAMES = 8
COARSE = CHANNELS // AVG
FINE = FRAMES * AVG
TILE = 16
LANES = 128


def dft_table():
    index = np.arange(COARSE)
    angle = 2.0 * math.pi * (index[:, None] * index[None, :] % COARSE) / COARSE
    cosine, sine = np.cos(angle) / 64.0, np.sin(angle) / 64.0
    table = np.block([[cosine, sine], [-sine, cosine]]).astype(np.float32)
    high = table.astype(jnp.bfloat16)
    low = (table - high.astype(np.float32)).astype(jnp.bfloat16)
    return np.concatenate([high, high, low], axis=1)


def twiddles():
    angle = 2.0 * math.pi * np.arange(AVG)[:, None] * np.arange(LANES)[None, :] / CHANNELS
    return np.cos(angle).astype(np.float32), np.sin(angle).astype(np.float32)


def times(value, numerator, length):
    re, im = value
    numerator %= length
    if numerator == 0:
        return re, im
    if 4 * numerator == length:
        return im, -re
    if 2 * numerator == length:
        return -re, -im
    if 4 * numerator == 3 * length:
        return -im, re
    cosine = math.cos(2.0 * math.pi * numerator / length)
    sine = math.sin(2.0 * math.pi * numerator / length)
    if 8 * numerator == length:
        return (re + im) * cosine, (im - re) * cosine
    if 8 * numerator == 3 * length:
        return (im - re) * sine, (re + im) * -sine
    return re * cosine + im * sine, im * cosine - re * sine


def small_dft(values):
    length = len(values)
    if length == 1:
        return values
    even, odd = small_dft(values[0::2]), small_dft(values[1::2])
    odd = [times(value, k, length) for k, value in enumerate(odd)]
    return [(e[0] + o[0], e[1] + o[1]) for e, o in zip(even, odd)] + [
        (e[0] - o[0], e[1] - o[1]) for e, o in zip(even, odd)
    ]


def channelize_kernel(
    groups, z_ref, v_ref, taps_ref, cos_ref, sin_ref, table_ref, *refs
):
    outs, (filt, y_re, y_im, g_ref) = refs[:groups], refs[groups:]

    @pl.loop(0, CHANNELS // LANES)
    def _(j):
        lane = pl.multiple_of(j * LANES, LANES)
        taps = [
            jnp.broadcast_to(taps_ref[p : p + 1, pl.ds(lane, LANES)], (TILE, LANES))
            for p in range(TAPS)
        ]
        for c in range(2):
            total = [None] * FRAMES
            for f in range(FRAMES + TAPS - 1):
                v = v_ref[c, :, pl.ds(f * CHANNELS + lane, LANES)].astype(jnp.float32)
                for t in range(max(0, f - TAPS + 1), min(FRAMES, f + 1)):
                    term = taps[f - t] * v
                    total[t] = term if f == t else total[t] + term
                    if f - t == TAPS - 1:
                        filt[c, t, j] = total[t]

    @pl.loop(0, FRAMES)
    def _(t):
        for g in range(TILE // 8):
            rows = slice(8 * g, 8 * g + 8)
            first = []
            for j0 in range(4):
                part = small_dft(
                    [(filt[0, t, j, rows, :], filt[1, t, j, rows, :]) for j in range(j0, AVG, 4)]
                )
                first.append([times(value, j0 * ka, AVG) for ka, value in enumerate(part)])
            for ka in range(8):
                last = small_dft([first[j0][ka] for j0 in range(4)])
                for kb in range(4):
                    k = ka + 8 * kb
                    re, im = last[kb]
                    if k:
                        cosine, sine = cos_ref[k : k + 1, :], sin_ref[k : k + 1, :]
                        re, im = re * cosine + im * sine, im * cosine - re * sine
                    at = pl.ds(8 * g * FINE + t * AVG + k, 8, stride=FINE)
                    y_re[at, :] = re
                    y_im[at, :] = im

    @pl.loop(0, TILE)
    def _(s):
        at = pl.ds(pl.multiple_of(s * FINE, FINE), FINE)
        value = jnp.concatenate([y_re[at, :], y_im[at, :]], axis=1)
        high = value.astype(jnp.bfloat16)
        low = (value - high.astype(jnp.float32)).astype(jnp.bfloat16)
        spectrum = lax.dot_general(
            table_ref[...],
            jnp.concatenate([high, low, high], axis=1),
            (((1,), (1,)), ((), ())),
            preferred_element_type=jnp.float32,
        )
        for c in range(2):
            for h in range(FINE // LANES):
                g_ref[2 * c + h, pl.ds(s, COARSE, stride=TILE), :] = spectrum[
                    c * COARSE : (c + 1) * COARSE, h * LANES : (h + 1) * LANES
                ]

    width = COARSE // groups
    for d in range(groups):
        start = (z_ref[0] ^ d) * width

        @pl.loop(0, width)
        def _(q):
            at = pl.ds(pl.multiple_of((start + q) * TILE, TILE), TILE)
            outs[d][q] = jnp.concatenate(
                [g_ref[i, at, :] for i in range(4)], axis=1
            ).astype(jnp.bfloat16)


def channelize(voltages, fir_taps, tile, z, groups):
    samples = voltages.shape[2]
    cosine, sine = twiddles()
    table = dft_table()
    whole = lambda shape: pl.BlockSpec(shape, lambda i: (0,) * len(shape))
    piece = (COARSE // groups, TILE, 2 * FINE)
    return pl.pallas_call(
        functools.partial(channelize_kernel, groups),
        grid=(1,),
        in_specs=[
            pl.BlockSpec(memory_space=pltpu.SMEM),
            pl.BlockSpec((2, TILE, samples), lambda i: (0, tile, 0)),
            whole(fir_taps.shape),
            whole(cosine.shape),
            whole(sine.shape),
            whole(table.shape),
        ],
        out_specs=[whole(piece)] * groups,
        out_shape=[jax.ShapeDtypeStruct(piece, jnp.bfloat16)] * groups,
        scratch_shapes=[
            pltpu.VMEM((2, FRAMES, CHANNELS // LANES, TILE, LANES), jnp.float32),
            pltpu.VMEM((TILE * FINE, LANES), jnp.float32),
            pltpu.VMEM((TILE * FINE, LANES), jnp.float32),
            pltpu.VMEM((4, COARSE * TILE, LANES), jnp.float32),
        ],
        compiler_params=pltpu.CompilerParams(vmem_limit_bytes=48 << 20),
        cost_estimate=pl.CostEstimate(
            flops=16 * 10**9, bytes_accessed=10 * 10**6, transcendentals=0
        ),
        name="channelize",
    )(z, voltages, fir_taps, jnp.asarray(cosine), jnp.asarray(sine), jnp.asarray(table))


def correlate_kernel(batch, rows, cols, at_ref, *refs):
    pieces, (out_ref, left, right) = refs[:-3], refs[-3:]
    scale = 1.0 / FINE

    @pl.loop(0, batch)
    def _(q):
        for i, ref in enumerate(pieces):
            value = ref[q]
            size = value.shape[0]
            if i in rows:
                left[pl.ds(pl.multiple_of(at_ref[0, i], TILE), size), :] = value
            if i in cols:
                right[pl.ds(pl.multiple_of(at_ref[1, i], TILE), size), :] = value
        a, b = left[...], right[...]
        turned = jnp.concatenate([-b[:, FINE:], b[:, :FINE]], axis=1)
        for c, other in enumerate((b, turned)):
            product = scale * lax.dot_general(
                a, other, (((1,), (1,)), ((), ())), preferred_element_type=jnp.float32
            )
            parts = product.shape[1] // LANES
            for x in range(parts):
                out_ref[c, q, pl.ds(x, a.shape[0], stride=parts), :] = product[
                    :, x * LANES : (x + 1) * LANES
                ]


def correlate(pieces, places, row_count, col_count):
    coarse = pieces[0].shape[0]
    batch = 2
    at = jnp.stack(
        [jnp.stack([jnp.int32(0) if p[k] is None else p[k] for p in places]) for k in range(2)]
    )
    rows = {i for i, p in enumerate(places) if p[0] is not None}
    cols = {i for i, p in enumerate(places) if p[1] is not None}
    out_rows = row_count * col_count // LANES
    return pl.pallas_call(
        functools.partial(correlate_kernel, batch, rows, cols),
        grid=(coarse // batch,),
        in_specs=[pl.BlockSpec(memory_space=pltpu.SMEM)]
        + [pl.BlockSpec((batch,) + p.shape[1:], lambda i: (i, 0, 0)) for p in pieces],
        out_specs=pl.BlockSpec((2, batch, out_rows, LANES), lambda i: (0, i, 0, 0)),
        out_shape=jax.ShapeDtypeStruct((2, coarse, out_rows, LANES), jnp.float32),
        scratch_shapes=[
            pltpu.VMEM((row_count, 2 * FINE), jnp.bfloat16),
            pltpu.VMEM((col_count, 2 * FINE), jnp.bfloat16),
        ],
        compiler_params=pltpu.CompilerParams(vmem_limit_bytes=48 << 20),
        cost_estimate=pl.CostEstimate(
            flops=8 * coarse * row_count * col_count * FINE,
            bytes_accessed=8 * coarse * row_count * col_count,
            transcendentals=0,
        ),
        name="correlate",
    )(at, *pieces)


def swap(value, axis, d):
    return lax.ppermute(value, axis, [(i, i ^ d) for i in range(lax.axis_size(axis))])


def shards(voltages, fir_taps):
    groups = lax.axis_size("freq")
    z, x, b = (lax.axis_index(name) for name in ("freq", "brow", "bcol"))
    streams = voltages.shape[1]
    block = streams * groups
    pieces, places = [], []

    def exchange(value, at):
        over = swap(value, "bcol", 2)
        for e, part in enumerate((value, swap(value, "bcol", 1), over, swap(over, "bcol", 1))):
            pieces.append(part)
            places.append(((b ^ e) * block + at, x * block + at if e == 0 else None))
        pieces.append(swap(value, "brow", 1))
        places.append((None, (x ^ 1) * block + at))

    if streams % TILE == 0:
        for tile in range(streams // TILE):
            local = channelize(voltages, fir_taps, tile, z[None], groups)
            for d in range(groups):
                value = local[d] if d == 0 else swap(local[d], "freq", d)
                exchange(value, (z ^ d) * streams + tile * TILE)
    else:
        padded = jnp.pad(voltages, ((0, 0), (0, -streams % TILE), (0, 0)))
        zero = jnp.zeros((1,), jnp.int32)
        local = jnp.concatenate(
            [
                jnp.concatenate(channelize(padded, fir_taps, tile, zero, groups), axis=0)
                for tile in range(padded.shape[1] // TILE)
            ],
            axis=1,
        )[:, :streams]
        exchange(lax.all_to_all(local, "freq", 0, 1, tiled=True), 0)
    row_count, col_count = 4 * block, 2 * block
    result = correlate(pieces, places, row_count, col_count)
    return result.reshape(2, result.shape[1], row_count, 2, 1, block)


def solution(mesh):
    in_specs = (P(None, ("brow", "bcol", "freq"), None), P())
    out_specs = P(None, "freq", "brow", None, "bcol", None)
    return jax.shard_map(shards, mesh=mesh, in_specs=in_specs, out_specs=out_specs, check_vma=False)
```

```python
import functools
import math

import jax
import jax.numpy as jnp
import numpy as np
from jax import lax
from jax.experimental import pallas as pl
from jax.experimental.pallas import tpu as pltpu
from jax.sharding import PartitionSpec as P

CHANNELS = 4096
TAPS = 16
AVG = 32
FRAMES = 8
COARSE = CHANNELS // AVG
FINE = FRAMES * AVG
TILE = 16
LANES = 128
PITCH = TILE + 1
VMEM = 60 << 20
AHEAD = 3


def dft_table():
    index = np.arange(COARSE)
    angle = 2.0 * math.pi * (index[:, None] * index[None, :] % COARSE) / COARSE
    cosine, sine = np.cos(angle) / 64.0, np.sin(angle) / 64.0
    table = np.block([[cosine, sine], [-sine, cosine]]).astype(np.float32)
    high = table.astype(jnp.bfloat16)
    low = (table - high.astype(np.float32)).astype(jnp.bfloat16)
    return np.concatenate([high, high, low], axis=1)


def twiddles():
    angle = 2.0 * math.pi * np.arange(AVG)[:, None] * np.arange(LANES)[None, :] / CHANNELS
    return np.cos(angle).astype(np.float32), np.sin(angle).astype(np.float32)


def times(value, numerator, length):
    re, im = value
    numerator %= length
    if numerator == 0:
        return re, im
    if 4 * numerator == length:
        return im, -re
    if 2 * numerator == length:
        return -re, -im
    if 4 * numerator == 3 * length:
        return -im, re
    cosine = math.cos(2.0 * math.pi * numerator / length)
    sine = math.sin(2.0 * math.pi * numerator / length)
    if 8 * numerator == length:
        return (re + im) * cosine, (im - re) * cosine
    if 8 * numerator == 3 * length:
        return (im - re) * sine, (re + im) * -sine
    return re * cosine + im * sine, im * cosine - re * sine


def small_dft(values):
    length = len(values)
    if length == 1:
        return values
    even, odd = small_dft(values[0::2]), small_dft(values[1::2])
    odd = [times(value, k, length) for k, value in enumerate(odd)]
    return [(e[0] + o[0], e[1] + o[1]) for e, o in zip(even, odd)] + [
        (e[0] - o[0], e[1] - o[1]) for e, o in zip(even, odd)
    ]


def channelize_kernel(pieces, z_ref, v_ref, taps_ref, cos_ref, sin_ref, table_ref, *refs):
    outs, (filt, g_ref) = refs[: len(pieces)], refs[len(pieces) :]

    @pl.loop(0, CHANNELS // LANES)
    def _(j):
        lane = pl.multiple_of(j * LANES, LANES)
        taps = [
            jnp.broadcast_to(taps_ref[p : p + 1, pl.ds(lane, LANES)], (TILE, LANES))
            for p in range(TAPS)
        ]
        for c in range(2):
            total = [None] * FRAMES
            for f in range(FRAMES + TAPS - 1):
                v = v_ref[c, :, pl.ds(f * CHANNELS + lane, LANES)].astype(jnp.float32)
                for t in range(max(0, f - TAPS + 1), min(FRAMES, f + 1)):
                    term = taps[f - t] * v
                    total[t] = term if f == t else total[t] + term
                    if f - t == TAPS - 1:
                        filt[c, j, pl.ds(t, TILE, stride=FRAMES), :] = total[t]

    @pl.loop(0, TILE, unroll=2)
    def _(s):
        rows = pl.ds(pl.multiple_of(s * FRAMES, FRAMES), FRAMES)
        first = []
        for j0 in range(4):
            part = small_dft([(filt[0, j, rows, :], filt[1, j, rows, :]) for j in range(j0, AVG, 4)])
            first.append([times(value, j0 * ka, AVG) for ka, value in enumerate(part)])
        turned = [None] * AVG
        for ka in range(8):
            last = small_dft([first[j0][ka] for j0 in range(4)])
            for kb in range(4):
                k = ka + 8 * kb
                re, im = last[kb]
                if k:
                    cosine, sine = cos_ref[k : k + 1, :], sin_ref[k : k + 1, :]
                    re, im = re * cosine + im * sine, im * cosine - re * sine
                turned[k] = jnp.concatenate([re, im], axis=1)
        value = jnp.concatenate(turned, axis=0)
        high = value.astype(jnp.bfloat16)
        low = (value - high.astype(jnp.float32)).astype(jnp.bfloat16)
        spectrum = lax.dot_general(
            table_ref[...],
            jnp.concatenate([high, low, high], axis=1),
            (((1,), (1,)), ((), ())),
            preferred_element_type=jnp.float32,
        )
        for c in range(2):
            for h in range(FINE // LANES):
                g_ref[2 * c + h, pl.ds(s, COARSE, stride=PITCH), :] = spectrum[
                    c * COARSE : (c + 1) * COARSE, h * LANES : (h + 1) * LANES
                ]

    for (d, start, count, width), out in zip(pieces, outs):
        base = (z_ref[0] ^ d) * width + start

        @pl.loop(0, count)
        def _(q):
            at = pl.ds((base + q) * PITCH, TILE)
            out[q] = jnp.concatenate([g_ref[i, at, :] for i in range(4)], axis=1).astype(jnp.bfloat16)


def channelize(voltages, fir_taps, tile, z, groups, cuts):
    samples = voltages.shape[2]
    cosine, sine = twiddles()
    table = dft_table()
    whole = lambda shape: pl.BlockSpec(shape, lambda i: (0,) * len(shape))
    pieces = [(d, start, count, COARSE // groups) for d in range(groups) for start, count in cuts]
    shapes = [(count, TILE, 2 * FINE) for _, _, count, _ in pieces]
    outs = pl.pallas_call(
        functools.partial(channelize_kernel, pieces),
        grid=(1,),
        in_specs=[
            pl.BlockSpec(memory_space=pltpu.SMEM),
            pl.BlockSpec((2, TILE, samples), lambda i: (0, tile, 0)),
            whole(fir_taps.shape),
            whole(cosine.shape),
            whole(sine.shape),
            whole(table.shape),
        ],
        out_specs=[whole(shape) for shape in shapes],
        out_shape=[jax.ShapeDtypeStruct(shape, jnp.bfloat16) for shape in shapes],
        scratch_shapes=[
            pltpu.VMEM((2, CHANNELS // LANES, TILE * FRAMES, LANES), jnp.float32),
            pltpu.VMEM((4, COARSE * PITCH, LANES), jnp.float32),
        ],
        compiler_params=pltpu.CompilerParams(vmem_limit_bytes=VMEM),
        cost_estimate=pl.CostEstimate(
            flops=14 * 10**9, bytes_accessed=10 * 10**6, transcendentals=0
        ),
        name="channelize",
    )(z, voltages, fir_taps, jnp.asarray(cosine), jnp.asarray(sine), jnp.asarray(table))
    return {(d, start): out for (d, start, _, _), out in zip(pieces, outs)}


def correlate_kernel(batch, kinds, at_ref, *refs):
    pieces, (out_ref, left, right) = refs[: len(kinds)], refs[-3:]
    scale = 1.0 / FINE

    @pl.loop(0, batch)
    def _(q):
        for i, (kind, ref) in enumerate(zip(kinds, pieces)):
            at = pl.multiple_of(at_ref[i], TILE)
            if kind == "rows":
                block = left.shape[0] // ref.shape[0]
                for e in range(ref.shape[0]):
                    left[pl.ds(e * block + at, ref.shape[2]), :] = ref[e, q]
            else:
                right[pl.ds(at, ref.shape[1]), :] = ref[q]
        a, b = left[...], right[...]
        turned = jnp.concatenate([-b[:, FINE:], b[:, :FINE]], axis=1)
        for c, other in enumerate((b, turned)):
            product = scale * lax.dot_general(
                a, other, (((1,), (1,)), ((), ())), preferred_element_type=jnp.float32
            )
            parts = product.shape[1] // LANES
            for x in range(parts):
                out_ref[c, q, pl.ds(x, a.shape[0], stride=parts), :] = product[
                    :, x * LANES : (x + 1) * LANES
                ]


def correlate(result, pieces, start, count, coarse, row_count, col_count):
    batch = 2
    at = jnp.stack([place for _, _, _, place in pieces])
    out_rows = row_count * col_count // LANES
    in_specs = [pl.BlockSpec(memory_space=pltpu.SMEM)]
    for kind, value, first, _ in pieces:
        skip = (start - first) // batch
        if kind == "rows":
            shape = (value.shape[0], batch) + value.shape[2:]
            in_specs.append(pl.BlockSpec(shape, lambda i, skip=skip: (0, i + skip, 0, 0)))
        else:
            shape = (batch,) + value.shape[1:]
            in_specs.append(pl.BlockSpec(shape, lambda i, skip=skip: (i + skip, 0, 0)))
    operands = [at] + [value for _, value, _, _ in pieces]
    aliases = {}
    if result is not None:
        aliases = {len(operands): 0}
        operands.append(result)
        in_specs.append(pl.BlockSpec(memory_space=pl.ANY))
    return pl.pallas_call(
        functools.partial(correlate_kernel, batch, [piece[0] for piece in pieces]),
        grid=(count // batch,),
        in_specs=in_specs,
        out_specs=pl.BlockSpec(
            (2, batch, out_rows, LANES), lambda i: (0, i + start // batch, 0, 0)
        ),
        out_shape=jax.ShapeDtypeStruct((2, coarse, out_rows, LANES), jnp.float32),
        scratch_shapes=[
            pltpu.VMEM((row_count, 2 * FINE), jnp.bfloat16),
            pltpu.VMEM((col_count, 2 * FINE), jnp.bfloat16),
        ],
        input_output_aliases=aliases,
        compiler_params=pltpu.CompilerParams(vmem_limit_bytes=VMEM),
        cost_estimate=pl.CostEstimate(
            flops=20 * count * row_count * col_count * FINE,
            bytes_accessed=8 * count * row_count * col_count,
            transcendentals=0,
        ),
        name="correlate",
    )(*operands)


def swap(value, axis, d):
    return lax.ppermute(value, axis, [(i, i ^ d) for i in range(lax.axis_size(axis))])


def shards(voltages, fir_taps):
    groups = lax.axis_size("freq")
    z, x = lax.axis_index("freq"), lax.axis_index("brow")
    streams = voltages.shape[1]
    block = streams * groups
    coarse = COARSE // groups
    pieces = []

    def exchange(value, first, at):
        pieces.append(("rows", lax.all_gather(value, "bcol"), first, at))
        pieces.append(("cols", value, first, x * block + at))
        pieces.append(("cols", swap(value, "brow", 1), first, (x ^ 1) * block + at))

    if streams % TILE == 0 and coarse % 4 == 0:
        tiles = streams // TILE
        sent = []
        for tile in range(tiles):
            half = coarse // 2
            cuts = [(0, coarse)] if tile < tiles - 1 else [(0, half), (half, half)]
            local = channelize(voltages, fir_taps, tile, z[None], groups, cuts)
            for first, _ in cuts:
                for d in range(groups):
                    value = local[d, first]
                    if d:
                        if len(sent) >= AHEAD:
                            value, _ = lax.optimization_barrier((value, sent[-AHEAD]))
                        value = swap(value, "freq", d)
                        sent.append(value)
                    exchange(value, first, (z ^ d) * streams + tile * TILE)
        cuts = [(0, half), (half, half)]
    else:
        padded = jnp.pad(voltages, ((0, 0), (0, -streams % TILE), (0, 0)))
        zero = jnp.zeros((1,), jnp.int32)
        cuts = [(0, coarse)]
        local = [
            channelize(padded, fir_taps, tile, zero, groups, cuts)
            for tile in range(padded.shape[1] // TILE)
        ]
        local = jnp.concatenate(
            [jnp.concatenate([part[d, 0] for d in range(groups)], axis=0) for part in local], axis=1
        )[:, :streams]
        exchange(lax.all_to_all(local, "freq", 0, 1, tiled=True), 0, jnp.int32(0))
    row_count, col_count = 4 * block, 2 * block
    result = None
    for start, count in cuts:
        used = [p for p in pieces if p[2] <= start < p[2] + p[1].shape[-3]]
        result = correlate(result, used, start, count, coarse, row_count, col_count)
    return result.reshape(2, coarse, row_count, 2, 1, block)


def solution(mesh):
    in_specs = (P(None, ("brow", "bcol", "freq"), None), P())
    out_specs = P(None, "freq", "brow", None, "bcol", None)
    return jax.shard_map(shards, mesh=mesh, in_specs=in_specs, out_specs=out_specs, check_vma=False)
```

```python
import functools
import math

import jax
import jax.numpy as jnp
import numpy as np
from jax import lax
from jax.experimental import pallas as pl
from jax.experimental.pallas import tpu as pltpu
from jax.sharding import PartitionSpec as P

CHANNELS = 4096
TAPS = 16
AVG = 32
FRAMES = 8
COARSE = CHANNELS // AVG
FINE = FRAMES * AVG
TILE = 16
LANES = 128
PITCH = TILE + 1
VMEM = 60 << 20


def dft_table():
    index = np.arange(COARSE)
    angle = 2.0 * math.pi * (index[:, None] * index[None, :] % COARSE) / COARSE
    cosine, sine = np.cos(angle) / 64.0, np.sin(angle) / 64.0
    table = np.block([[cosine, sine], [-sine, cosine]]).astype(np.float32)
    high = table.astype(jnp.bfloat16)
    low = (table - high.astype(np.float32)).astype(jnp.bfloat16)
    return np.concatenate([high, high, low], axis=1)


def twiddles():
    angle = 2.0 * math.pi * np.arange(AVG)[:, None] * np.arange(LANES)[None, :] / CHANNELS
    return np.cos(angle).astype(np.float32), np.sin(angle).astype(np.float32)


def times(value, numerator, length):
    re, im = value
    numerator %= length
    if numerator == 0:
        return re, im
    if 4 * numerator == length:
        return im, -re
    if 2 * numerator == length:
        return -re, -im
    if 4 * numerator == 3 * length:
        return -im, re
    cosine = math.cos(2.0 * math.pi * numerator / length)
    sine = math.sin(2.0 * math.pi * numerator / length)
    if 8 * numerator == length:
        return (re + im) * cosine, (im - re) * cosine
    if 8 * numerator == 3 * length:
        return (im - re) * sine, (re + im) * -sine
    return re * cosine + im * sine, im * cosine - re * sine


def small_dft(values):
    length = len(values)
    if length == 1:
        return values
    even, odd = small_dft(values[0::2]), small_dft(values[1::2])
    odd = [times(value, k, length) for k, value in enumerate(odd)]
    return [(e[0] + o[0], e[1] + o[1]) for e, o in zip(even, odd)] + [
        (e[0] - o[0], e[1] - o[1]) for e, o in zip(even, odd)
    ]


def channelize_kernel(pieces, z_ref, v_ref, taps_ref, cos_ref, sin_ref, table_ref, *refs):
    outs, (filt, g_ref) = refs[: len(pieces)], refs[len(pieces) :]

    @pl.loop(0, CHANNELS // LANES)
    def _(j):
        lane = pl.multiple_of(j * LANES, LANES)
        taps = [
            jnp.broadcast_to(taps_ref[p : p + 1, pl.ds(lane, LANES)], (TILE, LANES))
            for p in range(TAPS)
        ]
        for c in range(2):
            total = [None] * FRAMES
            for f in range(FRAMES + TAPS - 1):
                v = v_ref[c, :, pl.ds(f * CHANNELS + lane, LANES)].astype(jnp.float32)
                for t in range(max(0, f - TAPS + 1), min(FRAMES, f + 1)):
                    term = taps[f - t] * v
                    total[t] = term if f == t else total[t] + term
                    if f - t == TAPS - 1:
                        filt[c, j, pl.ds(t, TILE, stride=FRAMES), :] = total[t]

    @pl.loop(0, TILE, unroll=2)
    def _(s):
        rows = pl.ds(pl.multiple_of(s * FRAMES, FRAMES), FRAMES)
        first = []
        for j0 in range(4):
            part = small_dft([(filt[0, j, rows, :], filt[1, j, rows, :]) for j in range(j0, AVG, 4)])
            first.append([times(value, j0 * ka, AVG) for ka, value in enumerate(part)])
        turned = [None] * AVG
        for ka in range(8):
            last = small_dft([first[j0][ka] for j0 in range(4)])
            for kb in range(4):
                k = ka + 8 * kb
                re, im = last[kb]
                if k:
                    cosine, sine = cos_ref[k : k + 1, :], sin_ref[k : k + 1, :]
                    re, im = re * cosine + im * sine, im * cosine - re * sine
                turned[k] = jnp.concatenate([re, im], axis=1)
        value = jnp.concatenate(turned, axis=0)
        high = value.astype(jnp.bfloat16)
        low = (value - high.astype(jnp.float32)).astype(jnp.bfloat16)
        spectrum = lax.dot_general(
            table_ref[...],
            jnp.concatenate([high, low, high], axis=1),
            (((1,), (1,)), ((), ())),
            preferred_element_type=jnp.float32,
        )
        for c in range(2):
            for h in range(FINE // LANES):
                g_ref[2 * c + h, pl.ds(s, COARSE, stride=PITCH), :] = spectrum[
                    c * COARSE : (c + 1) * COARSE, h * LANES : (h + 1) * LANES
                ]

    for (d, start, count, width), out in zip(pieces, outs):
        base = (z_ref[0] ^ d) * width + start

        @pl.loop(0, count)
        def _(q):
            at = pl.ds((base + q) * PITCH, TILE)
            out[q] = jnp.concatenate([g_ref[i, at, :] for i in range(4)], axis=1).astype(jnp.bfloat16)


def channelize(voltages, fir_taps, tile, z, groups, cuts):
    samples = voltages.shape[2]
    cosine, sine = twiddles()
    table = dft_table()
    whole = lambda shape: pl.BlockSpec(shape, lambda i: (0,) * len(shape))
    pieces = [(d, start, count, COARSE // groups) for d in range(groups) for start, count in cuts]
    shapes = [(count, TILE, 2 * FINE) for _, _, count, _ in pieces]
    outs = pl.pallas_call(
        functools.partial(channelize_kernel, pieces),
        grid=(1,),
        in_specs=[
            pl.BlockSpec(memory_space=pltpu.SMEM),
            pl.BlockSpec((2, TILE, samples), lambda i: (0, tile, 0)),
            whole(fir_taps.shape),
            whole(cosine.shape),
            whole(sine.shape),
            whole(table.shape),
        ],
        out_specs=[whole(shape) for shape in shapes],
        out_shape=[jax.ShapeDtypeStruct(shape, jnp.bfloat16) for shape in shapes],
        scratch_shapes=[
            pltpu.VMEM((2, CHANNELS // LANES, TILE * FRAMES, LANES), jnp.float32),
            pltpu.VMEM((4, COARSE * PITCH, LANES), jnp.float32),
        ],
        compiler_params=pltpu.CompilerParams(vmem_limit_bytes=VMEM),
        cost_estimate=pl.CostEstimate(
            flops=14 * 10**9, bytes_accessed=10 * 10**6, transcendentals=0
        ),
        name="channelize",
    )(z, voltages, fir_taps, jnp.asarray(cosine), jnp.asarray(sine), jnp.asarray(table))
    return {(d, start): out for (d, start, _, _), out in zip(pieces, outs)}


def correlate_kernel(batch, places, at_ref, *refs):
    arrays, (out_ref, right) = refs[: len(places)], refs[-2:]
    scale = 1.0 / FINE
    used = [
        (ref, n, place)
        for ref, some in zip(arrays, places)
        for n, place in enumerate(some)
    ]
    for q in range(batch):
        for ref, n, (_, col) in used:
            if col is not None:
                at = pl.multiple_of(at_ref[col], TILE)
                right[q, pl.ds(at, ref.shape[2]), :] = ref[n, q]
        rows = [(ref[n, q], row) for ref, n, (row, _) in used if row is not None]
        a, b = jnp.concatenate([value for value, _ in rows], axis=0), right[q]
        turned = jnp.concatenate([-b[:, FINE:], b[:, :FINE]], axis=1)
        product = scale * lax.dot_general(
            a,
            jnp.concatenate([b, turned], axis=0),
            (((1,), (1,)), ((), ())),
            preferred_element_type=jnp.float32,
        )
        parts = b.shape[0] // LANES
        start = 0
        for value, row in rows:
            size = value.shape[0]
            at = pl.multiple_of(at_ref[row] * parts, TILE * parts)
            for c in range(2):
                for x in range(parts):
                    lane = (c * parts + x) * LANES
                    out_ref[c, q, pl.ds(at + x, size, stride=parts), :] = product[
                        start : start + size, lane : lane + LANES
                    ]
            start += size


def correlate(result, arrays, start, count, coarse, row_count, col_count):
    batch = 2
    out_rows = row_count * col_count // LANES
    in_specs = [pl.BlockSpec(memory_space=pltpu.SMEM)]
    at, places = [], []
    for value, first, wanted in arrays:
        skip = (start - first) // batch
        shape = (value.shape[0], batch) + value.shape[2:]
        in_specs.append(pl.BlockSpec(shape, lambda i, skip=skip: (0, i + skip, 0, 0)))
        places.append([])
        for pair in wanted:
            numbered = []
            for place in pair:
                numbered.append(None if place is None else len(at))
                at += [] if place is None else [place]
            places[-1].append(tuple(numbered))
    operands = [jnp.stack(at)] + [value for value, _, _ in arrays]
    aliases = {}
    if result is not None:
        aliases = {len(operands): 0}
        operands.append(result)
        in_specs.append(pl.BlockSpec(memory_space=pl.ANY))
    return pl.pallas_call(
        functools.partial(correlate_kernel, batch, places),
        grid=(count // batch,),
        in_specs=in_specs,
        out_specs=pl.BlockSpec(
            (2, batch, out_rows, LANES), lambda i: (0, i + start // batch, 0, 0)
        ),
        out_shape=jax.ShapeDtypeStruct((2, coarse, out_rows, LANES), jnp.float32),
        scratch_shapes=[pltpu.VMEM((batch, col_count, 2 * FINE), jnp.bfloat16)],
        input_output_aliases=aliases,
        compiler_params=pltpu.CompilerParams(vmem_limit_bytes=VMEM),
        cost_estimate=pl.CostEstimate(
            flops=20 * count * row_count * col_count * FINE,
            bytes_accessed=8 * count * row_count * col_count,
            transcendentals=0,
        ),
        name="correlate",
    )(*operands)


def swap(value, axis, d):
    return lax.ppermute(value, axis, [(i, i ^ d) for i in range(lax.axis_size(axis))])


def after(values, earlier):
    held = lax.optimization_barrier((tuple(values), tuple(earlier)))[0]
    return list(held)


def shards(voltages, fir_taps):
    groups = lax.axis_size("freq")
    z, x, b = (lax.axis_index(name) for name in ("freq", "brow", "bcol"))
    streams = voltages.shape[1]
    block = streams * groups
    coarse = COARSE // groups
    arrays = []

    def place(value, first, offsets, e=0, over=False):
        wanted = []
        for at in offsets:
            row = None if over else (b ^ e) * block + at
            col = (x ^ 1) * block + at if over else x * block + at if e == 0 else None
            wanted.append((row, col))
        return value, first, wanted

    def spread(state, arrived, first, offsets):
        mine, over_x, over_y, before = state
        pieces = jnp.stack(arrived)
        if mine is not None:
            pieces = after([pieces], [over_x, over_y])[0]
        state = pieces, swap(pieces, "brow", 1), swap(pieces, "bcol", 2), (first, offsets)
        arrays.append(place(state[1], first, offsets, over=True))
        arrays.append(place(pieces, first, offsets))
        arrays.append(place(state[2], first, offsets, 2))
        if mine is not None:
            inner(mine, over_y, before)
        return state

    def inner(mine, over_y, before):
        first, offsets = before
        other = swap(jnp.concatenate([mine, over_y], axis=0), "bcol", 1)
        wanted = place(None, first, offsets, 1)[2] + place(None, first, offsets, 3)[2]
        arrays.append((other, first, wanted))

    if streams % TILE == 0 and coarse % 4 == 0:
        tiles, half = streams // TILE, coarse // 2
        state, sent, waiting = (None,) * 4, [], ([], 0, [])
        for tile in range(tiles):
            last = tile == tiles - 1
            cuts = [(0, half), (half, half)] if last else [(0, coarse)]
            local = channelize(voltages, fir_taps, tile, z[None], groups, cuts)
            whole = [local[0, first] for first, _ in cuts]
            at = [(z ^ d) * streams + tile * TILE for d in range(groups)]
            arrived, first, offsets = waiting
            own = whole[0] if len(whole) == 1 else jnp.concatenate(whole, axis=0)
            waiting = arrived + [own], first, offsets + [at[0]]
            if last:
                batches = [(first, range(1, groups)) for first, _ in cuts]
            else:
                batches = [(0, range(1, groups // 2 + 1)), (0, range(groups // 2 + 1, groups))]
            for first, ds in batches:
                values = after([local[d, first] for d in ds], sent)
                sent = [swap(value, "freq", d) for value, d in zip(values, ds)]
                state = spread(state, *waiting)
                waiting = list(sent), first, [at[d] for d in ds]
        state = spread(state, *waiting)
        cuts = [(0, half), (half, half)]
    else:
        padded = jnp.pad(voltages, ((0, 0), (0, -streams % TILE), (0, 0)))
        zero = jnp.zeros((1,), jnp.int32)
        cuts = [(0, coarse)]
        local = [
            channelize(padded, fir_taps, tile, zero, groups, cuts)
            for tile in range(padded.shape[1] // TILE)
        ]
        local = jnp.concatenate(
            [jnp.concatenate([part[d, 0] for d in range(groups)], axis=0) for part in local], axis=1
        )[:, :streams]
        local = lax.all_to_all(local, "freq", 0, 1, tiled=True)
        state = spread((None,) * 4, [local], 0, [jnp.int32(0)])
    inner(state[0], state[2], state[3])
    row_count, col_count = 4 * block, 2 * block
    result = None
    for start, count in cuts:
        used = [a for a in arrays if a[1] <= start < a[1] + a[0].shape[1]]
        result = correlate(result, used, start, count, coarse, row_count, col_count)
    return result.reshape(2, coarse, row_count, 2, 1, block)


def solution(mesh):
    in_specs = (P(None, ("brow", "bcol", "freq"), None), P())
    out_specs = P(None, "freq", "brow", None, "bcol", None)
    return jax.shard_map(shards, mesh=mesh, in_specs=in_specs, out_specs=out_specs, check_vma=False)
```

```python
import functools
import math

import jax
import jax.numpy as jnp
import numpy as np
from jax import lax
from jax.experimental import pallas as pl
from jax.experimental.pallas import tpu as pltpu
from jax.sharding import PartitionSpec as P

CHANNELS = 4096
TAPS = 16
AVG = 32
FRAMES = 8
COARSE = CHANNELS // AVG
FINE = FRAMES * AVG
TILE = 16
LANES = 128
PITCH = TILE + 1
VMEM = 60 << 20


def dft_table():
    index = np.arange(COARSE)
    angle = 2.0 * math.pi * (index[:, None] * index[None, :] % COARSE) / COARSE
    cosine, sine = np.cos(angle) / 64.0, np.sin(angle) / 64.0
    table = np.block([[cosine, sine], [-sine, cosine]]).astype(np.float32)
    high = table.astype(jnp.bfloat16)
    low = (table - high.astype(np.float32)).astype(jnp.bfloat16)
    return np.concatenate([high, high, low], axis=1)


def twiddles():
    angle = 2.0 * math.pi * np.arange(AVG)[:, None] * np.arange(LANES)[None, :] / CHANNELS
    return np.cos(angle).astype(np.float32), np.sin(angle).astype(np.float32)


def times(value, numerator, length):
    re, im = value
    numerator %= length
    if numerator == 0:
        return re, im
    if 4 * numerator == length:
        return im, -re
    if 2 * numerator == length:
        return -re, -im
    if 4 * numerator == 3 * length:
        return -im, re
    cosine = math.cos(2.0 * math.pi * numerator / length)
    sine = math.sin(2.0 * math.pi * numerator / length)
    if 8 * numerator == length:
        return (re + im) * cosine, (im - re) * cosine
    if 8 * numerator == 3 * length:
        return (im - re) * sine, (re + im) * -sine
    return re * cosine + im * sine, im * cosine - re * sine


def small_dft(values):
    length = len(values)
    if length == 1:
        return values
    even, odd = small_dft(values[0::2]), small_dft(values[1::2])
    odd = [times(value, k, length) for k, value in enumerate(odd)]
    return [(e[0] + o[0], e[1] + o[1]) for e, o in zip(even, odd)] + [
        (e[0] - o[0], e[1] - o[1]) for e, o in zip(even, odd)
    ]


def channelize_kernel(pieces, z_ref, v_ref, taps_ref, cos_ref, sin_ref, table_ref, *refs):
    outs, (filt, g_ref) = refs[: len(pieces)], refs[len(pieces) :]

    @pl.loop(0, CHANNELS // LANES)
    def _(j):
        lane = pl.multiple_of(j * LANES, LANES)
        taps = [
            jnp.broadcast_to(taps_ref[p : p + 1, pl.ds(lane, LANES)], (TILE, LANES))
            for p in range(TAPS)
        ]
        for c in range(2):
            total = [None] * FRAMES
            for f in range(FRAMES + TAPS - 1):
                v = v_ref[c, :, pl.ds(f * CHANNELS + lane, LANES)].astype(jnp.float32)
                for t in range(max(0, f - TAPS + 1), min(FRAMES, f + 1)):
                    term = taps[f - t] * v
                    total[t] = term if f == t else total[t] + term
                    if f - t == TAPS - 1:
                        filt[c, j, pl.ds(t, TILE, stride=FRAMES), :] = total[t]

    @pl.loop(0, TILE, unroll=2)
    def _(s):
        rows = pl.ds(pl.multiple_of(s * FRAMES, FRAMES), FRAMES)
        first = []
        for j0 in range(4):
            part = small_dft([(filt[0, j, rows, :], filt[1, j, rows, :]) for j in range(j0, AVG, 4)])
            first.append([times(value, j0 * ka, AVG) for ka, value in enumerate(part)])
        turned = [None] * AVG
        for ka in range(8):
            last = small_dft([first[j0][ka] for j0 in range(4)])
            for kb in range(4):
                k = ka + 8 * kb
                re, im = last[kb]
                if k:
                    cosine, sine = cos_ref[k : k + 1, :], sin_ref[k : k + 1, :]
                    re, im = re * cosine + im * sine, im * cosine - re * sine
                turned[k] = jnp.concatenate([re, im], axis=1)
        value = jnp.concatenate(turned, axis=0)
        high = value.astype(jnp.bfloat16)
        low = (value - high.astype(jnp.float32)).astype(jnp.bfloat16)
        spectrum = lax.dot_general(
            table_ref[...],
            jnp.concatenate([high, low, high], axis=1),
            (((1,), (1,)), ((), ())),
            preferred_element_type=jnp.float32,
        )
        for c in range(2):
            for h in range(FINE // LANES):
                g_ref[2 * c + h, pl.ds(s, COARSE, stride=PITCH), :] = spectrum[
                    c * COARSE : (c + 1) * COARSE, h * LANES : (h + 1) * LANES
                ]

    for (d, start, count, width), out in zip(pieces, outs):
        base = (z_ref[0] ^ d) * width + start

        @pl.loop(0, count)
        def _(q):
            at = pl.ds((base + q) * PITCH, TILE)
            out[q] = jnp.concatenate([g_ref[i, at, :] for i in range(4)], axis=1).astype(jnp.bfloat16)


def channelize(voltages, fir_taps, tile, z, groups, cuts):
    samples = voltages.shape[2]
    cosine, sine = twiddles()
    table = dft_table()
    whole = lambda shape: pl.BlockSpec(shape, lambda i: (0,) * len(shape))
    pieces = [(d, start, count, COARSE // groups) for d, start, count in cuts]
    shapes = [(count, TILE, 2 * FINE) for _, _, count, _ in pieces]
    outs = pl.pallas_call(
        functools.partial(channelize_kernel, pieces),
        grid=(1,),
        in_specs=[
            pl.BlockSpec(memory_space=pltpu.SMEM),
            pl.BlockSpec((2, TILE, samples), lambda i: (0, tile, 0)),
            whole(fir_taps.shape),
            whole(cosine.shape),
            whole(sine.shape),
            whole(table.shape),
        ],
        out_specs=[whole(shape) for shape in shapes],
        out_shape=[jax.ShapeDtypeStruct(shape, jnp.bfloat16) for shape in shapes],
        scratch_shapes=[
            pltpu.VMEM((2, CHANNELS // LANES, TILE * FRAMES, LANES), jnp.float32),
            pltpu.VMEM((4, COARSE * PITCH, LANES), jnp.float32),
        ],
        compiler_params=pltpu.CompilerParams(vmem_limit_bytes=VMEM),
        cost_estimate=pl.CostEstimate(
            flops=14 * 10**9, bytes_accessed=10 * 10**6, transcendentals=0
        ),
        name="channelize",
    )(z, voltages, fir_taps, jnp.asarray(cosine), jnp.asarray(sine), jnp.asarray(table))
    return {(d, start): out for (d, start, _, _), out in zip(pieces, outs)}


def correlate_kernel(batch, joined, places, at_ref, *refs):
    arrays, (out_ref, right) = refs[: len(places)], refs[-2:]
    scale = 1.0 / FINE
    used = [
        (ref, n, place)
        for ref, some in zip(arrays, places)
        for n, place in enumerate(some)
    ]
    for q in range(batch):
        for ref, n, (_, col) in used:
            if col is not None:
                at = pl.multiple_of(at_ref[col], TILE)
                right[q, pl.ds(at, ref.shape[2]), :] = ref[n, q]
        rows = [(ref[n, q], row) for ref, n, (row, _) in used if row is not None]
        a, b = jnp.concatenate([value for value, _ in rows], axis=0), right[q]
        turned = jnp.concatenate([-b[:, FINE:], b[:, :FINE]], axis=1)
        others = [jnp.concatenate([b, turned], axis=0)] if joined else [b, turned]
        product = [
            scale
            * lax.dot_general(
                a, other, (((1,), (1,)), ((), ())), preferred_element_type=jnp.float32
            )
            for other in others
        ]
        product = product[0] if joined else jnp.concatenate(product, axis=1)
        parts = b.shape[0] // LANES
        start = 0
        for value, row in rows:
            size = value.shape[0]
            at = pl.multiple_of(at_ref[row] * parts, TILE * parts)
            for c in range(2):
                for x in range(parts):
                    lane = (c * parts + x) * LANES
                    out_ref[c, q, pl.ds(at + x, size, stride=parts), :] = product[
                        start : start + size, lane : lane + LANES
                    ]
            start += size


def correlate(result, arrays, start, count, coarse, row_count, col_count, batch, joined):
    out_rows = row_count * col_count // LANES
    in_specs = [pl.BlockSpec(memory_space=pltpu.SMEM)]
    at, places = [], []
    for value, first, wanted in arrays:
        skip = (start - first) // batch
        shape = (value.shape[0], batch) + value.shape[2:]
        in_specs.append(pl.BlockSpec(shape, lambda i, skip=skip: (0, i + skip, 0, 0)))
        places.append([])
        for pair in wanted:
            numbered = []
            for place in pair:
                numbered.append(None if place is None else len(at))
                at += [] if place is None else [place]
            places[-1].append(tuple(numbered))
    operands = [jnp.stack(at)] + [value for value, _, _ in arrays]
    aliases = {}
    if result is not None:
        aliases = {len(operands): 0}
        operands.append(result)
        in_specs.append(pl.BlockSpec(memory_space=pl.ANY))
    return pl.pallas_call(
        functools.partial(correlate_kernel, batch, joined, places),
        grid=(count // batch,),
        in_specs=in_specs,
        out_specs=pl.BlockSpec(
            (2, batch, out_rows, LANES), lambda i: (0, i + start // batch, 0, 0)
        ),
        out_shape=jax.ShapeDtypeStruct((2, coarse, out_rows, LANES), jnp.float32),
        scratch_shapes=[pltpu.VMEM((batch, col_count, 2 * FINE), jnp.bfloat16)],
        input_output_aliases=aliases,
        compiler_params=pltpu.CompilerParams(vmem_limit_bytes=VMEM),
        cost_estimate=pl.CostEstimate(
            flops=20 * count * row_count * col_count * FINE,
            bytes_accessed=8 * count * row_count * col_count,
            transcendentals=0,
        ),
        name="correlate",
    )(*operands)


def swap(value, axis, d):
    return lax.ppermute(value, axis, [(i, i ^ d) for i in range(lax.axis_size(axis))])


def after(values, earlier):
    held = lax.optimization_barrier((tuple(values), tuple(earlier)))[0]
    return list(held)


def shards(voltages, fir_taps):
    groups = lax.axis_size("freq")
    z, x, b = (lax.axis_index(name) for name in ("freq", "brow", "bcol"))
    streams = voltages.shape[1]
    block = streams * groups
    coarse = COARSE // groups
    half = coarse // 2
    arrays = []

    def place(value, first, offsets, e=0, over=False):
        wanted = []
        for at in offsets:
            row = None if over else (b ^ e) * block + at
            col = (x ^ 1) * block + at if over else x * block + at if e == 0 else None
            wanted.append((row, col))
        return value, first, wanted

    def spread(pieces, first, offsets, earlier):
        pieces = after([pieces], earlier)[0]
        over_x, over_y = swap(pieces, "brow", 1), swap(pieces, "bcol", 2)
        arrays.append(place(over_x, first, offsets, over=True))
        arrays.append(place(pieces, first, offsets))
        arrays.append(place(over_y, first, offsets, 2))
        return over_x, over_y

    def inner(pieces, over_y, first, offsets, earlier):
        both = after([jnp.concatenate([pieces, over_y], axis=0)], earlier)[0]
        other = swap(both, "bcol", 1)
        wanted = place(None, first, offsets, 1)[2] + place(None, first, offsets, 3)[2]
        arrays.append((other, first, wanted))
        return other

    def at(tile, d):
        return (z ^ d) * streams + tile * TILE

    if streams == 2 * TILE and groups == 4:

        def send(value, d, earlier):
            return swap(after([value], earlier)[0], "freq", d)

        local = channelize(voltages, fir_taps, 0, z[None], 4, [(d, 0, coarse) for d in range(4)])
        own_a = local[0, 0][None]
        a1, a2, a3 = (swap(local[d, 0], "freq", d) for d in (1, 2, 3))
        x0, y0 = spread(own_a, 0, [at(0, 0)], [])

        cuts = [(0, 0, coarse), (1, 0, coarse), (2, 0, coarse), (3, 0, half), (3, half, half)]
        local = channelize(voltages, fir_taps, 1, z[None], 4, cuts)
        pieces_1 = jnp.stack([a1, local[0, 0]])
        b2 = send(local[2, 0], 2, [a1])
        x1, y1 = spread(pieces_1, 0, [at(0, 1), at(1, 0)], [x0, y0])

        b1 = send(local[1, 0], 1, [a2, a3])
        core_0 = inner(own_a, y0, 0, [at(0, 0)], [a2, a3])
        pieces_2 = jnp.stack([a2, a3])
        x2, y2 = spread(pieces_2, 0, [at(0, 2), at(0, 3)], [x1, y1])

        b3 = send(local[3, 0], 3, [b1, core_0])
        c3 = send(local[3, half], 3, [b1, b2])
        core_1 = inner(pieces_1, y1, 0, [at(0, 1), at(1, 0)], [b1, b2, core_0])
        pieces_3 = jnp.stack([b1, b2])
        x3, y3 = spread(pieces_3, 0, [at(1, 1), at(1, 2)], [x2, y2])

        core_2 = inner(pieces_2, y2, 0, [at(0, 2), at(0, 3)], [b3, core_1])
        x4, y4 = spread(b3[None], 0, [at(1, 3)], [x3, y3, c3])
        core_3 = inner(pieces_3, y3, 0, [at(1, 1), at(1, 2)], [core_2])
        x5, y5 = spread(c3[None], half, [at(1, 3)], [x3, y3, core_2])
        core_4 = inner(b3[None], y4, 0, [at(1, 3)], [core_3])
        inner(c3[None], y5, half, [at(1, 3)], [core_4])
        steps = [(0, half, 4, False), (half, half, 2, True)]
    else:
        padded = jnp.pad(voltages, ((0, 0), (0, -streams % TILE), (0, 0)))
        zero = jnp.zeros((1,), jnp.int32)
        cuts = [(d, 0, coarse) for d in range(groups)]
        local = [
            channelize(padded, fir_taps, tile, zero, groups, cuts)
            for tile in range(padded.shape[1] // TILE)
        ]
        local = jnp.concatenate(
            [jnp.concatenate([part[d, 0] for d in range(groups)], axis=0) for part in local], axis=1
        )[:, :streams]
        pieces = lax.all_to_all(local, "freq", 0, 1, tiled=True)[None]
        start = [jnp.int32(0)]
        _, over_y = spread(pieces, 0, start, [])
        inner(pieces, over_y, 0, start, [])
        steps = [(0, coarse, 1, True)]
    row_count, col_count = 4 * block, 2 * block
    result = None
    for start, count, batch, joined in steps:
        used = [a for a in arrays if a[1] <= start < a[1] + a[0].shape[1]]
        result = correlate(
            result, used, start, count, coarse, row_count, col_count, batch, joined
        )
    return result.reshape(2, coarse, row_count, 2, 1, block)


def solution(mesh):
    in_specs = (P(None, ("brow", "bcol", "freq"), None), P())
    out_specs = P(None, "freq", "brow", None, "bcol", None)
    return jax.shard_map(shards, mesh=mesh, in_specs=in_specs, out_specs=out_specs, check_vma=False)
```

```python
import functools
import math

import jax
import jax.numpy as jnp
import numpy as np
from jax import lax
from jax.experimental import pallas as pl
from jax.experimental.pallas import tpu as pltpu
from jax.sharding import PartitionSpec as P

CHANNELS = 4096
TAPS = 16
AVG = 32
FRAMES = 8
COARSE = CHANNELS // AVG
FINE = FRAMES * AVG
TILE = 16
LANES = 128
PITCH = TILE + 1
VMEM = 60 << 20


def dft_table():
    index = np.arange(COARSE)
    angle = 2.0 * math.pi * (index[:, None] * index[None, :] % COARSE) / COARSE
    cosine, sine = np.cos(angle) / 64.0, np.sin(angle) / 64.0
    table = np.block([[cosine, sine], [-sine, cosine]]).astype(np.float32)
    high = table.astype(jnp.bfloat16)
    low = (table - high.astype(np.float32)).astype(jnp.bfloat16)
    return np.concatenate([high, high, low], axis=1)


def twiddles():
    angle = 2.0 * math.pi * np.arange(AVG)[:, None] * np.arange(LANES)[None, :] / CHANNELS
    return np.cos(angle).astype(np.float32), np.sin(angle).astype(np.float32)


def times(value, numerator, length):
    re, im = value
    numerator %= length
    if numerator == 0:
        return re, im
    if 4 * numerator == length:
        return im, -re
    if 2 * numerator == length:
        return -re, -im
    if 4 * numerator == 3 * length:
        return -im, re
    cosine = math.cos(2.0 * math.pi * numerator / length)
    sine = math.sin(2.0 * math.pi * numerator / length)
    if 8 * numerator == length:
        return (re + im) * cosine, (im - re) * cosine
    if 8 * numerator == 3 * length:
        return (im - re) * sine, (re + im) * -sine
    return re * cosine + im * sine, im * cosine - re * sine


def small_dft(values):
    length = len(values)
    if length == 1:
        return values
    even, odd = small_dft(values[0::2]), small_dft(values[1::2])
    odd = [times(value, k, length) for k, value in enumerate(odd)]
    return [(e[0] + o[0], e[1] + o[1]) for e, o in zip(even, odd)] + [
        (e[0] - o[0], e[1] - o[1]) for e, o in zip(even, odd)
    ]


def channelize_kernel(pieces, z_ref, v_ref, taps_ref, cos_ref, sin_ref, table_ref, *refs):
    outs, (filt, g_ref) = refs[: len(pieces)], refs[len(pieces) :]

    @pl.loop(0, CHANNELS // LANES)
    def _(j):
        lane = pl.multiple_of(j * LANES, LANES)
        taps = [
            jnp.broadcast_to(taps_ref[p : p + 1, pl.ds(lane, LANES)], (TILE, LANES))
            for p in range(TAPS)
        ]
        for c in range(2):
            total = [None] * FRAMES
            for f in range(FRAMES + TAPS - 1):
                v = v_ref[c, :, pl.ds(f * CHANNELS + lane, LANES)].astype(jnp.float32)
                for t in range(max(0, f - TAPS + 1), min(FRAMES, f + 1)):
                    term = taps[f - t] * v
                    total[t] = term if f == t else total[t] + term
                    if f - t == TAPS - 1:
                        filt[c, j, pl.ds(t, TILE, stride=FRAMES), :] = total[t]

    @pl.loop(0, TILE, unroll=2)
    def _(s):
        rows = pl.ds(pl.multiple_of(s * FRAMES, FRAMES), FRAMES)
        first = []
        for j0 in range(4):
            part = small_dft([(filt[0, j, rows, :], filt[1, j, rows, :]) for j in range(j0, AVG, 4)])
            first.append([times(value, j0 * ka, AVG) for ka, value in enumerate(part)])
        turned = [None] * AVG
        for ka in range(8):
            last = small_dft([first[j0][ka] for j0 in range(4)])
            for kb in range(4):
                k = ka + 8 * kb
                re, im = last[kb]
                if k:
                    cosine, sine = cos_ref[k : k + 1, :], sin_ref[k : k + 1, :]
                    re, im = re * cosine + im * sine, im * cosine - re * sine
                turned[k] = jnp.concatenate([re, im], axis=1)
        value = jnp.concatenate(turned, axis=0)
        high = value.astype(jnp.bfloat16)
        low = (value - high.astype(jnp.float32)).astype(jnp.bfloat16)
        spectrum = lax.dot_general(
            table_ref[...],
            jnp.concatenate([high, low, high], axis=1),
            (((1,), (1,)), ((), ())),
            preferred_element_type=jnp.float32,
        )
        for c in range(2):
            for h in range(FINE // LANES):
                g_ref[2 * c + h, pl.ds(s, COARSE, stride=PITCH), :] = spectrum[
                    c * COARSE : (c + 1) * COARSE, h * LANES : (h + 1) * LANES
                ]

    for (d, start, count, width), out in zip(pieces, outs):
        base = (z_ref[0] ^ d) * width + start

        @pl.loop(0, count)
        def _(q):
            at = pl.ds((base + q) * PITCH, TILE)
            out[q] = jnp.concatenate([g_ref[i, at, :] for i in range(4)], axis=1).astype(jnp.bfloat16)


def channelize(voltages, fir_taps, tile, z, groups, cuts):
    samples = voltages.shape[2]
    cosine, sine = twiddles()
    table = dft_table()
    whole = lambda shape: pl.BlockSpec(shape, lambda i: (0,) * len(shape))
    pieces = [(d, start, count, COARSE // groups) for d, start, count in cuts]
    shapes = [(count, TILE, 2 * FINE) for _, _, count, _ in pieces]
    outs = pl.pallas_call(
        functools.partial(channelize_kernel, pieces),
        grid=(1,),
        in_specs=[
            pl.BlockSpec(memory_space=pltpu.SMEM),
            pl.BlockSpec((2, TILE, samples), lambda i: (0, tile, 0)),
            whole(fir_taps.shape),
            whole(cosine.shape),
            whole(sine.shape),
            whole(table.shape),
        ],
        out_specs=[whole(shape) for shape in shapes],
        out_shape=[jax.ShapeDtypeStruct(shape, jnp.bfloat16) for shape in shapes],
        scratch_shapes=[
            pltpu.VMEM((2, CHANNELS // LANES, TILE * FRAMES, LANES), jnp.float32),
            pltpu.VMEM((4, COARSE * PITCH, LANES), jnp.float32),
        ],
        compiler_params=pltpu.CompilerParams(vmem_limit_bytes=VMEM),
        cost_estimate=pl.CostEstimate(
            flops=14 * 10**9, bytes_accessed=10 * 10**6, transcendentals=0
        ),
        name="channelize",
    )(z, voltages, fir_taps, jnp.asarray(cosine), jnp.asarray(sine), jnp.asarray(table))
    return {(d, start): out for (d, start, _, _), out in zip(pieces, outs)}


def correlate_kernel(batch, places, at_ref, *refs):
    pieces, (out_ref, right) = refs[: len(places)], refs[-2:]
    scale = 1.0 / FINE
    for q in range(batch):
        for ref, (_, col) in zip(pieces, places):
            if col is not None:
                at = pl.multiple_of(at_ref[col], TILE)
                right[q, pl.ds(at, ref.shape[1]), :] = ref[q]
        rows = [(ref[q], row) for ref, (row, _) in zip(pieces, places) if row is not None]
        a, b = jnp.concatenate([value for value, _ in rows], axis=0), right[q]
        turned = jnp.concatenate([-b[:, FINE:], b[:, :FINE]], axis=1)
        parts = b.shape[0] // LANES
        for c, other in enumerate((b, turned)):
            product = scale * lax.dot_general(
                a, other, (((1,), (1,)), ((), ())), preferred_element_type=jnp.float32
            )
            start = 0
            for value, row in rows:
                size = value.shape[0]
                at = pl.multiple_of(at_ref[row] * parts, TILE * parts)
                for x in range(parts):
                    out_ref[c, q, pl.ds(at + x, size, stride=parts), :] = product[
                        start : start + size, x * LANES : (x + 1) * LANES
                    ]
                start += size


def correlate(result, pieces, start, count, coarse, row_count, col_count, batch):
    out_rows = row_count * col_count // LANES
    in_specs = [pl.BlockSpec(memory_space=pltpu.SMEM)]
    at, places = [], []
    for value, skip, row, col in pieces:
        shape = (batch,) + value.shape[1:]
        in_specs.append(pl.BlockSpec(shape, lambda i, skip=skip // batch: (i + skip, 0, 0)))
        numbered = []
        for place in (row, col):
            numbered.append(None if place is None else len(at))
            at += [] if place is None else [place]
        places.append(numbered)
    operands = [jnp.stack(at)] + [piece[0] for piece in pieces]
    aliases = {}
    if result is not None:
        aliases = {len(operands): 0}
        operands.append(result)
        in_specs.append(pl.BlockSpec(memory_space=pl.ANY))
    return pl.pallas_call(
        functools.partial(correlate_kernel, batch, places),
        grid=(count // batch,),
        in_specs=in_specs,
        out_specs=pl.BlockSpec(
            (2, batch, out_rows, LANES), lambda i: (0, i + start // batch, 0, 0)
        ),
        out_shape=jax.ShapeDtypeStruct((2, coarse, out_rows, LANES), jnp.float32),
        scratch_shapes=[pltpu.VMEM((batch, col_count, 2 * FINE), jnp.bfloat16)],
        input_output_aliases=aliases,
        compiler_params=pltpu.CompilerParams(vmem_limit_bytes=VMEM),
        cost_estimate=pl.CostEstimate(
            flops=20 * count * row_count * col_count * FINE,
            bytes_accessed=8 * count * row_count * col_count,
            transcendentals=0,
        ),
        name="correlate",
    )(*operands)


def swap(value, axis, d):
    return lax.ppermute(value, axis, [(i, i ^ d) for i in range(lax.axis_size(axis))])


def shards(voltages, fir_taps):
    groups = lax.axis_size("freq")
    z, x, b = (lax.axis_index(name) for name in ("freq", "brow", "bcol"))
    streams = voltages.shape[1]
    block = streams * groups
    coarse = COARSE // groups
    known = []

    def note(value, parts, rows=None, cols=False):
        offset = 0
        for first, count, at in parts:
            row = None if rows is None else (b ^ rows) * block + at
            col = (x ^ 1) * block + at if rows is None else x * block + at if rows == 0 else None
            known.append((value, offset, first, count, row, col))
            offset += count

    def join(pieces):
        return jnp.concatenate([value for value, _ in pieces], axis=0)

    def parts_of(pieces):
        return [part for _, parts in pieces for part in parts]

    earlier = []

    def turn(over_freq, spread, inner):
        values = [piece[0] for piece, _ in over_freq]
        values += [join(spread)] if spread else []
        values += [join([piece for piece, _ in inner])] if inner else []
        if earlier:
            values = list(lax.optimization_barrier((tuple(values), tuple(earlier)))[0])
        earlier.clear()
        arrived, over_y = [], None
        for (piece, d), value in zip(over_freq, values):
            value = swap(value, "freq", d)
            earlier.append(value)
            arrived.append((value, piece[1]))
            note(value, piece[1], 0)
        values = values[len(over_freq) :]
        if spread:
            value, parts = values.pop(0), parts_of(spread)
            over_x, over_y = swap(value, "brow", 1), swap(value, "bcol", 2)
            earlier.extend([over_x, over_y])
            note(over_x, parts)
            note(over_y, parts, 2)
            over_y = over_y, parts
        if inner:
            value = swap(values.pop(0), "bcol", 1)
            earlier.append(value)
            offset = 0
            for (_, parts), e in inner:
                for first, count, at in parts:
                    known.append((value, offset, first, count, (b ^ e ^ 1) * block + at, None))
                    offset += count
        return arrived, over_y

    if streams == 2 * TILE and groups == 4:
        half = coarse // 2

        def made(tile, cuts):
            local = channelize(voltages, fir_taps, tile, z[None], groups, cuts)
            return {
                (d, first): (
                    local[d, first],
                    [(first, count, (z ^ d) * streams + tile * TILE)],
                )
                for d, first, count in cuts
            }

        p = made(0, [(d, 0, coarse) for d in range(4)])
        own_a = p[0, 0]
        note(own_a[0], own_a[1], 0)
        (a2, a1), y1 = turn([(p[2, 0], 2), (p[1, 0], 1)], [own_a], [(own_a, 0)])
        r = made(
            1, [(0, 0, coarse), (1, 0, coarse)] + [(d, at, half) for d in (2, 3) for at in (0, half)]
        )
        own_b = r[0, 0]
        note(own_b[0], own_b[1], 0)
        (a3, b1), y2 = turn([(p[3, 0], 3), (r[1, 0], 1)], [a1, a2], [(y1, 2), (a1, 0), (a2, 0)])
        (b2, b3), y3 = turn(
            [(r[2, 0], 2), (r[3, 0], 3)], [a3, own_b], [(y2, 2), (a3, 0), (own_b, 0)]
        )
        (c2, c3), y4 = turn(
            [(r[2, half], 2), (r[3, half], 3)],
            [b1, b2, b3],
            [(y3, 2), (b1, 0), (b2, 0), (b3, 0)],
        )
        _, y5 = turn([], [c2, c3], [(y4, 2), (c2, 0), (c3, 0)])
        turn([], [], [(y5, 2)])
        steps = [(0, half, 4), (half, half, 4)]
    else:
        padded = jnp.pad(voltages, ((0, 0), (0, -streams % TILE), (0, 0)))
        zero = jnp.zeros((1,), jnp.int32)
        cuts = [(d, 0, coarse) for d in range(groups)]
        local = [
            channelize(padded, fir_taps, tile, zero, groups, cuts)
            for tile in range(padded.shape[1] // TILE)
        ]
        local = jnp.concatenate(
            [jnp.concatenate([part[d, 0] for d in range(groups)], axis=0) for part in local], axis=1
        )[:, :streams]
        local = lax.all_to_all(local, "freq", 0, 1, tiled=True)
        own = local, [(0, coarse, jnp.int32(0))]
        note(own[0], own[1], 0)
        _, over_y = turn([], [own], [(own, 0)])
        turn([], [], [(over_y, 2)])
        steps = [(0, coarse, 1)]
    row_count, col_count = 4 * block, 2 * block
    result = None
    for start, count, batch in steps:
        used = [
            (value, offset + start - first, row, col)
            for value, offset, first, size, row, col in known
            if first <= start < first + size
        ]
        result = correlate(result, used, start, count, coarse, row_count, col_count, batch)
    return result.reshape(2, coarse, row_count, 2, 1, block)


def solution(mesh):
    in_specs = (P(None, ("brow", "bcol", "freq"), None), P())
    out_specs = P(None, "freq", "brow", None, "bcol", None)
    return jax.shard_map(shards, mesh=mesh, in_specs=in_specs, out_specs=out_specs, check_vma=False)
```

```python
import functools
import math

import jax
import jax.numpy as jnp
import numpy as np
from jax import lax
from jax.experimental import pallas as pl
from jax.experimental.pallas import tpu as pltpu
from jax.sharding import PartitionSpec as P

CHANNELS = 4096
TAPS = 16
AVG = 32
FRAMES = 8
COARSE = CHANNELS // AVG
FINE = FRAMES * AVG
TILE = 16
LANES = 128
PITCH = TILE + 1
VMEM = 60 << 20
CHUNKS = 4


def dft_table():
    index = np.arange(COARSE)
    angle = 2.0 * math.pi * (index[:, None] * index[None, :] % COARSE) / COARSE
    cosine, sine = np.cos(angle) / 64.0, np.sin(angle) / 64.0
    table = np.block([[cosine, sine], [-sine, cosine]]).astype(np.float32)
    high = table.astype(jnp.bfloat16)
    low = (table - high.astype(np.float32)).astype(jnp.bfloat16)
    return np.concatenate([high, high, low], axis=1)


def twiddles():
    angle = 2.0 * math.pi * np.arange(AVG)[:, None] * np.arange(LANES)[None, :] / CHANNELS
    return np.cos(angle).astype(np.float32), np.sin(angle).astype(np.float32)


def times(value, numerator, length):
    re, im = value
    numerator %= length
    if numerator == 0:
        return re, im
    if 4 * numerator == length:
        return im, -re
    if 2 * numerator == length:
        return -re, -im
    if 4 * numerator == 3 * length:
        return -im, re
    cosine = math.cos(2.0 * math.pi * numerator / length)
    sine = math.sin(2.0 * math.pi * numerator / length)
    if 8 * numerator == length:
        return (re + im) * cosine, (im - re) * cosine
    if 8 * numerator == 3 * length:
        return (im - re) * sine, (re + im) * -sine
    return re * cosine + im * sine, im * cosine - re * sine


def small_dft(values):
    length = len(values)
    if length == 1:
        return values
    even, odd = small_dft(values[0::2]), small_dft(values[1::2])
    odd = [times(value, k, length) for k, value in enumerate(odd)]
    return [(e[0] + o[0], e[1] + o[1]) for e, o in zip(even, odd)] + [
        (e[0] - o[0], e[1] - o[1]) for e, o in zip(even, odd)
    ]


def channelize_kernel(pieces, tile, pair, unroll, z_ref, v_hbm, taps_ref, cos_ref, sin_ref, table_ref, *refs):
    count = len(pieces)
    outs, stages = refs[:count], refs[count : 2 * count]
    v_ref, filt, g_ref, in_sem, out_sem = refs[2 * count :]
    chunk = CHANNELS // CHUNKS
    spans = FRAMES + TAPS - 1
    rows = pl.ds(tile * TILE, TILE)
    for k in range(CHUNKS):
        for f in range(spans):
            lanes = pl.ds(f * CHANNELS + k * chunk, chunk)
            pltpu.make_async_copy(
                v_hbm.at[:, rows, lanes], v_ref.at[:, :, lanes], in_sem.at[k]
            ).start()

    for k in range(CHUNKS):
        lanes = pl.ds(0, spans * chunk)
        pltpu.make_async_copy(v_hbm.at[:, rows, lanes], v_ref.at[:, :, lanes], in_sem.at[k]).wait()

        @pl.loop(k * (chunk // LANES), (k + 1) * (chunk // LANES))
        def _(j):
            lane = pl.multiple_of(j * LANES, LANES)
            taps = [
                jnp.broadcast_to(taps_ref[p : p + 1, pl.ds(lane, LANES)], (TILE, LANES))
                for p in range(TAPS)
            ]
            for c in range(2):
                total = [None] * FRAMES
                for f in range(spans):
                    v = v_ref[c, :, pl.ds(f * CHANNELS + lane, LANES)].astype(jnp.float32)
                    for t in range(max(0, f - TAPS + 1), min(FRAMES, f + 1)):
                        term = taps[f - t] * v
                        total[t] = term if f == t else total[t] + term
                        if f - t == TAPS - 1:
                            filt[c, j, pl.ds(t, TILE, stride=FRAMES), :] = total[t]

    def turned_fft(s):
        rows = pl.ds(pl.multiple_of(s * FRAMES, FRAMES), FRAMES)
        first = []
        for j0 in range(4):
            part = small_dft([(filt[0, j, rows, :], filt[1, j, rows, :]) for j in range(j0, AVG, 4)])
            first.append([times(value, j0 * ka, AVG) for ka, value in enumerate(part)])
        turned = [None] * AVG
        for ka in range(8):
            last = small_dft([first[j0][ka] for j0 in range(4)])
            for kb in range(4):
                k = ka + 8 * kb
                re, im = last[kb]
                if k:
                    cosine, sine = cos_ref[k : k + 1, :], sin_ref[k : k + 1, :]
                    re, im = re * cosine + im * sine, im * cosine - re * sine
                turned[k] = jnp.concatenate([re, im], axis=1)
        return turned

    @pl.loop(0, TILE // pair, unroll=unroll)
    def _(i):
        turned = []
        for s in range(pair):
            turned += turned_fft(i * pair + s)
        value = jnp.concatenate(turned, axis=0)
        high = value.astype(jnp.bfloat16)
        low = (value - high.astype(jnp.float32)).astype(jnp.bfloat16)
        spectrum = lax.dot_general(
            table_ref[...],
            jnp.concatenate([high, low, high], axis=1),
            (((1,), (1,)), ((), ())),
            preferred_element_type=jnp.float32,
        )
        for s in range(pair):
            for c in range(2):
                for h in range(FINE // LANES):
                    lane = s * FINE + h * LANES
                    g_ref[2 * c + h, pl.ds(i * pair + s, COARSE, stride=PITCH), :] = spectrum[
                        c * COARSE : (c + 1) * COARSE, lane : lane + LANES
                    ]

    copies = []
    for n, ((d, start, size, width), out, stage) in enumerate(zip(pieces, outs, stages)):
        base = (z_ref[0] ^ d) * width + start

        @pl.loop(0, size, unroll=2)
        def _(q):
            at = pl.ds((base + q) * PITCH, TILE)
            stage[q] = jnp.concatenate([g_ref[i, at, :] for i in range(4)], axis=1).astype(
                jnp.bfloat16
            )

        copies.append(pltpu.make_async_copy(stage, out, out_sem.at[n]))
        copies[-1].start()
    for copy in copies:
        copy.wait()


def channelize(voltages, fir_taps, tile, z, groups, cuts, pair=1, unroll=4):
    samples = voltages.shape[2]
    cosine, sine = twiddles()
    table = dft_table()
    whole = lambda shape: pl.BlockSpec(shape, lambda i: (0,) * len(shape))
    pieces = [(d, start, count, COARSE // groups) for d, start, count in cuts]
    shapes = [(count, TILE, 2 * FINE) for _, _, count, _ in pieces]
    outs = pl.pallas_call(
        functools.partial(channelize_kernel, pieces, tile, pair, unroll),
        grid=(1,),
        in_specs=[
            pl.BlockSpec(memory_space=pltpu.SMEM),
            pl.BlockSpec(memory_space=pl.ANY),
            whole(fir_taps.shape),
            whole(cosine.shape),
            whole(sine.shape),
            whole(table.shape),
        ],
        out_specs=[pl.BlockSpec(memory_space=pl.ANY)] * len(shapes),
        out_shape=[jax.ShapeDtypeStruct(shape, jnp.bfloat16) for shape in shapes],
        scratch_shapes=[pltpu.VMEM(shape, jnp.bfloat16) for shape in shapes]
        + [
            pltpu.VMEM((2, TILE, samples), jnp.bfloat16),
            pltpu.VMEM((2, CHANNELS // LANES, TILE * FRAMES, LANES), jnp.float32),
            pltpu.VMEM((4, COARSE * PITCH, LANES), jnp.float32),
            pltpu.SemaphoreType.DMA((CHUNKS,)),
            pltpu.SemaphoreType.DMA((len(shapes),)),
        ],
        compiler_params=pltpu.CompilerParams(vmem_limit_bytes=VMEM),
        cost_estimate=pl.CostEstimate(
            flops=14 * 10**9, bytes_accessed=10 * 10**6, transcendentals=0
        ),
        name="channelize",
    )(z, voltages, fir_taps, jnp.asarray(cosine), jnp.asarray(sine), jnp.asarray(table))
    return {(d, start): out for (d, start, _, _), out in zip(pieces, outs)}


def correlate_kernel(batch, places, at_ref, *refs):
    pieces, (out_ref, mark_ref, right) = refs[: len(places)], refs[-3:]
    mark_ref[...] = jnp.zeros_like(mark_ref)
    scale = 1.0 / FINE
    for q in range(batch):
        for ref, (_, col) in zip(pieces, places):
            if col is not None:
                at = pl.multiple_of(at_ref[col], TILE)
                right[q, pl.ds(at, ref.shape[1]), :] = ref[q]
        rows = [(ref[q], row) for ref, (row, _) in zip(pieces, places) if row is not None]
        a, b = jnp.concatenate([value for value, _ in rows], axis=0), right[q]
        turned = jnp.concatenate([-b[:, FINE:], b[:, :FINE]], axis=1)
        parts = b.shape[0] // LANES
        for c, other in enumerate((b, turned)):
            product = scale * lax.dot_general(
                a, other, (((1,), (1,)), ((), ())), preferred_element_type=jnp.float32
            )
            start = 0
            for value, row in rows:
                size = value.shape[0]
                at = pl.multiple_of(at_ref[row] * parts, TILE * parts)
                for x in range(parts):
                    out_ref[c, q, pl.ds(at + x, size, stride=parts), :] = product[
                        start : start + size, x * LANES : (x + 1) * LANES
                    ]
                start += size


def correlate(result, pieces, start, count, coarse, row_count, col_count, batch):
    out_rows = row_count * col_count // LANES
    in_specs = [pl.BlockSpec(memory_space=pltpu.SMEM)]
    at, places = [], []
    for value, skip, row, col in pieces:
        shape = (batch,) + value.shape[1:]
        in_specs.append(pl.BlockSpec(shape, lambda i, skip=skip // batch: (i + skip, 0, 0)))
        numbered = []
        for place in (row, col):
            numbered.append(None if place is None else len(at))
            at += [] if place is None else [place]
        places.append(numbered)
    operands = [jnp.stack(at)] + [piece[0] for piece in pieces]
    aliases = {}
    if result is not None:
        aliases = {len(operands): 0}
        operands.append(result)
        in_specs.append(pl.BlockSpec(memory_space=pl.ANY))
    return pl.pallas_call(
        functools.partial(correlate_kernel, batch, places),
        grid=(count // batch,),
        in_specs=in_specs,
        out_specs=[
            pl.BlockSpec((2, batch, out_rows, LANES), lambda i: (0, i + start // batch, 0, 0)),
            pl.BlockSpec((8, LANES), lambda i: (0, 0)),
        ],
        out_shape=[
            jax.ShapeDtypeStruct((2, coarse, out_rows, LANES), jnp.float32),
            jax.ShapeDtypeStruct((8, LANES), jnp.float32),
        ],
        scratch_shapes=[pltpu.VMEM((batch, col_count, 2 * FINE), jnp.bfloat16)],
        input_output_aliases=aliases,
        compiler_params=pltpu.CompilerParams(vmem_limit_bytes=VMEM),
        cost_estimate=pl.CostEstimate(
            flops=20 * count * row_count * col_count * FINE,
            bytes_accessed=8 * count * row_count * col_count,
            transcendentals=0,
        ),
        name="correlate",
    )(*operands)


def swap(value, axis, d):
    return lax.ppermute(value, axis, [(i, i ^ d) for i in range(lax.axis_size(axis))])


def after(values, earlier):
    if not earlier or not values:
        return list(values)
    return list(lax.optimization_barrier((tuple(values), tuple(earlier)))[0])


def shards(voltages, fir_taps):
    groups = lax.axis_size("freq")
    z, x, b = (lax.axis_index(name) for name in ("freq", "brow", "bcol"))
    streams = voltages.shape[1]
    block = streams * groups
    coarse = COARSE // groups
    known = []

    def note(value, parts, rows=None, cols=False):
        offset = 0
        for first, count, at in parts:
            row = None if rows is None else (b ^ rows) * block + at
            col = (x ^ 1) * block + at if rows is None else x * block + at if rows == 0 else None
            known.append((value, offset, first, count, row, col))
            offset += count

    def join(pieces):
        return jnp.concatenate([value for value, _ in pieces], axis=0)

    def parts_of(pieces):
        return [part for _, parts in pieces for part in parts]

    freq_done, near_done = [], []

    def turn(over_freq, spread, inner):
        arrived, over_y = [], None
        values = after([piece[0] for piece, _ in over_freq], freq_done)
        if over_freq:
            freq_done.clear()
        for (piece, d), value in zip(over_freq, values):
            value = swap(value, "freq", d)
            freq_done.append(value)
            arrived.append((value, piece[1]))
            note(value, piece[1], 0)
        values = [join(spread)] if spread else []
        values += [join([piece for piece, _ in inner])] if inner else []
        values = after(values, near_done)
        near_done.clear()
        if spread:
            value, parts = values.pop(0), parts_of(spread)
            over_x, over_y = swap(value, "brow", 1), swap(value, "bcol", 2)
            near_done.extend([over_x, over_y])
            note(over_x, parts)
            note(over_y, parts, 2)
            over_y = over_y, parts
        if inner:
            value = swap(values.pop(0), "bcol", 1)
            near_done.append(value)
            offset = 0
            for (_, parts), e in inner:
                for first, count, at in parts:
                    known.append((value, offset, first, count, (b ^ e ^ 1) * block + at, None))
                    offset += count
        return arrived, over_y

    def fill(result, start, count, batch):
        used = [
            (value, offset + start - first, row, col)
            for value, offset, first, size, row, col in known
            if first <= start < first + size
        ]
        return correlate(result, used, start, count, coarse, 4 * block, 2 * block, batch)

    if streams == 2 * TILE and groups == 4:
        half = coarse // 2

        def made(tile, cuts, *form):
            local = channelize(voltages, fir_taps, tile, z[None], groups, cuts, *form)
            return {
                (d, first): (
                    local[d, first],
                    [(first, count, (z ^ d) * streams + tile * TILE)],
                )
                for d, first, count in cuts
            }

        p = made(0, [(d, 0, coarse) for d in (2, 1, 3, 0)], 2, 2)
        own_a = p[0, 0]
        note(own_a[0], own_a[1], 0)
        (a2, a1), y1 = turn([(p[2, 0], 2), (p[1, 0], 1)], [own_a], [(own_a, 0)])
        r = made(
            1, [(0, 0, coarse), (1, 0, coarse)] + [(d, at, half) for d in (2, 3) for at in (0, half)]
        )
        own_b = r[0, 0]
        note(own_b[0], own_b[1], 0)
        (a3, b1), y2 = turn([(p[3, 0], 3), (r[1, 0], 1)], [a1, a2], [(y1, 2), (a1, 0), (a2, 0)])
        (b2, b3), y3 = turn(
            [(r[2, 0], 2), (r[3, 0], 3)], [a3, own_b], [(y2, 2), (a3, 0), (own_b, 0)]
        )
        (c2, c3), y4 = turn(
            [(r[2, half], 2), (r[3, half], 3)],
            [b1, b2, b3],
            [(y3, 2), (b1, 0), (b2, 0), (b3, 0)],
        )
        _, y5 = turn([], [c2, c3], [(y4, 2)])
        result, mark = fill(None, 0, half, 4)
        near_done.append(mark)
        turn([], [], [(y5, 2), (c2, 0), (c3, 0)])
        result, _ = fill(result, half, half, 4)
    else:
        padded = jnp.pad(voltages, ((0, 0), (0, -streams % TILE), (0, 0)))
        zero = jnp.zeros((1,), jnp.int32)
        cuts = [(d, 0, coarse) for d in range(groups)]
        local = [
            channelize(padded, fir_taps, tile, zero, groups, cuts)
            for tile in range(padded.shape[1] // TILE)
        ]
        local = jnp.concatenate(
            [jnp.concatenate([part[d, 0] for d in range(groups)], axis=0) for part in local], axis=1
        )[:, :streams]
        local = lax.all_to_all(local, "freq", 0, 1, tiled=True)
        own = local, [(0, coarse, jnp.int32(0))]
        note(own[0], own[1], 0)
        _, over_y = turn([], [own], [(own, 0)])
        turn([], [], [(over_y, 2)])
        result, _ = fill(None, 0, coarse, 1)
    return result.reshape(2, coarse, 4 * block, 2, 1, block)


def solution(mesh):
    in_specs = (P(None, ("brow", "bcol", "freq"), None), P())
    out_specs = P(None, "freq", "brow", None, "bcol", None)
    return jax.shard_map(shards, mesh=mesh, in_specs=in_specs, out_specs=out_specs, check_vma=False)
```

```python
import functools
import math

import jax
import jax.numpy as jnp
import numpy as np
from jax import lax
from jax.experimental import pallas as pl
from jax.experimental.pallas import tpu as pltpu
from jax.sharding import PartitionSpec as P

CHANNELS = 4096
TAPS = 16
AVG = 32
FRAMES = 8
COARSE = CHANNELS // AVG
FINE = FRAMES * AVG
TILE = 16
LANES = 128
PITCH = TILE + 1
VMEM = 60 << 20
CHUNKS = 4


def dft_table():
    index = np.arange(COARSE)
    angle = 2.0 * math.pi * (index[:, None] * index[None, :] % COARSE) / COARSE
    cosine, sine = np.cos(angle) / 64.0, np.sin(angle) / 64.0
    table = np.block([[cosine, sine], [-sine, cosine]]).astype(np.float32)
    high = table.astype(jnp.bfloat16)
    low = (table - high.astype(np.float32)).astype(jnp.bfloat16)
    return np.concatenate([high, high, low], axis=1)


def twiddles():
    angle = 2.0 * math.pi * np.arange(AVG)[:, None] * np.arange(LANES)[None, :] / CHANNELS
    return np.cos(angle).astype(np.float32), np.sin(angle).astype(np.float32)


def times(value, numerator, length):
    re, im = value
    numerator %= length
    if numerator == 0:
        return re, im
    if 4 * numerator == length:
        return im, -re
    if 2 * numerator == length:
        return -re, -im
    if 4 * numerator == 3 * length:
        return -im, re
    cosine = math.cos(2.0 * math.pi * numerator / length)
    sine = math.sin(2.0 * math.pi * numerator / length)
    if 8 * numerator == length:
        return (re + im) * cosine, (im - re) * cosine
    if 8 * numerator == 3 * length:
        return (im - re) * sine, (re + im) * -sine
    return re * cosine + im * sine, im * cosine - re * sine


def small_dft(values):
    length = len(values)
    if length == 1:
        return values
    even, odd = small_dft(values[0::2]), small_dft(values[1::2])
    odd = [times(value, k, length) for k, value in enumerate(odd)]
    return [(e[0] + o[0], e[1] + o[1]) for e, o in zip(even, odd)] + [
        (e[0] - o[0], e[1] - o[1]) for e, o in zip(even, odd)
    ]


def channelize_kernel(pieces, tile, pitch, unroll, z_ref, v_hbm, taps_ref, cos_ref, sin_ref, table_ref, *refs):
    count = len(pieces)
    outs, stages = refs[:count], refs[count : 2 * count]
    v_ref, filt, g_ref, in_sem, out_sem = refs[2 * count :]
    chunk = CHANNELS // CHUNKS
    spans = FRAMES + TAPS - 1
    rows = pl.ds(tile * TILE, TILE)
    for k in range(CHUNKS):
        for f in range(spans):
            lanes = pl.ds(f * CHANNELS + k * chunk, chunk)
            pltpu.make_async_copy(
                v_hbm.at[:, rows, lanes], v_ref.at[:, :, lanes], in_sem.at[k]
            ).start()

    for k in range(CHUNKS):
        lanes = pl.ds(0, spans * chunk)
        pltpu.make_async_copy(v_hbm.at[:, rows, lanes], v_ref.at[:, :, lanes], in_sem.at[k]).wait()

        @pl.loop(k * (chunk // LANES), (k + 1) * (chunk // LANES))
        def _(j):
            lane = pl.multiple_of(j * LANES, LANES)
            taps = [
                jnp.broadcast_to(taps_ref[p : p + 1, pl.ds(lane, LANES)], (TILE, LANES))
                for p in range(TAPS)
            ]
            for c in range(2):
                total = [None] * FRAMES
                for f in range(spans):
                    v = v_ref[c, :, pl.ds(f * CHANNELS + lane, LANES)].astype(jnp.float32)
                    for t in range(max(0, f - TAPS + 1), min(FRAMES, f + 1)):
                        term = taps[f - t] * v
                        total[t] = term if f == t else total[t] + term
                        if f - t == TAPS - 1:
                            filt[c, j, pl.ds(t, TILE, stride=pitch), :] = total[t]

    def turned_fft(s):
        rows = pl.ds(s * pitch, FRAMES)
        first = []
        for j0 in range(4):
            part = small_dft([(filt[0, j, rows, :], filt[1, j, rows, :]) for j in range(j0, AVG, 4)])
            first.append([times(value, j0 * ka, AVG) for ka, value in enumerate(part)])
        turned = [None] * AVG
        for ka in range(8):
            last = small_dft([first[j0][ka] for j0 in range(4)])
            for kb in range(4):
                k = ka + 8 * kb
                re, im = last[kb]
                if k:
                    cosine, sine = cos_ref[k : k + 1, :], sin_ref[k : k + 1, :]
                    re, im = re * cosine + im * sine, im * cosine - re * sine
                turned[k] = jnp.concatenate([re, im], axis=1)
        return turned

    @pl.loop(0, TILE, unroll=unroll)
    def _(s):
        value = jnp.concatenate(turned_fft(s), axis=0)
        high = value.astype(jnp.bfloat16)
        low = (value - high.astype(jnp.float32)).astype(jnp.bfloat16)
        spectrum = lax.dot_general(
            table_ref[...],
            jnp.concatenate([high, low, high], axis=1),
            (((1,), (1,)), ((), ())),
            preferred_element_type=jnp.float32,
        )
        for c in range(2):
            for h in range(FINE // LANES):
                g_ref[2 * c + h, pl.ds(s, COARSE, stride=PITCH), :] = spectrum[
                    c * COARSE : (c + 1) * COARSE, h * LANES : (h + 1) * LANES
                ]

    copies = []
    for n, ((d, start, size, width), out, stage) in enumerate(zip(pieces, outs, stages)):
        base = (z_ref[0] ^ d) * width + start

        @pl.loop(0, size, unroll=2)
        def _(q):
            at = pl.ds((base + q) * PITCH, TILE)
            stage[q] = jnp.concatenate([g_ref[i, at, :] for i in range(4)], axis=1).astype(
                jnp.bfloat16
            )

        copies.append(pltpu.make_async_copy(stage, out, out_sem.at[n]))
        copies[-1].start()
    for copy in copies:
        copy.wait()


def channelize(voltages, fir_taps, tile, z, groups, cuts, pitch=FRAMES, unroll=4):
    samples = voltages.shape[2]
    cosine, sine = twiddles()
    table = dft_table()
    whole = lambda shape: pl.BlockSpec(shape, lambda i: (0,) * len(shape))
    pieces = [(d, start, count, COARSE // groups) for d, start, count in cuts]
    shapes = [(count, TILE, 2 * FINE) for _, _, count, _ in pieces]
    outs = pl.pallas_call(
        functools.partial(channelize_kernel, pieces, tile, pitch, unroll),
        grid=(1,),
        in_specs=[
            pl.BlockSpec(memory_space=pltpu.SMEM),
            pl.BlockSpec(memory_space=pl.ANY),
            whole(fir_taps.shape),
            whole(cosine.shape),
            whole(sine.shape),
            whole(table.shape),
        ],
        out_specs=[pl.BlockSpec(memory_space=pl.ANY)] * len(shapes),
        out_shape=[jax.ShapeDtypeStruct(shape, jnp.bfloat16) for shape in shapes],
        scratch_shapes=[pltpu.VMEM(shape, jnp.bfloat16) for shape in shapes]
        + [
            pltpu.VMEM((2, TILE, samples), jnp.bfloat16),
            pltpu.VMEM((2, CHANNELS // LANES, TILE * pitch, LANES), jnp.float32),
            pltpu.VMEM((4, COARSE * PITCH, LANES), jnp.float32),
            pltpu.SemaphoreType.DMA((CHUNKS,)),
            pltpu.SemaphoreType.DMA((len(shapes),)),
        ],
        compiler_params=pltpu.CompilerParams(vmem_limit_bytes=VMEM),
        cost_estimate=pl.CostEstimate(
            flops=2 * 10**9, bytes_accessed=8 * 10**6, transcendentals=0
        ),
        name="channelize",
    )(z, voltages, fir_taps, jnp.asarray(cosine), jnp.asarray(sine), jnp.asarray(table))
    return {(d, start): out for (d, start, _, _), out in zip(pieces, outs)}


def correlate_kernel(batch, places, at_ref, *refs):
    pieces, (out_ref, mark_ref, right) = refs[: len(places)], refs[-3:]
    mark_ref[...] = jnp.zeros_like(mark_ref)
    scale = 1.0 / FINE
    for q in range(batch):
        for ref, (_, col) in zip(pieces, places):
            if col is not None:
                at = pl.multiple_of(at_ref[col], TILE)
                right[q, pl.ds(at, ref.shape[1]), :] = ref[q]
        rows = [(ref[q], row) for ref, (row, _) in zip(pieces, places) if row is not None]
        a, b = jnp.concatenate([value for value, _ in rows], axis=0), right[q]
        turned = jnp.concatenate([-b[:, FINE:], b[:, :FINE]], axis=1)
        parts = b.shape[0] // LANES
        for c, other in enumerate((b, turned)):
            product = scale * lax.dot_general(
                a, other, (((1,), (1,)), ((), ())), preferred_element_type=jnp.float32
            )
            start = 0
            for value, row in rows:
                size = value.shape[0]
                at = pl.multiple_of(at_ref[row] * parts, TILE * parts)
                for x in range(parts):
                    out_ref[c, q, pl.ds(at + x, size, stride=parts), :] = product[
                        start : start + size, x * LANES : (x + 1) * LANES
                    ]
                start += size


def correlate(result, mark, pieces, start, count, coarse, row_count, col_count, batch):
    out_rows = row_count * col_count // LANES
    in_specs = [pl.BlockSpec(memory_space=pltpu.SMEM)]
    at, places = [], []
    for value, skip, row, col in pieces:
        shape = (batch,) + value.shape[1:]
        in_specs.append(pl.BlockSpec(shape, lambda i, skip=skip // batch: (i + skip, 0, 0)))
        numbered = []
        for place in (row, col):
            numbered.append(None if place is None else len(at))
            at += [] if place is None else [place]
        places.append(numbered)
    operands = [jnp.stack(at)] + [piece[0] for piece in pieces]
    aliases = {}
    if result is not None:
        aliases = {len(operands): 0}
        operands += [result, mark]
        in_specs += [pl.BlockSpec(memory_space=pl.ANY)] * 2
    return pl.pallas_call(
        functools.partial(correlate_kernel, batch, places),
        grid=(count // batch,),
        in_specs=in_specs,
        out_specs=[
            pl.BlockSpec((2, batch, out_rows, LANES), lambda i: (0, i + start // batch, 0, 0)),
            pl.BlockSpec((8, LANES), lambda i: (0, 0)),
        ],
        out_shape=[
            jax.ShapeDtypeStruct((2, coarse, out_rows, LANES), jnp.float32),
            jax.ShapeDtypeStruct((8, LANES), jnp.float32),
        ],
        scratch_shapes=[pltpu.VMEM((batch, col_count, 2 * FINE), jnp.bfloat16)],
        input_output_aliases=aliases,
        compiler_params=pltpu.CompilerParams(vmem_limit_bytes=VMEM),
        cost_estimate=pl.CostEstimate(
            flops=20 * count * row_count * col_count * FINE,
            bytes_accessed=8 * count * row_count * col_count,
            transcendentals=0,
        ),
        name="correlate",
    )(*operands)


def swap(value, axis, d):
    return lax.ppermute(value, axis, [(i, i ^ d) for i in range(lax.axis_size(axis))])


def after(values, earlier):
    if not earlier or not values:
        return list(values)
    return list(lax.optimization_barrier((tuple(values), tuple(earlier)))[0])


def shards(voltages, fir_taps):
    groups = lax.axis_size("freq")
    z, x, b = (lax.axis_index(name) for name in ("freq", "brow", "bcol"))
    streams = voltages.shape[1]
    block = streams * groups
    coarse = COARSE // groups
    known = []

    def note(value, parts, rows=None, cols=False):
        offset = 0
        for first, count, at in parts:
            row = None if rows is None else (b ^ rows) * block + at
            col = (x ^ 1) * block + at if rows is None else x * block + at if rows == 0 else None
            known.append((value, offset, first, count, row, col))
            offset += count

    def join(pieces):
        return jnp.concatenate([value for value, _ in pieces], axis=0)

    def parts_of(pieces):
        return [part for _, parts in pieces for part in parts]

    freq_done, near_done = [], []

    def turn(over_freq, spread, inner, apart=False):
        if not apart:
            freq_done.extend(near_done)
            near_done[:] = freq_done
        arrived, over_y = [], None
        values = after([piece[0] for piece, _ in over_freq], freq_done)
        freq_done.clear()
        for (piece, d), value in zip(over_freq, values):
            value = swap(value, "freq", d)
            freq_done.append(value)
            arrived.append((value, piece[1]))
            note(value, piece[1], 0)
        values = [join(spread)] if spread else []
        values += [join([piece for piece, _ in inner])] if inner else []
        values = after(values, near_done)
        near_done.clear()
        if spread:
            value, parts = values.pop(0), parts_of(spread)
            over_x, over_y = swap(value, "brow", 1), swap(value, "bcol", 2)
            near_done.extend([over_x, over_y])
            note(over_x, parts)
            note(over_y, parts, 2)
            over_y = over_y, parts
        if inner:
            value = swap(values.pop(0), "bcol", 1)
            near_done.append(value)
            offset = 0
            for (_, parts), e in inner:
                for first, count, at in parts:
                    known.append((value, offset, first, count, (b ^ e ^ 1) * block + at, None))
                    offset += count
        return arrived, over_y

    def fill(result, start, count, batch, mark=None):
        used = [
            (value, offset + start - first, row, col)
            for value, offset, first, size, row, col in known
            if first <= start < first + size
        ]
        return correlate(result, mark, used, start, count, coarse, 4 * block, 2 * block, batch)

    if streams == 2 * TILE and groups == 4:
        half = coarse // 2

        def made(tile, cuts, *form):
            local = channelize(voltages, fir_taps, tile, z[None], groups, cuts, *form)
            return {
                (d, first): (
                    local[d, first],
                    [(first, count, (z ^ d) * streams + tile * TILE)],
                )
                for d, first, count in cuts
            }

        p = made(0, [(d, 0, coarse) for d in (2, 1, 3, 0)], FRAMES + 1)
        own_a = p[0, 0]
        note(own_a[0], own_a[1], 0)
        (a2, a1), y1 = turn([(p[2, 0], 2), (p[1, 0], 1)], [own_a], [(own_a, 0)])
        r = made(
            1, [(0, 0, coarse), (1, 0, coarse)] + [(d, at, half) for d in (2, 3) for at in (0, half)]
        )
        own_b = r[0, 0]
        note(own_b[0], own_b[1], 0)
        near_done.append(own_b[0])
        (a3, b1), y2 = turn(
            [(p[3, 0], 3), (r[1, 0], 1)], [a1, a2], [(y1, 2), (a1, 0), (a2, 0)], apart=True
        )
        (b2, b3), y3 = turn(
            [(r[2, 0], 2), (r[3, 0], 3)], [a3, own_b], [(y2, 2), (a3, 0), (own_b, 0)]
        )
        (c2, c3), y4 = turn(
            [(r[2, half], 2), (r[3, half], 3)],
            [b1, b2, b3],
            [(y3, 2), (b1, 0), (b2, 0), (b3, 0)],
        )
        _, y5 = turn([], [c2, c3], [(y4, 2)])
        result, mark = fill(None, 0, half, 2)
        near_done.append(mark)
        y5 = after([y5[0]], [mark])[0], y5[1]
        turn([], [], [(y5, 2), (c2, 0), (c3, 0)])
        result, _ = fill(result, half, half, 2, mark)
    else:
        padded = jnp.pad(voltages, ((0, 0), (0, -streams % TILE), (0, 0)))
        zero = jnp.zeros((1,), jnp.int32)
        cuts = [(d, 0, coarse) for d in range(groups)]
        local = [
            channelize(padded, fir_taps, tile, zero, groups, cuts)
            for tile in range(padded.shape[1] // TILE)
        ]
        local = jnp.concatenate(
            [jnp.concatenate([part[d, 0] for d in range(groups)], axis=0) for part in local], axis=1
        )[:, :streams]
        local = lax.all_to_all(local, "freq", 0, 1, tiled=True)
        own = local, [(0, coarse, jnp.int32(0))]
        note(own[0], own[1], 0)
        _, over_y = turn([], [own], [(own, 0)])
        turn([], [], [(over_y, 2)])
        result, _ = fill(None, 0, coarse, 1)
    return result.reshape(2, coarse, 4 * block, 2, 1, block)


def solution(mesh):
    in_specs = (P(None, ("brow", "bcol", "freq"), None), P())
    out_specs = P(None, "freq", "brow", None, "bcol", None)
    return jax.shard_map(shards, mesh=mesh, in_specs=in_specs, out_specs=out_specs, check_vma=False)
```

```python
import functools
import math

import jax
import jax.numpy as jnp
import numpy as np
from jax import lax
from jax.experimental import pallas as pl
from jax.experimental.pallas import tpu as pltpu
from jax.sharding import PartitionSpec as P

CHANNELS = 4096
TAPS = 16
AVG = 32
FRAMES = 8
COARSE = CHANNELS // AVG
FINE = FRAMES * AVG
TILE = 16
LANES = 128
PITCH = TILE + 1
VMEM = 24 << 20
CHUNKS = 4


def dft_table():
    index = np.arange(COARSE)
    angle = 2.0 * math.pi * (index[:, None] * index[None, :] % COARSE) / COARSE
    cosine, sine = np.cos(angle) / 64.0, np.sin(angle) / 64.0
    table = np.block([[cosine, sine], [-sine, cosine]]).astype(np.float32)
    high = table.astype(jnp.bfloat16)
    low = (table - high.astype(np.float32)).astype(jnp.bfloat16)
    return np.concatenate([high, high, low], axis=1)


def twiddles():
    angle = 2.0 * math.pi * np.arange(AVG)[:, None] * np.arange(LANES)[None, :] / CHANNELS
    return np.cos(angle).astype(np.float32), np.sin(angle).astype(np.float32)


def times(value, numerator, length):
    re, im = value
    numerator %= length
    if numerator == 0:
        return re, im
    if 4 * numerator == length:
        return im, -re
    if 2 * numerator == length:
        return -re, -im
    if 4 * numerator == 3 * length:
        return -im, re
    cosine = math.cos(2.0 * math.pi * numerator / length)
    sine = math.sin(2.0 * math.pi * numerator / length)
    if 8 * numerator == length:
        return (re + im) * cosine, (im - re) * cosine
    if 8 * numerator == 3 * length:
        return (im - re) * sine, (re + im) * -sine
    return re * cosine + im * sine, im * cosine - re * sine


def small_dft(values):
    length = len(values)
    if length == 1:
        return values
    even, odd = small_dft(values[0::2]), small_dft(values[1::2])
    odd = [times(value, k, length) for k, value in enumerate(odd)]
    return [(e[0] + o[0], e[1] + o[1]) for e, o in zip(even, odd)] + [
        (e[0] - o[0], e[1] - o[1]) for e, o in zip(even, odd)
    ]


def channelize_kernel(pieces, tile, once, unroll, z_ref, v_hbm, taps_ref, cos_ref, sin_ref, table_ref, *refs):
    count = len(pieces)
    outs, stages = refs[:count], refs[count : 2 * count]
    v_ref, filt, g_ref, in_sem, out_sem = refs[2 * count :]
    chunk = CHANNELS // CHUNKS
    spans = FRAMES + TAPS - 1
    rows = pl.ds(tile * TILE, TILE)
    for k in range(CHUNKS):
        for f in range(spans):
            lanes = pl.ds(f * CHANNELS + k * chunk, chunk)
            pltpu.make_async_copy(
                v_hbm.at[:, rows, lanes], v_ref.at[:, :, lanes], in_sem.at[k]
            ).start()

    for k in range(CHUNKS):
        lanes = pl.ds(0, spans * chunk)
        pltpu.make_async_copy(v_hbm.at[:, rows, lanes], v_ref.at[:, :, lanes], in_sem.at[k]).wait()

        @pl.loop(k * (chunk // LANES), (k + 1) * (chunk // LANES))
        def _(j):
            lane = pl.multiple_of(j * LANES, LANES)
            taps = [
                jnp.broadcast_to(taps_ref[p : p + 1, pl.ds(lane, LANES)], (TILE, LANES))
                for p in range(TAPS)
            ]
            for c in range(2):
                total = [None] * FRAMES
                for f in range(spans):
                    v = v_ref[c, :, pl.ds(f * CHANNELS + lane, LANES)].astype(jnp.float32)
                    for t in range(max(0, f - TAPS + 1), min(FRAMES, f + 1)):
                        term = taps[f - t] * v
                        total[t] = term if f == t else total[t] + term
                        if f - t == TAPS - 1:
                            filt[c, j, pl.ds(t, TILE, stride=FRAMES), :] = total[t]

    def turned_fft(s):
        rows = pl.ds(pl.multiple_of(s * FRAMES, FRAMES), FRAMES)
        first = []
        for j0 in range(4):
            part = small_dft([(filt[0, j, rows, :], filt[1, j, rows, :]) for j in range(j0, AVG, 4)])
            first.append([times(value, j0 * ka, AVG) for ka, value in enumerate(part)])
        turned = [None] * AVG
        for ka in range(8):
            last = small_dft([first[j0][ka] for j0 in range(4)])
            for kb in range(4):
                k = ka + 8 * kb
                re, im = last[kb]
                if k:
                    cosine, sine = cos_ref[k : k + 1, :], sin_ref[k : k + 1, :]
                    re, im = re * cosine + im * sine, im * cosine - re * sine
                turned[k] = jnp.concatenate([re, im], axis=1)
        return turned

    @pl.loop(0, TILE, unroll=unroll)
    def _(s):
        value = jnp.concatenate(turned_fft(s), axis=0)
        high = value.astype(jnp.bfloat16)
        low = (value - high.astype(jnp.float32)).astype(jnp.bfloat16)

        def product(table, data):
            return lax.dot_general(
                table, data, (((1,), (1,)), ((), ())), preferred_element_type=jnp.float32
            )

        size = 2 * COARSE
        if once:
            both = product(
                jnp.concatenate([table_ref[:, :size], table_ref[:, 2 * size :]], axis=0), high
            )
            spectrum = both[:size] + (both[size:] + product(table_ref[:, :size], low))
        else:
            spectrum = product(table_ref[...], jnp.concatenate([high, low, high], axis=1))
        for c in range(2):
            for h in range(FINE // LANES):
                g_ref[2 * c + h, pl.ds(s, COARSE, stride=PITCH), :] = spectrum[
                    c * COARSE : (c + 1) * COARSE, h * LANES : (h + 1) * LANES
                ]

    copies = []
    for n, ((d, start, size, width), out, stage) in enumerate(zip(pieces, outs, stages)):
        base = (z_ref[0] ^ d) * width + start

        @pl.loop(0, size, unroll=2)
        def _(q):
            at = pl.ds((base + q) * PITCH, TILE)
            stage[q] = jnp.concatenate([g_ref[i, at, :] for i in range(4)], axis=1).astype(
                jnp.bfloat16
            )

        copies.append(pltpu.make_async_copy(stage, out, out_sem.at[n]))
        copies[-1].start()
    for copy in copies:
        copy.wait()


def channelize(voltages, fir_taps, tile, z, groups, cuts, once=False, unroll=4):
    samples = voltages.shape[2]
    cosine, sine = twiddles()
    table = dft_table()
    whole = lambda shape: pl.BlockSpec(shape, lambda i: (0,) * len(shape))
    pieces = [(d, start, count, COARSE // groups) for d, start, count in cuts]
    shapes = [(count, TILE, 2 * FINE) for _, _, count, _ in pieces]
    outs = pl.pallas_call(
        functools.partial(channelize_kernel, pieces, tile, once, unroll),
        grid=(1,),
        in_specs=[
            pl.BlockSpec(memory_space=pltpu.SMEM),
            pl.BlockSpec(memory_space=pl.ANY),
            whole(fir_taps.shape),
            whole(cosine.shape),
            whole(sine.shape),
            whole(table.shape),
        ],
        out_specs=[pl.BlockSpec(memory_space=pl.ANY)] * len(shapes),
        out_shape=[jax.ShapeDtypeStruct(shape, jnp.bfloat16) for shape in shapes],
        scratch_shapes=[pltpu.VMEM(shape, jnp.bfloat16) for shape in shapes]
        + [
            pltpu.VMEM((2, TILE, samples), jnp.bfloat16),
            pltpu.VMEM((2, CHANNELS // LANES, TILE * FRAMES, LANES), jnp.float32),
            pltpu.VMEM((4, COARSE * PITCH, LANES), jnp.float32),
            pltpu.SemaphoreType.DMA((CHUNKS,)),
            pltpu.SemaphoreType.DMA((len(shapes),)),
        ],
        compiler_params=pltpu.CompilerParams(vmem_limit_bytes=VMEM),
        cost_estimate=pl.CostEstimate(
            flops=2 * 10**9, bytes_accessed=8 * 10**6, transcendentals=0
        ),
        name="channelize",
    )(z, voltages, fir_taps, jnp.asarray(cosine), jnp.asarray(sine), jnp.asarray(table))
    return {(d, start): out for (d, start, _, _), out in zip(pieces, outs)}


def correlate_kernel(batch, start, places, at_ref, *refs):
    pieces, (out_hbm, mark_ref, right, out_ref, out_sem) = refs[: len(places)], refs[-5:]
    scale = 1.0 / FINE
    step = pl.program_id(0)
    mark_ref[...] = jnp.zeros_like(mark_ref)
    slots = out_ref.shape[0]

    def copy_out(q, slot):
        return pltpu.make_async_copy(out_ref.at[slot], out_hbm.at[:, q], out_sem.at[slot])

    for q in range(batch):
        slot = q % slots
        for ref, (_, col) in zip(pieces, places):
            if col is not None:
                at = pl.multiple_of(at_ref[col], TILE)
                right[q, pl.ds(at, ref.shape[1]), :] = ref[q]
        rows = [(ref[q], row) for ref, (row, _) in zip(pieces, places) if row is not None]
        a, b = jnp.concatenate([value for value, _ in rows], axis=0), right[q]
        turned = jnp.concatenate([-b[:, FINE:], b[:, :FINE]], axis=1)
        parts = b.shape[0] // LANES
        channel = start + step * batch + q
        if q < slots:

            @pl.when(step > 0)
            def _():
                copy_out(channel, slot).wait()
        else:
            copy_out(channel, slot).wait()
        for c, other in enumerate((b, turned)):
            product = scale * lax.dot_general(
                a, other, (((1,), (1,)), ((), ())), preferred_element_type=jnp.float32
            )
            first = 0
            for value, row in rows:
                size = value.shape[0]
                at = pl.multiple_of(at_ref[row] * parts, TILE * parts)
                for x in range(parts):
                    out_ref[slot, c, pl.ds(at + x, size, stride=parts), :] = product[
                        first : first + size, x * LANES : (x + 1) * LANES
                    ]
                first += size
        copy_out(channel, slot).start()

    @pl.when(step == pl.num_programs(0) - 1)
    def _():
        for slot in range(slots):
            copy_out(start, slot).wait()


def correlate(result, mark, pieces, start, count, coarse, row_count, col_count, batch):
    out_rows = row_count * col_count // LANES
    in_specs = [pl.BlockSpec(memory_space=pltpu.SMEM)]
    at, places = [], []
    for value, skip, row, col in pieces:
        shape = (batch,) + value.shape[1:]
        in_specs.append(pl.BlockSpec(shape, lambda i, skip=skip // batch: (i + skip, 0, 0)))
        numbered = []
        for place in (row, col):
            numbered.append(None if place is None else len(at))
            at += [] if place is None else [place]
        places.append(numbered)
    operands = [jnp.stack(at)] + [piece[0] for piece in pieces]
    aliases = {}
    if result is not None:
        aliases = {len(operands): 0}
        operands += [result, mark]
        in_specs += [pl.BlockSpec(memory_space=pl.ANY)] * 2
    slots = min(2, batch)
    return pl.pallas_call(
        functools.partial(correlate_kernel, batch, start, places),
        grid=(count // batch,),
        in_specs=in_specs,
        out_specs=[
            pl.BlockSpec(memory_space=pl.ANY),
            pl.BlockSpec((8, LANES), lambda i: (0, 0)),
        ],
        out_shape=[
            jax.ShapeDtypeStruct((2, coarse, out_rows, LANES), jnp.float32),
            jax.ShapeDtypeStruct((8, LANES), jnp.float32),
        ],
        scratch_shapes=[
            pltpu.VMEM((batch, col_count, 2 * FINE), jnp.bfloat16),
            pltpu.VMEM((slots, 2, out_rows, LANES), jnp.float32),
            pltpu.SemaphoreType.DMA((slots,)),
        ],
        input_output_aliases=aliases,
        compiler_params=pltpu.CompilerParams(vmem_limit_bytes=VMEM),
        cost_estimate=pl.CostEstimate(
            flops=20 * count * row_count * col_count * FINE,
            bytes_accessed=8 * count * row_count * col_count,
            transcendentals=0,
        ),
        name="correlate",
    )(*operands)


def swap(value, axis, d):
    return lax.ppermute(value, axis, [(i, i ^ d) for i in range(lax.axis_size(axis))])


def after(values, earlier):
    if not earlier or not values:
        return list(values)
    return list(lax.optimization_barrier((tuple(values), tuple(earlier)))[0])


def shards(voltages, fir_taps):
    groups = lax.axis_size("freq")
    z, x, b = (lax.axis_index(name) for name in ("freq", "brow", "bcol"))
    streams = voltages.shape[1]
    block = streams * groups
    coarse = COARSE // groups
    known = []

    def note(value, parts, rows=None, cols=False):
        offset = 0
        for first, count, at in parts:
            row = None if rows is None else (b ^ rows) * block + at
            col = (x ^ 1) * block + at if rows is None else x * block + at if rows == 0 else None
            known.append((value, offset, first, count, row, col))
            offset += count

    def join(pieces):
        return jnp.concatenate([value for value, _ in pieces], axis=0)

    def parts_of(pieces):
        return [part for _, parts in pieces for part in parts]

    freq_done, near_done = [], []

    def turn(over_freq, spread, inner, apart=False):
        if not apart:
            freq_done.extend(near_done)
            near_done[:] = freq_done
        arrived, over_y = [], None
        values = after([piece[0] for piece, _ in over_freq], freq_done)
        freq_done.clear()
        for (piece, d), value in zip(over_freq, values):
            value = swap(value, "freq", d)
            freq_done.append(value)
            arrived.append((value, piece[1]))
            note(value, piece[1], 0)
        values = [join(spread)] if spread else []
        values += [join([piece for piece, _ in inner])] if inner else []
        values = after(values, near_done)
        near_done.clear()
        if spread:
            value, parts = values.pop(0), parts_of(spread)
            over_x, over_y = swap(value, "brow", 1), swap(value, "bcol", 2)
            near_done.extend([over_x, over_y])
            note(over_x, parts)
            note(over_y, parts, 2)
            over_y = over_y, parts
        if inner:
            value = swap(values.pop(0), "bcol", 1)
            near_done.append(value)
            offset = 0
            for (_, parts), e in inner:
                for first, count, at in parts:
                    known.append((value, offset, first, count, (b ^ e ^ 1) * block + at, None))
                    offset += count
        return arrived, over_y

    def fill(result, start, count, batch, mark=None):
        used = [
            (value, offset + start - first, row, col)
            for value, offset, first, size, row, col in known
            if first <= start < first + size
        ]
        return correlate(result, mark, used, start, count, coarse, 4 * block, 2 * block, batch)

    if streams == 2 * TILE and groups == 4:
        half = coarse // 2

        def made(tile, cuts, *form):
            local = channelize(voltages, fir_taps, tile, z[None], groups, cuts, *form)
            return {
                (d, first): (
                    local[d, first],
                    [(first, count, (z ^ d) * streams + tile * TILE)],
                )
                for d, first, count in cuts
            }

        p = made(0, [(d, 0, coarse) for d in (2, 1, 3, 0)], True)
        own_a = p[0, 0]
        note(own_a[0], own_a[1], 0)
        (a2, a1), y1 = turn([(p[2, 0], 2), (p[1, 0], 1)], [own_a], [(own_a, 0)])
        r = made(
            1, [(0, 0, coarse), (1, 0, coarse)] + [(d, at, half) for d in (2, 3) for at in (0, half)]
        )
        own_b = r[0, 0]
        note(own_b[0], own_b[1], 0)
        near_done.append(own_b[0])
        (a3, b1), y2 = turn(
            [(p[3, 0], 3), (r[1, 0], 1)], [a1, a2], [(y1, 2), (a1, 0), (a2, 0)], apart=True
        )
        (b2, b3), y3 = turn(
            [(r[2, 0], 2), (r[3, 0], 3)], [a3, own_b], [(y2, 2), (a3, 0), (own_b, 0)]
        )
        (c2, c3), y4 = turn(
            [(r[2, half], 2), (r[3, half], 3)],
            [b1, b2, b3],
            [(y3, 2), (b1, 0), (b2, 0), (b3, 0)],
        )
        _, y5 = turn([], [c2, c3], [(y4, 2)])
        result, mark = fill(None, 0, half, 4)
        near_done.append(mark)
        y5 = after([y5[0]], [mark])[0], y5[1]
        turn([], [], [(y5, 2), (c2, 0), (c3, 0)])
        result, _ = fill(result, half, half, 4, mark)
    else:
        padded = jnp.pad(voltages, ((0, 0), (0, -streams % TILE), (0, 0)))
        zero = jnp.zeros((1,), jnp.int32)
        cuts = [(d, 0, coarse) for d in range(groups)]
        local = [
            channelize(padded, fir_taps, tile, zero, groups, cuts)
            for tile in range(padded.shape[1] // TILE)
        ]
        local = jnp.concatenate(
            [jnp.concatenate([part[d, 0] for d in range(groups)], axis=0) for part in local], axis=1
        )[:, :streams]
        local = lax.all_to_all(local, "freq", 0, 1, tiled=True)
        own = local, [(0, coarse, jnp.int32(0))]
        note(own[0], own[1], 0)
        _, over_y = turn([], [own], [(own, 0)])
        turn([], [], [(over_y, 2)])
        result, _ = fill(None, 0, coarse, 1)
    return result.reshape(2, coarse, 4 * block, 2, 1, block)


def solution(mesh):
    in_specs = (P(None, ("brow", "bcol", "freq"), None), P())
    out_specs = P(None, "freq", "brow", None, "bcol", None)
    return jax.shard_map(shards, mesh=mesh, in_specs=in_specs, out_specs=out_specs, check_vma=False)
```

```python
import functools
import math

import jax
import jax.numpy as jnp
import numpy as np
from jax import lax
from jax.experimental import pallas as pl
from jax.experimental.pallas import tpu as pltpu
from jax.sharding import PartitionSpec as P

CHANNELS = 4096
TAPS = 16
AVG = 32
FRAMES = 8
COARSE = CHANNELS // AVG
FINE = FRAMES * AVG
TILE = 16
LANES = 128
PITCH = TILE + 1
VMEM = 60 << 20
CHUNKS = 4


def dft_table():
    index = np.arange(COARSE)
    angle = 2.0 * math.pi * (index[:, None] * index[None, :] % COARSE) / COARSE
    cosine, sine = np.cos(angle) / 64.0, np.sin(angle) / 64.0
    table = np.block([[cosine, sine], [-sine, cosine]]).astype(np.float32)
    high = table.astype(jnp.bfloat16)
    low = (table - high.astype(np.float32)).astype(jnp.bfloat16)
    return np.concatenate([high, high, low], axis=1)


def twiddles():
    angle = 2.0 * math.pi * np.arange(AVG)[:, None] * np.arange(LANES)[None, :] / CHANNELS
    return np.cos(angle).astype(np.float32), np.sin(angle).astype(np.float32)


def times(value, numerator, length):
    re, im = value
    numerator %= length
    if numerator == 0:
        return re, im
    if 4 * numerator == length:
        return im, -re
    if 2 * numerator == length:
        return -re, -im
    if 4 * numerator == 3 * length:
        return -im, re
    cosine = math.cos(2.0 * math.pi * numerator / length)
    sine = math.sin(2.0 * math.pi * numerator / length)
    if 8 * numerator == length:
        return (re + im) * cosine, (im - re) * cosine
    if 8 * numerator == 3 * length:
        return (im - re) * sine, (re + im) * -sine
    return re * cosine + im * sine, im * cosine - re * sine


def small_dft(values):
    length = len(values)
    if length == 1:
        return values
    even, odd = small_dft(values[0::2]), small_dft(values[1::2])
    odd = [times(value, k, length) for k, value in enumerate(odd)]
    return [(e[0] + o[0], e[1] + o[1]) for e, o in zip(even, odd)] + [
        (e[0] - o[0], e[1] - o[1]) for e, o in zip(even, odd)
    ]


def channelize_kernel(pieces, tile, z_ref, v_hbm, taps_ref, cos_ref, sin_ref, table_ref, *refs):
    count = len(pieces)
    outs, stages = refs[:count], refs[count : 2 * count]
    v_ref, filt, g_ref, in_sem, out_sem = refs[2 * count :]
    chunk = CHANNELS // CHUNKS
    spans = FRAMES + TAPS - 1
    rows = pl.ds(tile * TILE, TILE)
    for k in range(CHUNKS):
        for f in range(spans):
            lanes = pl.ds(f * CHANNELS + k * chunk, chunk)
            pltpu.make_async_copy(
                v_hbm.at[:, rows, lanes], v_ref.at[:, :, lanes], in_sem.at[k]
            ).start()

    for k in range(CHUNKS):
        lanes = pl.ds(0, spans * chunk)
        pltpu.make_async_copy(v_hbm.at[:, rows, lanes], v_ref.at[:, :, lanes], in_sem.at[k]).wait()

        @pl.loop(k * (chunk // LANES), (k + 1) * (chunk // LANES))
        def _(j):
            lane = pl.multiple_of(j * LANES, LANES)
            taps = [
                jnp.broadcast_to(taps_ref[p : p + 1, pl.ds(lane, LANES)], (TILE, LANES))
                for p in range(TAPS)
            ]
            for c in range(2):
                total = [None] * FRAMES
                for f in range(spans):
                    v = v_ref[c, :, pl.ds(f * CHANNELS + lane, LANES)].astype(jnp.float32)
                    for t in range(max(0, f - TAPS + 1), min(FRAMES, f + 1)):
                        term = taps[f - t] * v
                        total[t] = term if f == t else total[t] + term
                        if f - t == TAPS - 1:
                            filt[c, j, pl.ds(t, TILE, stride=FRAMES), :] = total[t]

    def turned_fft(s):
        rows = pl.ds(pl.multiple_of(s * FRAMES, FRAMES), FRAMES)
        first = []
        for j0 in range(4):
            part = small_dft([(filt[0, j, rows, :], filt[1, j, rows, :]) for j in range(j0, AVG, 4)])
            first.append([times(value, j0 * ka, AVG) for ka, value in enumerate(part)])
        turned = [None] * AVG
        for ka in range(8):
            last = small_dft([first[j0][ka] for j0 in range(4)])
            for kb in range(4):
                k = ka + 8 * kb
                re, im = last[kb]
                if k:
                    cosine, sine = cos_ref[k : k + 1, :], sin_ref[k : k + 1, :]
                    re, im = re * cosine + im * sine, im * cosine - re * sine
                turned[k] = jnp.concatenate([re, im], axis=1)
        return turned

    @pl.loop(0, TILE, unroll=4)
    def _(s):
        value = jnp.concatenate(turned_fft(s), axis=0)
        high = value.astype(jnp.bfloat16)
        low = (value - high.astype(jnp.float32)).astype(jnp.bfloat16)
        spectrum = lax.dot_general(
            table_ref[...],
            jnp.concatenate([high, low, high], axis=1),
            (((1,), (1,)), ((), ())),
            preferred_element_type=jnp.float32,
        )
        for c in range(2):
            for h in range(FINE // LANES):
                g_ref[2 * c + h, pl.ds(s, COARSE, stride=PITCH), :] = spectrum[
                    c * COARSE : (c + 1) * COARSE, h * LANES : (h + 1) * LANES
                ]

    copies = []
    for n, ((d, start, size, width), out, stage) in enumerate(zip(pieces, outs, stages)):
        base = (z_ref[0] ^ d) * width + start

        @pl.loop(0, size, unroll=min(8, size))
        def _(q):
            at = pl.ds((base + q) * PITCH, TILE)
            stage[q] = jnp.concatenate([g_ref[i, at, :] for i in range(4)], axis=1).astype(
                jnp.bfloat16
            )

        copies.append(pltpu.make_async_copy(stage, out, out_sem.at[n]))
        copies[-1].start()
    for copy in copies:
        copy.wait()


def channelize(voltages, fir_taps, tile, z, groups, cuts):
    samples = voltages.shape[2]
    cosine, sine = twiddles()
    table = dft_table()
    whole = lambda shape: pl.BlockSpec(shape, lambda i: (0,) * len(shape))
    pieces = [(d, start, count, COARSE // groups) for d, start, count in cuts]
    shapes = [(count, TILE, 2 * FINE) for _, _, count, _ in pieces]
    outs = pl.pallas_call(
        functools.partial(channelize_kernel, pieces, tile),
        grid=(1,),
        in_specs=[
            pl.BlockSpec(memory_space=pltpu.SMEM),
            pl.BlockSpec(memory_space=pl.ANY),
            whole(fir_taps.shape),
            whole(cosine.shape),
            whole(sine.shape),
            whole(table.shape),
        ],
        out_specs=[pl.BlockSpec(memory_space=pl.ANY)] * len(shapes),
        out_shape=[jax.ShapeDtypeStruct(shape, jnp.bfloat16) for shape in shapes],
        scratch_shapes=[pltpu.VMEM(shape, jnp.bfloat16) for shape in shapes]
        + [
            pltpu.VMEM((2, TILE, samples), jnp.bfloat16),
            pltpu.VMEM((2, CHANNELS // LANES, TILE * FRAMES, LANES), jnp.float32),
            pltpu.VMEM((4, COARSE * PITCH, LANES), jnp.float32),
            pltpu.SemaphoreType.DMA((CHUNKS,)),
            pltpu.SemaphoreType.DMA((len(shapes),)),
        ],
        compiler_params=pltpu.CompilerParams(vmem_limit_bytes=VMEM),
        cost_estimate=pl.CostEstimate(
            flops=2 * 10**9, bytes_accessed=8 * 10**6, transcendentals=0
        ),
        name="channelize",
    )(z, voltages, fir_taps, jnp.asarray(cosine), jnp.asarray(sine), jnp.asarray(table))
    return {(d, start): out for (d, start, _, _), out in zip(pieces, outs)}


def correlate_kernel(batch, places, at_ref, *refs):
    groups, (out_ref, mark_ref, right) = refs[: len(places)], refs[-3:]
    mark_ref[...] = jnp.zeros_like(mark_ref)
    scale = 1.0 / FINE
    pieces = [
        (ref.at[n, 0], place) for ref, some in zip(groups, places) for n, place in enumerate(some)
    ]
    for q in range(batch):
        for ref, (_, col) in pieces:
            if col is not None:
                at = pl.multiple_of(at_ref[col], TILE)
                right[q, pl.ds(at, ref.shape[1]), :] = ref[q]
        rows = [(ref[q], row) for ref, (row, _) in pieces if row is not None]
        a, b = jnp.concatenate([value for value, _ in rows], axis=0), right[q]
        turned = jnp.concatenate([-b[:, FINE:], b[:, :FINE]], axis=1)
        parts = b.shape[0] // LANES
        for c, other in enumerate((b, turned)):
            product = scale * lax.dot_general(
                a, other, (((1,), (1,)), ((), ())), preferred_element_type=jnp.float32
            )
            start = 0
            for value, row in rows:
                size = value.shape[0]
                at = pl.multiple_of(at_ref[row] * parts, TILE * parts)
                for x in range(parts):
                    out_ref[c, q, pl.ds(at + x, size, stride=parts), :] = product[
                        start : start + size, x * LANES : (x + 1) * LANES
                    ]
                start += size


def correlate(result, mark, groups, start, count, coarse, row_count, col_count, batch):
    out_rows = row_count * col_count // LANES
    in_specs = [pl.BlockSpec(memory_space=pltpu.SMEM)]
    at, places = [], []
    for value, size, block, part, wanted in groups:
        shape = (size, 1, batch) + value.shape[3:]
        in_specs.append(
            pl.BlockSpec(shape, lambda i, block=block, part=part: (block, part, i, 0, 0))
        )
        places.append([])
        for pair in wanted:
            numbered = []
            for place in pair:
                numbered.append(None if place is None else len(at))
                at += [] if place is None else [place]
            places[-1].append(numbered)
    operands = [jnp.stack(at)] + [group[0] for group in groups]
    aliases = {}
    if result is not None:
        aliases = {len(operands): 0}
        operands += [result, mark]
        in_specs += [pl.BlockSpec(memory_space=pl.ANY)] * 2
    return pl.pallas_call(
        functools.partial(correlate_kernel, batch, places),
        grid=(count // batch,),
        in_specs=in_specs,
        out_specs=[
            pl.BlockSpec((2, batch, out_rows, LANES), lambda i: (0, i + start // batch, 0, 0)),
            pl.BlockSpec((8, LANES), lambda i: (0, 0)),
        ],
        out_shape=[
            jax.ShapeDtypeStruct((2, coarse, out_rows, LANES), jnp.float32),
            jax.ShapeDtypeStruct((8, LANES), jnp.float32),
        ],
        scratch_shapes=[pltpu.VMEM((batch, col_count, 2 * FINE), jnp.bfloat16)],
        input_output_aliases=aliases,
        compiler_params=pltpu.CompilerParams(vmem_limit_bytes=VMEM),
        cost_estimate=pl.CostEstimate(
            flops=20 * count * row_count * col_count * FINE,
            bytes_accessed=8 * count * row_count * col_count,
            transcendentals=0,
        ),
        name="correlate",
    )(*operands)


def swap(value, axis, d):
    return lax.ppermute(value, axis, [(i, i ^ d) for i in range(lax.axis_size(axis))])


def after(values, earlier):
    if not earlier or not values:
        return list(values)
    return list(lax.optimization_barrier((tuple(values), tuple(earlier)))[0])


def shards(voltages, fir_taps):
    groups = lax.axis_size("freq")
    z, x, b = (lax.axis_index(name) for name in ("freq", "brow", "bcol"))
    streams = voltages.shape[1]
    block = streams * groups
    coarse = COARSE // groups
    paired = streams == 2 * TILE and groups == 4
    unit = coarse // 2 if paired else coarse
    known = []

    def note(value, parts):
        offset, last = 0, None
        for units, at, e in parts:
            row = None if e is None else (b ^ e) * block + at
            col = (x ^ 1) * block + at if e is None else x * block + at if e == 0 else None
            if units != last:
                known.append((value, offset, units, []))
            known[-1][3].append((row, col))
            offset, last = offset + len(units), units

    def fill(result, which, batch, mark=None):
        used = []
        for value, offset, units, wanted in known:
            if which in units:
                split = value.reshape((-1, len(units), unit) + value.shape[1:])
                index = offset // len(units) // len(wanted)
                used.append((split, len(wanted), index, units.index(which), wanted))
        return correlate(
            result, mark, used, which * unit, unit, coarse, 4 * block, 2 * block, batch
        )

    def join(pieces):
        return pieces[0][0] if len(pieces) == 1 else jnp.concatenate([p[0] for p in pieces], axis=0)

    def parts_of(pieces, e):
        return [(units, at, e) for _, parts in pieces for units, at in parts]

    freq_done, near_done = [], []

    def over_freq(pieces, earlier=()):
        values = after([piece[0] for piece, _ in pieces], freq_done + list(earlier))
        freq_done[:] = [swap(value, "freq", d) for value, (_, d) in zip(values, pieces)]
        return [(value, piece[1]) for value, (piece, _) in zip(freq_done, pieces)]

    def near(spread, inner, earlier=()):
        values = [join(spread)] if spread else []
        values += [join([piece for piece, _ in inner])] if inner else []
        values = after(values, near_done + list(earlier))
        near_done.clear()
        over_y = None
        if spread:
            value = values.pop(0)
            over_x, over_y = swap(value, "brow", 1), swap(value, "bcol", 2)
            near_done.extend([over_x, over_y])
            note(value, parts_of(spread, 0))
            note(over_x, parts_of(spread, None))
            note(over_y, parts_of(spread, 2))
            over_y = over_y, [part for _, parts in spread for part in parts]
        if inner:
            near_done.append(swap(values.pop(0), "bcol", 1))
            note(near_done[-1], [part for piece, e in inner for part in parts_of([piece], e ^ 1)])
        return over_y

    if paired:

        def made(tile, cuts):
            local = channelize(voltages, fir_taps, tile, z[None], groups, cuts)
            return {
                (d, first): (
                    local[d, first],
                    [
                        (
                            (0, 1) if count == coarse else (first // unit,),
                            (z ^ d) * streams + tile * TILE,
                        )
                    ],
                )
                for d, first, count in cuts
            }

        p = made(0, [(d, 0, coarse) for d in (2, 1, 3, 0)])
        own_a = p[0, 0]
        a2, a1 = over_freq([(p[2, 0], 2), (p[1, 0], 1)])
        y1 = near([own_a], [(own_a, 0)])
        r = made(
            1, [(0, 0, coarse), (1, 0, coarse)] + [(d, at, unit) for d in (2, 3) for at in (0, unit)]
        )
        own_b = r[0, 0]
        a3, b1 = over_freq([(p[3, 0], 3), (r[1, 0], 1)])
        y2 = near([a1, a2], [(y1, 2), (a1, 0), (a2, 0)], [own_b[0]])
        sent = freq_done + near_done
        b2, b3 = over_freq([(r[2, 0], 2), (r[3, 0], 3)], near_done)
        y3 = near([a3, own_b], [(y2, 2), (a3, 0), (own_b, 0)], sent)
        sent = freq_done + near_done
        c2, c3 = over_freq([(r[2, unit], 2), (r[3, unit], 3)], near_done)
        y4 = near([b1, b2, b3], [(y3, 2), (b1, 0), (b2, 0), (b3, 0)], sent)
        y5 = near([c2, c3], [(y4, 2)], freq_done)
        result, mark = fill(None, 0, 4)
        y5 = after([y5[0]], [mark])[0], y5[1]
        near([], [(y5, 2), (c2, 0), (c3, 0)], [mark])
        result, _ = fill(result, 1, 4, mark)
    else:
        padded = jnp.pad(voltages, ((0, 0), (0, -streams % TILE), (0, 0)))
        zero = jnp.zeros((1,), jnp.int32)
        cuts = [(d, 0, coarse) for d in range(groups)]
        local = [
            channelize(padded, fir_taps, tile, zero, groups, cuts)
            for tile in range(padded.shape[1] // TILE)
        ]
        local = jnp.concatenate(
            [jnp.concatenate([part[d, 0] for d in range(groups)], axis=0) for part in local], axis=1
        )[:, :streams]
        local = lax.all_to_all(local, "freq", 0, 1, tiled=True)
        own = local, [((0,), jnp.int32(0))]
        over_y = near([own], [(own, 0)])
        near([], [(over_y, 2)])
        result, _ = fill(None, 0, 1)
    return result.reshape(2, coarse, 4 * block, 2, 1, block)


def solution(mesh):
    in_specs = (P(None, ("brow", "bcol", "freq"), None), P())
    out_specs = P(None, "freq", "brow", None, "bcol", None)
    return jax.shard_map(shards, mesh=mesh, in_specs=in_specs, out_specs=out_specs, check_vma=False)
```

```python
import functools
import math

import jax
import jax.numpy as jnp
import numpy as np
from jax import lax
from jax.experimental import pallas as pl
from jax.experimental.pallas import tpu as pltpu
from jax.sharding import PartitionSpec as P

CHANNELS = 4096
TAPS = 16
AVG = 32
FRAMES = 8
COARSE = CHANNELS // AVG
FINE = FRAMES * AVG
TILE = 16
LANES = 128
PITCH = TILE + 1
VMEM = 63 << 20
CHUNKS = 4


def dft_table():
    index = np.arange(COARSE)
    angle = 2.0 * math.pi * (index[:, None] * index[None, :] % COARSE) / COARSE
    cosine, sine = np.cos(angle) / 64.0, np.sin(angle) / 64.0
    table = np.block([[cosine, sine], [-sine, cosine]]).astype(np.float32)
    high = table.astype(jnp.bfloat16)
    low = (table - high.astype(np.float32)).astype(jnp.bfloat16)
    return np.concatenate([high, high, low], axis=1)


def twiddles():
    angle = 2.0 * math.pi * np.arange(AVG)[:, None] * np.arange(LANES)[None, :] / CHANNELS
    return np.cos(angle).astype(np.float32), np.sin(angle).astype(np.float32)


def times(value, numerator, length):
    re, im = value
    numerator %= length
    if numerator == 0:
        return re, im
    if 4 * numerator == length:
        return im, -re
    if 2 * numerator == length:
        return -re, -im
    if 4 * numerator == 3 * length:
        return -im, re
    cosine = math.cos(2.0 * math.pi * numerator / length)
    sine = math.sin(2.0 * math.pi * numerator / length)
    if 8 * numerator == length:
        return (re + im) * cosine, (im - re) * cosine
    if 8 * numerator == 3 * length:
        return (im - re) * sine, (re + im) * -sine
    return re * cosine + im * sine, im * cosine - re * sine


def small_dft(values):
    length = len(values)
    if length == 1:
        return values
    even, odd = small_dft(values[0::2]), small_dft(values[1::2])
    odd = [times(value, k, length) for k, value in enumerate(odd)]
    return [(e[0] + o[0], e[1] + o[1]) for e, o in zip(even, odd)] + [
        (e[0] - o[0], e[1] - o[1]) for e, o in zip(even, odd)
    ]


def channelize_kernel(pieces, tile, z_ref, v_hbm, taps_ref, cos_ref, sin_ref, table_ref, *refs):
    count = len(pieces)
    outs, stages = refs[:count], refs[count : 2 * count]
    v_ref, filt, g_ref, in_sem, out_sem = refs[2 * count :]
    chunk = CHANNELS // CHUNKS
    spans = FRAMES + TAPS - 1
    rows = pl.ds(tile * TILE, TILE)
    for k in range(CHUNKS):
        for f in range(spans):
            lanes = pl.ds(f * CHANNELS + k * chunk, chunk)
            pltpu.make_async_copy(
                v_hbm.at[:, rows, lanes], v_ref.at[:, :, lanes], in_sem.at[k]
            ).start()

    for k in range(CHUNKS):
        lanes = pl.ds(0, spans * chunk)
        pltpu.make_async_copy(v_hbm.at[:, rows, lanes], v_ref.at[:, :, lanes], in_sem.at[k]).wait()

        @pl.loop(k * (chunk // LANES), (k + 1) * (chunk // LANES))
        def _(j):
            lane = pl.multiple_of(j * LANES, LANES)
            taps = [
                jnp.broadcast_to(taps_ref[p : p + 1, pl.ds(lane, LANES)], (8, LANES))
                for p in range(TAPS)
            ]
            for c, g in ((c, g) for c in range(2) for g in range(0, TILE, 8)):
                total = [None] * FRAMES
                for f in range(spans):
                    v = v_ref[c, :, pl.ds(f * CHANNELS + lane, LANES)].astype(jnp.float32)[g : g + 8]
                    for t in range(max(0, f - TAPS + 1), min(FRAMES, f + 1)):
                        term = taps[f - t] * v
                        total[t] = term if f == t else total[t] + term
                        if f - t == TAPS - 1:
                            filt[c, j, pl.ds(g * FRAMES + t, 8, stride=FRAMES), :] = total[t]

    def turned_fft(s):
        rows = pl.ds(pl.multiple_of(s * FRAMES, FRAMES), FRAMES)
        first = []
        for j0 in range(4):
            part = small_dft([(filt[0, j, rows, :], filt[1, j, rows, :]) for j in range(j0, AVG, 4)])
            first.append([times(value, j0 * ka, AVG) for ka, value in enumerate(part)])
        turned = [None] * AVG
        for ka in range(8):
            last = small_dft([first[j0][ka] for j0 in range(4)])
            for kb in range(4):
                k = ka + 8 * kb
                re, im = last[kb]
                if k:
                    cosine, sine = cos_ref[k : k + 1, :], sin_ref[k : k + 1, :]
                    re, im = re * cosine + im * sine, im * cosine - re * sine
                turned[k] = jnp.concatenate([re, im], axis=1)
        return turned

    @pl.loop(0, TILE, unroll=4)
    def _(s):
        value = jnp.concatenate(turned_fft(s), axis=0)
        high = value.astype(jnp.bfloat16)
        low = (value - high.astype(jnp.float32)).astype(jnp.bfloat16)
        spectrum = lax.dot_general(
            table_ref[...],
            jnp.concatenate([high, low, high], axis=1),
            (((1,), (1,)), ((), ())),
            preferred_element_type=jnp.float32,
        )
        for c in range(2):
            for h in range(FINE // LANES):
                g_ref[2 * c + h, pl.ds(s, COARSE, stride=PITCH), :] = spectrum[
                    c * COARSE : (c + 1) * COARSE, h * LANES : (h + 1) * LANES
                ]

    copies = []
    for n, ((d, start, size, width), out, stage) in enumerate(zip(pieces, outs, stages)):
        base = (z_ref[0] ^ d) * width + start

        @pl.loop(0, size, unroll=min(8, size))
        def _(q):
            at = pl.ds((base + q) * PITCH, TILE)
            stage[q] = jnp.concatenate([g_ref[i, at, :] for i in range(4)], axis=1).astype(
                jnp.bfloat16
            )

        copies.append(pltpu.make_async_copy(stage, out, out_sem.at[n]))
        copies[-1].start()
    for copy in copies:
        copy.wait()


def channelize(voltages, fir_taps, tile, z, groups, cuts):
    samples = voltages.shape[2]
    cosine, sine = twiddles()
    table = dft_table()
    whole = lambda shape: pl.BlockSpec(shape, lambda i: (0,) * len(shape))
    pieces = [(d, start, count, COARSE // groups) for d, start, count in cuts]
    shapes = [(count, TILE, 2 * FINE) for _, _, count, _ in pieces]
    outs = pl.pallas_call(
        functools.partial(channelize_kernel, pieces, tile),
        grid=(1,),
        in_specs=[
            pl.BlockSpec(memory_space=pltpu.SMEM),
            pl.BlockSpec(memory_space=pl.ANY),
            whole(fir_taps.shape),
            whole(cosine.shape),
            whole(sine.shape),
            whole(table.shape),
        ],
        out_specs=[pl.BlockSpec(memory_space=pl.ANY)] * len(shapes),
        out_shape=[jax.ShapeDtypeStruct(shape, jnp.bfloat16) for shape in shapes],
        scratch_shapes=[pltpu.VMEM(shape, jnp.bfloat16) for shape in shapes]
        + [
            pltpu.VMEM((2, TILE, samples), jnp.bfloat16),
            pltpu.VMEM((2, CHANNELS // LANES, TILE * FRAMES, LANES), jnp.float32),
            pltpu.VMEM((4, COARSE * PITCH, LANES), jnp.float32),
            pltpu.SemaphoreType.DMA((CHUNKS,)),
            pltpu.SemaphoreType.DMA((len(shapes),)),
        ],
        compiler_params=pltpu.CompilerParams(vmem_limit_bytes=VMEM),
        cost_estimate=pl.CostEstimate(
            flops=2 * 10**9, bytes_accessed=8 * 10**6, transcendentals=0
        ),
        name="channelize",
    )(z, voltages, fir_taps, jnp.asarray(cosine), jnp.asarray(sine), jnp.asarray(table))
    return {(d, start): out for (d, start, _, _), out in zip(pieces, outs)}


def correlate_kernel(batch, places, at_ref, *refs):
    groups, (out_ref, mark_ref, right) = refs[: len(places)], refs[-3:]
    mark_ref[...] = jnp.zeros_like(mark_ref)
    scale = 1.0 / FINE
    pieces = [
        (ref.at[n, 0], place) for ref, some in zip(groups, places) for n, place in enumerate(some)
    ]
    for q in range(batch):
        for ref, (_, col) in pieces:
            if col is not None:
                at = pl.multiple_of(at_ref[col], TILE)
                right[q, pl.ds(at, ref.shape[1]), :] = ref[q]
        rows = [(ref[q], row) for ref, (row, _) in pieces if row is not None]
        a, b = jnp.concatenate([value for value, _ in rows], axis=0), right[q]
        turned = jnp.concatenate([-b[:, FINE:], b[:, :FINE]], axis=1)
        parts = b.shape[0] // LANES
        for c, other in enumerate((b, turned)):
            product = scale * lax.dot_general(
                a, other, (((1,), (1,)), ((), ())), preferred_element_type=jnp.float32
            )
            start = 0
            for value, row in rows:
                size = value.shape[0]
                at = pl.multiple_of(at_ref[row] * parts, TILE * parts)
                for x in range(parts):
                    out_ref[c, q, pl.ds(at + x, size, stride=parts), :] = product[
                        start : start + size, x * LANES : (x + 1) * LANES
                    ]
                start += size


def correlate(result, mark, groups, start, count, coarse, row_count, col_count, batch):
    out_rows = row_count * col_count // LANES
    in_specs = [pl.BlockSpec(memory_space=pltpu.SMEM)]
    at, places = [], []
    for value, size, block, part, wanted in groups:
        shape = (size, 1, batch) + value.shape[3:]
        in_specs.append(
            pl.BlockSpec(shape, lambda i, block=block, part=part: (block, part, i, 0, 0))
        )
        places.append([])
        for pair in wanted:
            numbered = []
            for place in pair:
                numbered.append(None if place is None else len(at))
                at += [] if place is None else [place]
            places[-1].append(numbered)
    operands = [jnp.stack(at)] + [group[0] for group in groups]
    aliases = {}
    if result is not None:
        aliases = {len(operands): 0}
        operands += [result, mark]
        in_specs += [pl.BlockSpec(memory_space=pl.ANY)] * 2
    return pl.pallas_call(
        functools.partial(correlate_kernel, batch, places),
        grid=(count // batch,),
        in_specs=in_specs,
        out_specs=[
            pl.BlockSpec((2, batch, out_rows, LANES), lambda i: (0, i + start // batch, 0, 0)),
            pl.BlockSpec((8, LANES), lambda i: (0, 0)),
        ],
        out_shape=[
            jax.ShapeDtypeStruct((2, coarse, out_rows, LANES), jnp.float32),
            jax.ShapeDtypeStruct((8, LANES), jnp.float32),
        ],
        scratch_shapes=[pltpu.VMEM((batch, col_count, 2 * FINE), jnp.bfloat16)],
        input_output_aliases=aliases,
        compiler_params=pltpu.CompilerParams(vmem_limit_bytes=VMEM),
        cost_estimate=pl.CostEstimate(
            flops=20 * count * row_count * col_count * FINE,
            bytes_accessed=8 * count * row_count * col_count,
            transcendentals=0,
        ),
        name="correlate",
    )(*operands)


def join_kernel(*refs):
    parts, out, sem = refs[:-2], refs[-2], refs[-1]
    copies, offset = [], 0
    for i, part in enumerate(parts):
        size = part.shape[0]
        copies.append(pltpu.make_async_copy(part, out.at[pl.ds(offset, size)], sem.at[i]))
        copies[-1].start()
        offset += size
    for copy in copies:
        copy.wait()


def joined(parts):
    if len(parts) == 1:
        return parts[0]
    shape = (sum(part.shape[0] for part in parts),) + parts[0].shape[1:]
    return pl.pallas_call(
        join_kernel,
        in_specs=[pl.BlockSpec(memory_space=pl.ANY)] * len(parts),
        out_specs=pl.BlockSpec(memory_space=pl.ANY),
        out_shape=jax.ShapeDtypeStruct(shape, parts[0].dtype),
        scratch_shapes=[pltpu.SemaphoreType.DMA((len(parts),))],
        compiler_params=pltpu.CompilerParams(vmem_limit_bytes=VMEM),
        cost_estimate=pl.CostEstimate(
            flops=0, bytes_accessed=4 * math.prod(shape), transcendentals=0
        ),
        name="join",
    )(*parts)


def swap(value, axis, d):
    return lax.ppermute(value, axis, [(i, i ^ d) for i in range(lax.axis_size(axis))])


def after(values, earlier):
    if not earlier or not values:
        return list(values)
    return list(lax.optimization_barrier((tuple(values), tuple(earlier)))[0])


def shards(voltages, fir_taps):
    groups = lax.axis_size("freq")
    z, x, b = (lax.axis_index(name) for name in ("freq", "brow", "bcol"))
    streams = voltages.shape[1]
    block = streams * groups
    coarse = COARSE // groups
    paired = streams == 2 * TILE and groups == 4
    unit = coarse // 2 if paired else coarse
    known = []

    def note(value, parts):
        offset, last = 0, None
        for units, at, e in parts:
            row = None if e is None else (b ^ e) * block + at
            col = (x ^ 1) * block + at if e is None else x * block + at if e == 0 else None
            if units != last:
                known.append((value, offset, units, []))
            known[-1][3].append((row, col))
            offset, last = offset + len(units), units

    def fill(result, which, batch, mark=None):
        used = []
        for value, offset, units, wanted in known:
            if which in units:
                split = value.reshape((-1, len(units), unit) + value.shape[1:])
                index = offset // len(units) // len(wanted)
                used.append((split, len(wanted), index, units.index(which), wanted))
        return correlate(
            result, mark, used, which * unit, unit, coarse, 4 * block, 2 * block, batch
        )

    def join(pieces):
        return joined([piece[0] for piece in pieces])

    def parts_of(pieces, e):
        return [(units, at, e) for _, parts in pieces for units, at in parts]

    freq_done, near_done = [], []

    def over_freq(pieces, earlier=()):
        values = after([piece[0] for piece, _ in pieces], freq_done + list(earlier))
        freq_done[:] = [swap(value, "freq", d) for value, (_, d) in zip(values, pieces)]
        return [(value, piece[1]) for value, (piece, _) in zip(freq_done, pieces)]

    def near(spread, inner, earlier=()):
        values = [join(spread)] if spread else []
        values += [join([piece for piece, _ in inner])] if inner else []
        values = after(values, near_done + list(earlier))
        near_done.clear()
        over_y = None
        if spread:
            value = values.pop(0)
            over_x, over_y = swap(value, "brow", 1), swap(value, "bcol", 2)
            near_done.extend([over_x, over_y])
            note(value, parts_of(spread, 0))
            note(over_x, parts_of(spread, None))
            note(over_y, parts_of(spread, 2))
            over_y = over_y, [part for _, parts in spread for part in parts]
        if inner:
            near_done.append(swap(values.pop(0), "bcol", 1))
            note(near_done[-1], [part for piece, e in inner for part in parts_of([piece], e ^ 1)])
        return over_y

    if paired:

        def made(tile, cuts):
            local = channelize(voltages, fir_taps, tile, z[None], groups, cuts)
            return {
                (d, first): (
                    local[d, first],
                    [
                        (
                            (0, 1) if count == coarse else (first // unit,),
                            (z ^ d) * streams + tile * TILE,
                        )
                    ],
                )
                for d, first, count in cuts
            }

        p = made(0, [(d, 0, coarse) for d in (2, 1, 3, 0)])
        own_a = p[0, 0]
        a2, a1 = over_freq([(p[2, 0], 2), (p[1, 0], 1)])
        y1 = near([own_a], [(own_a, 0)])
        r = made(
            1, [(0, 0, coarse), (1, 0, coarse)] + [(d, at, unit) for d in (2, 3) for at in (0, unit)]
        )
        own_b = r[0, 0]
        a3, b1 = over_freq([(p[3, 0], 3), (r[1, 0], 1)])
        y2 = near([a1, a2], [(y1, 2), (a1, 0), (a2, 0)], [own_b[0]])
        sent = freq_done + near_done
        b2, b3 = over_freq([(r[2, 0], 2), (r[3, 0], 3)], near_done)
        y3 = near([a3, own_b], [(y2, 2), (a3, 0), (own_b, 0)], sent)
        sent = freq_done + near_done
        c2, c3 = over_freq([(r[2, unit], 2), (r[3, unit], 3)], near_done)
        y4 = near([b1, b2, b3], [(y3, 2), (b1, 0), (b2, 0), (b3, 0)], sent)
        y5 = near([c2, c3], [(y4, 2)], freq_done)
        result, mark = fill(None, 0, 4)
        y5 = after([y5[0]], [mark])[0], y5[1]
        near([], [(y5, 2), (c2, 0), (c3, 0)], [mark])
        result, _ = fill(result, 1, 4, mark)
    else:
        padded = jnp.pad(voltages, ((0, 0), (0, -streams % TILE), (0, 0)))
        zero = jnp.zeros((1,), jnp.int32)
        cuts = [(d, 0, coarse) for d in range(groups)]
        local = [
            channelize(padded, fir_taps, tile, zero, groups, cuts)
            for tile in range(padded.shape[1] // TILE)
        ]
        local = jnp.concatenate(
            [jnp.concatenate([part[d, 0] for d in range(groups)], axis=0) for part in local], axis=1
        )[:, :streams]
        local = lax.all_to_all(local, "freq", 0, 1, tiled=True)
        own = local, [((0,), jnp.int32(0))]
        over_y = near([own], [(own, 0)])
        near([], [(over_y, 2)])
        result, _ = fill(None, 0, 1)
    return result.reshape(2, coarse, 4 * block, 2, 1, block)


def solution(mesh):
    in_specs = (P(None, ("brow", "bcol", "freq"), None), P())
    out_specs = P(None, "freq", "brow", None, "bcol", None)
    return jax.shard_map(shards, mesh=mesh, in_specs=in_specs, out_specs=out_specs, check_vma=False)
```

```python
import functools
import math

import jax
import jax.numpy as jnp
import numpy as np
from jax import lax
from jax.experimental import pallas as pl
from jax.experimental.pallas import tpu as pltpu
from jax.sharding import PartitionSpec as P

CHANNELS = 4096
TAPS = 16
AVG = 32
FRAMES = 8
COARSE = CHANNELS // AVG
FINE = FRAMES * AVG
TILE = 16
LANES = 128
PITCH = TILE + 1
VMEM = 63 << 20
CHUNKS = 4


def dft_table():
    index = np.arange(COARSE)
    angle = 2.0 * math.pi * (index[:, None] * index[None, :] % COARSE) / COARSE
    cosine, sine = np.cos(angle) / 64.0, np.sin(angle) / 64.0
    table = np.block([[cosine, sine], [-sine, cosine]]).astype(np.float32)
    high = table.astype(jnp.bfloat16)
    low = (table - high.astype(np.float32)).astype(jnp.bfloat16)
    return np.concatenate([high, high, low], axis=1)


def twiddles():
    angle = 2.0 * math.pi * np.arange(AVG)[:, None] * np.arange(LANES)[None, :] / CHANNELS
    return np.cos(angle).astype(np.float32), np.sin(angle).astype(np.float32)


def times(value, numerator, length):
    re, im = value
    numerator %= length
    if numerator == 0:
        return re, im
    if 4 * numerator == length:
        return im, -re
    if 2 * numerator == length:
        return -re, -im
    if 4 * numerator == 3 * length:
        return -im, re
    cosine = math.cos(2.0 * math.pi * numerator / length)
    sine = math.sin(2.0 * math.pi * numerator / length)
    if 8 * numerator == length:
        return (re + im) * cosine, (im - re) * cosine
    if 8 * numerator == 3 * length:
        return (im - re) * sine, (re + im) * -sine
    return re * cosine + im * sine, im * cosine - re * sine


def small_dft(values):
    length = len(values)
    if length == 1:
        return values
    even, odd = small_dft(values[0::2]), small_dft(values[1::2])
    odd = [times(value, k, length) for k, value in enumerate(odd)]
    return [(e[0] + o[0], e[1] + o[1]) for e, o in zip(even, odd)] + [
        (e[0] - o[0], e[1] - o[1]) for e, o in zip(even, odd)
    ]


def channelize_kernel(pieces, tile, z_ref, v_hbm, taps_ref, cos_ref, sin_ref, table_ref, *refs):
    count = len(pieces)
    outs, stages = refs[:count], refs[count : 2 * count]
    v_ref, filt, g_ref, in_sem, out_sem = refs[2 * count :]
    chunk = CHANNELS // CHUNKS
    spans = FRAMES + TAPS - 1
    rows = pl.ds(tile * TILE, TILE)
    for k in range(CHUNKS):
        for f in range(spans):
            lanes = pl.ds(f * CHANNELS + k * chunk, chunk)
            pltpu.make_async_copy(
                v_hbm.at[:, rows, lanes], v_ref.at[:, :, lanes], in_sem.at[k]
            ).start()

    for k in range(CHUNKS):
        lanes = pl.ds(0, spans * chunk)
        pltpu.make_async_copy(v_hbm.at[:, rows, lanes], v_ref.at[:, :, lanes], in_sem.at[k]).wait()

        @pl.loop(k * (chunk // LANES), (k + 1) * (chunk // LANES))
        def _(j):
            lane = pl.multiple_of(j * LANES, LANES)
            taps = [
                jnp.broadcast_to(taps_ref[p : p + 1, pl.ds(lane, LANES)], (8, LANES))
                for p in range(TAPS)
            ]
            for c, g in ((c, g) for c in range(2) for g in range(0, TILE, 8)):
                total = [None] * FRAMES
                for f in range(spans):
                    v = v_ref[c, :, pl.ds(f * CHANNELS + lane, LANES)].astype(jnp.float32)[g : g + 8]
                    for t in range(max(0, f - TAPS + 1), min(FRAMES, f + 1)):
                        term = taps[f - t] * v
                        total[t] = term if f == t else total[t] + term
                        if f - t == TAPS - 1:
                            filt[c, j, pl.ds(g * FRAMES + t, 8, stride=FRAMES), :] = total[t]

    def turned_fft(s):
        rows = pl.ds(pl.multiple_of(s * FRAMES, FRAMES), FRAMES)
        first = []
        for j0 in range(4):
            part = small_dft([(filt[0, j, rows, :], filt[1, j, rows, :]) for j in range(j0, AVG, 4)])
            first.append([times(value, j0 * ka, AVG) for ka, value in enumerate(part)])
        turned = [None] * AVG
        for ka in range(8):
            last = small_dft([first[j0][ka] for j0 in range(4)])
            for kb in range(4):
                k = ka + 8 * kb
                re, im = last[kb]
                if k:
                    cosine, sine = cos_ref[k : k + 1, :], sin_ref[k : k + 1, :]
                    re, im = re * cosine + im * sine, im * cosine - re * sine
                turned[k] = jnp.concatenate([re, im], axis=1)
        return turned

    @pl.loop(0, TILE, unroll=4)
    def _(s):
        value = jnp.concatenate(turned_fft(s), axis=0)
        high = value.astype(jnp.bfloat16)
        low = (value - high.astype(jnp.float32)).astype(jnp.bfloat16)
        spectrum = lax.dot_general(
            table_ref[...],
            jnp.concatenate([high, low, high], axis=1),
            (((1,), (1,)), ((), ())),
            preferred_element_type=jnp.float32,
        )
        for c in range(2):
            for h in range(FINE // LANES):
                g_ref[2 * c + h, pl.ds(s, COARSE, stride=PITCH), :] = spectrum[
                    c * COARSE : (c + 1) * COARSE, h * LANES : (h + 1) * LANES
                ]

    copies = []
    for n, ((d, start, size, width), out, stage) in enumerate(zip(pieces, outs, stages)):
        base = (z_ref[0] ^ d) * width + start

        @pl.loop(0, size, unroll=min(8, size))
        def _(q):
            at = pl.ds((base + q) * PITCH, TILE)
            stage[q] = jnp.concatenate([g_ref[i, at, :] for i in range(4)], axis=1).astype(
                jnp.bfloat16
            )

        copies.append(pltpu.make_async_copy(stage, out, out_sem.at[n]))
        copies[-1].start()
    for copy in copies:
        copy.wait()


def channelize(voltages, fir_taps, tile, z, groups, cuts):
    samples = voltages.shape[2]
    cosine, sine = twiddles()
    table = dft_table()
    whole = lambda shape: pl.BlockSpec(shape, lambda i: (0,) * len(shape))
    pieces = [(d, start, count, COARSE // groups) for d, start, count in cuts]
    shapes = [(count, TILE, 2 * FINE) for _, _, count, _ in pieces]
    outs = pl.pallas_call(
        functools.partial(channelize_kernel, pieces, tile),
        grid=(1,),
        in_specs=[
            pl.BlockSpec(memory_space=pltpu.SMEM),
            pl.BlockSpec(memory_space=pl.ANY),
            whole(fir_taps.shape),
            whole(cosine.shape),
            whole(sine.shape),
            whole(table.shape),
        ],
        out_specs=[pl.BlockSpec(memory_space=pl.ANY)] * len(shapes),
        out_shape=[jax.ShapeDtypeStruct(shape, jnp.bfloat16) for shape in shapes],
        scratch_shapes=[pltpu.VMEM(shape, jnp.bfloat16) for shape in shapes]
        + [
            pltpu.VMEM((2, TILE, samples), jnp.bfloat16),
            pltpu.VMEM((2, CHANNELS // LANES, TILE * FRAMES, LANES), jnp.float32),
            pltpu.VMEM((4, COARSE * PITCH, LANES), jnp.float32),
            pltpu.SemaphoreType.DMA((CHUNKS,)),
            pltpu.SemaphoreType.DMA((len(shapes),)),
        ],
        compiler_params=pltpu.CompilerParams(vmem_limit_bytes=VMEM),
        cost_estimate=pl.CostEstimate(
            flops=2 * 10**9, bytes_accessed=8 * 10**6, transcendentals=0
        ),
        name="channelize",
    )(z, voltages, fir_taps, jnp.asarray(cosine), jnp.asarray(sine), jnp.asarray(table))
    return {(d, start): out for (d, start, _, _), out in zip(pieces, outs)}


def correlate_kernel(batch, places, at_ref, *refs):
    groups, (out_ref, mark_ref, right) = refs[: len(places)], refs[-3:]
    mark_ref[...] = jnp.zeros_like(mark_ref)
    scale = 1.0 / FINE
    pieces = [
        (ref.at[n, 0], place) for ref, some in zip(groups, places) for n, place in enumerate(some)
    ]
    for q in range(batch):
        for ref, (_, col) in pieces:
            if col is not None:
                at = pl.multiple_of(at_ref[col], TILE)
                right[q, pl.ds(at, ref.shape[1]), :] = ref[q]
        rows = [(ref[q], row) for ref, (row, _) in pieces if row is not None]
        a, b = jnp.concatenate([value for value, _ in rows], axis=0), right[q]
        turned = jnp.concatenate([-b[:, FINE:], b[:, :FINE]], axis=1)
        parts = b.shape[0] // LANES
        for c, other in enumerate((b, turned)):
            product = scale * lax.dot_general(
                a, other, (((1,), (1,)), ((), ())), preferred_element_type=jnp.float32
            )
            start = 0
            for value, row in rows:
                size = value.shape[0]
                at = pl.multiple_of(at_ref[row] * parts, TILE * parts)
                for x in range(parts):
                    out_ref[c, q, pl.ds(at + x, size, stride=parts), :] = product[
                        start : start + size, x * LANES : (x + 1) * LANES
                    ]
                start += size


def correlate(result, mark, groups, start, count, coarse, row_count, col_count, batch):
    out_rows = row_count * col_count // LANES
    in_specs = [pl.BlockSpec(memory_space=pltpu.SMEM)]
    at, places = [], []
    for value, size, block, part, wanted in groups:
        shape = (size, 1, batch) + value.shape[3:]
        in_specs.append(
            pl.BlockSpec(shape, lambda i, block=block, part=part: (block, part, i, 0, 0))
        )
        places.append([])
        for pair in wanted:
            numbered = []
            for place in pair:
                numbered.append(None if place is None else len(at))
                at += [] if place is None else [place]
            places[-1].append(numbered)
    operands = [jnp.stack(at)] + [group[0] for group in groups]
    aliases = {}
    if result is not None:
        aliases = {len(operands): 0}
        operands += [result, mark]
        in_specs += [pl.BlockSpec(memory_space=pl.ANY)] * 2
    return pl.pallas_call(
        functools.partial(correlate_kernel, batch, places),
        grid=(count // batch,),
        in_specs=in_specs,
        out_specs=[
            pl.BlockSpec((2, batch, out_rows, LANES), lambda i: (0, i + start // batch, 0, 0)),
            pl.BlockSpec((8, LANES), lambda i: (0, 0)),
        ],
        out_shape=[
            jax.ShapeDtypeStruct((2, coarse, out_rows, LANES), jnp.float32),
            jax.ShapeDtypeStruct((8, LANES), jnp.float32),
        ],
        scratch_shapes=[pltpu.VMEM((batch, col_count, 2 * FINE), jnp.bfloat16)],
        input_output_aliases=aliases,
        compiler_params=pltpu.CompilerParams(vmem_limit_bytes=VMEM),
        cost_estimate=pl.CostEstimate(
            flops=20 * count * row_count * col_count * FINE,
            bytes_accessed=8 * count * row_count * col_count,
            transcendentals=0,
        ),
        name="correlate",
    )(*operands)


def join_kernel(*refs):
    parts, (out, held, in_sem, out_sem) = refs[:-4], refs[-4:]
    spans, offset = [], 0
    for part in parts:
        spans.append(pl.ds(offset, part.shape[0]))
        offset += part.shape[0]
    loads = [
        pltpu.make_async_copy(part, held.at[span], in_sem.at[i])
        for i, (part, span) in enumerate(zip(parts, spans))
    ]
    stores = [
        pltpu.make_async_copy(held.at[span], out.at[span], out_sem.at[i])
        for i, span in enumerate(spans)
    ]
    for load in loads:
        load.start()
    for load, store in zip(loads, stores):
        load.wait()
        store.start()
    for store in stores:
        store.wait()


def joined(parts):
    if len(parts) == 1:
        return parts[0]
    shape = (sum(part.shape[0] for part in parts),) + parts[0].shape[1:]
    return pl.pallas_call(
        join_kernel,
        in_specs=[pl.BlockSpec(memory_space=pl.ANY)] * len(parts),
        out_specs=pl.BlockSpec(memory_space=pl.ANY),
        out_shape=jax.ShapeDtypeStruct(shape, parts[0].dtype),
        scratch_shapes=[pltpu.VMEM(shape, parts[0].dtype)]
        + [pltpu.SemaphoreType.DMA((len(parts),))] * 2,
        compiler_params=pltpu.CompilerParams(vmem_limit_bytes=VMEM),
        cost_estimate=pl.CostEstimate(
            flops=0, bytes_accessed=4 * math.prod(shape), transcendentals=0
        ),
        name="join",
    )(*parts)


def swap(value, axis, d):
    return lax.ppermute(value, axis, [(i, i ^ d) for i in range(lax.axis_size(axis))])


def after(values, earlier):
    if not earlier or not values:
        return list(values)
    return list(lax.optimization_barrier((tuple(values), tuple(earlier)))[0])


def shards(voltages, fir_taps):
    groups = lax.axis_size("freq")
    z, x, b = (lax.axis_index(name) for name in ("freq", "brow", "bcol"))
    streams = voltages.shape[1]
    block = streams * groups
    coarse = COARSE // groups
    paired = streams == 2 * TILE and groups == 4
    unit = coarse // 2 if paired else coarse
    known = []

    def note(value, parts):
        offset, last = 0, None
        for units, at, e in parts:
            row = None if e is None else (b ^ e) * block + at
            col = (x ^ 1) * block + at if e is None else x * block + at if e == 0 else None
            if units != last:
                known.append((value, offset, units, []))
            known[-1][3].append((row, col))
            offset, last = offset + len(units), units

    def fill(result, which, batch, mark=None):
        used = []
        for value, offset, units, wanted in known:
            if which in units:
                split = value.reshape((-1, len(units), unit) + value.shape[1:])
                index = offset // len(units) // len(wanted)
                used.append((split, len(wanted), index, units.index(which), wanted))
        return correlate(
            result, mark, used, which * unit, unit, coarse, 4 * block, 2 * block, batch
        )

    def join(pieces):
        return joined([piece[0] for piece in pieces])

    def parts_of(pieces, e):
        return [(units, at, e) for _, parts in pieces for units, at in parts]

    freq_done, near_done = [], []

    def over_freq(pieces, earlier=()):
        values = after([piece[0] for piece, _ in pieces], freq_done + list(earlier))
        freq_done[:] = [swap(value, "freq", d) for value, (_, d) in zip(values, pieces)]
        return [(value, piece[1]) for value, (piece, _) in zip(freq_done, pieces)]

    def near(spread, inner, earlier=()):
        values = [join(spread)] if spread else []
        values += [join([piece for piece, _ in inner])] if inner else []
        values = after(values, near_done + list(earlier))
        near_done.clear()
        over_y = None
        if spread:
            value = values.pop(0)
            over_x, over_y = swap(value, "brow", 1), swap(value, "bcol", 2)
            near_done.extend([over_x, over_y])
            note(value, parts_of(spread, 0))
            note(over_x, parts_of(spread, None))
            note(over_y, parts_of(spread, 2))
            over_y = over_y, [part for _, parts in spread for part in parts]
        if inner:
            near_done.append(swap(values.pop(0), "bcol", 1))
            note(near_done[-1], [part for piece, e in inner for part in parts_of([piece], e ^ 1)])
        return over_y

    if paired:

        def made(tile, cuts):
            local = channelize(voltages, fir_taps, tile, z[None], groups, cuts)
            return {
                (d, first): (
                    local[d, first],
                    [
                        (
                            (0, 1) if count == coarse else (first // unit,),
                            (z ^ d) * streams + tile * TILE,
                        )
                    ],
                )
                for d, first, count in cuts
            }

        p = made(0, [(d, 0, coarse) for d in (2, 1, 3, 0)])
        own_a = p[0, 0]
        a2, a1 = over_freq([(p[2, 0], 2), (p[1, 0], 1)])
        y1 = near([own_a], [(own_a, 0)])
        r = made(
            1, [(0, 0, coarse), (1, 0, coarse)] + [(d, at, unit) for d in (2, 3) for at in (0, unit)]
        )
        own_b = r[0, 0]
        a3, b1 = over_freq([(p[3, 0], 3), (r[1, 0], 1)])
        y2 = near([a1, a2], [(y1, 2), (a1, 0), (a2, 0)], [own_b[0]])
        sent = freq_done + near_done
        b2, b3 = over_freq([(r[2, 0], 2), (r[3, 0], 3)], near_done)
        y3 = near([a3, own_b], [(y2, 2), (a3, 0), (own_b, 0)], sent)
        sent = freq_done + near_done
        c2, c3 = over_freq([(r[2, unit], 2), (r[3, unit], 3)], near_done)
        y4 = near([b1, b2, b3], [(y3, 2), (b1, 0), (b2, 0), (b3, 0)], sent)
        y5 = near([c2, c3], [(y4, 2)], freq_done)
        result, mark = fill(None, 0, 4)
        y5 = after([y5[0]], [mark])[0], y5[1]
        near([], [(y5, 2), (c2, 0), (c3, 0)], [mark])
        result, _ = fill(result, 1, 4, mark)
    else:
        padded = jnp.pad(voltages, ((0, 0), (0, -streams % TILE), (0, 0)))
        zero = jnp.zeros((1,), jnp.int32)
        cuts = [(d, 0, coarse) for d in range(groups)]
        local = [
            channelize(padded, fir_taps, tile, zero, groups, cuts)
            for tile in range(padded.shape[1] // TILE)
        ]
        local = jnp.concatenate(
            [jnp.concatenate([part[d, 0] for d in range(groups)], axis=0) for part in local], axis=1
        )[:, :streams]
        local = lax.all_to_all(local, "freq", 0, 1, tiled=True)
        own = local, [((0,), jnp.int32(0))]
        over_y = near([own], [(own, 0)])
        near([], [(over_y, 2)])
        result, _ = fill(None, 0, 1)
    return result.reshape(2, coarse, 4 * block, 2, 1, block)


def solution(mesh):
    in_specs = (P(None, ("brow", "bcol", "freq"), None), P())
    out_specs = P(None, "freq", "brow", None, "bcol", None)
    return jax.shard_map(shards, mesh=mesh, in_specs=in_specs, out_specs=out_specs, check_vma=False)
```

```python
import functools
import math

import jax
import jax.numpy as jnp
import numpy as np
from jax import lax
from jax.experimental import pallas as pl
from jax.experimental.pallas import tpu as pltpu
from jax.sharding import PartitionSpec as P

CHANNELS = 4096
TAPS = 16
AVG = 32
FRAMES = 8
COARSE = CHANNELS // AVG
FINE = FRAMES * AVG
TILE = 16
LANES = 128
PITCH = TILE + 1
VMEM = 60 << 20
CHUNKS = 4


def dft_table():
    index = np.arange(COARSE)
    angle = 2.0 * math.pi * (index[:, None] * index[None, :] % COARSE) / COARSE
    cosine, sine = np.cos(angle) / 64.0, np.sin(angle) / 64.0
    table = np.block([[cosine, sine], [-sine, cosine]]).astype(np.float32)
    high = table.astype(jnp.bfloat16)
    low = (table - high.astype(np.float32)).astype(jnp.bfloat16)
    return np.concatenate([high, high, low], axis=1)


def twiddles():
    angle = 2.0 * math.pi * np.arange(AVG)[:, None] * np.arange(LANES)[None, :] / CHANNELS
    return np.cos(angle).astype(np.float32), np.sin(angle).astype(np.float32)


def times(value, numerator, length):
    re, im = value
    numerator %= length
    if numerator == 0:
        return re, im
    if 4 * numerator == length:
        return im, -re
    if 2 * numerator == length:
        return -re, -im
    if 4 * numerator == 3 * length:
        return -im, re
    cosine = math.cos(2.0 * math.pi * numerator / length)
    sine = math.sin(2.0 * math.pi * numerator / length)
    if 8 * numerator == length:
        return (re + im) * cosine, (im - re) * cosine
    if 8 * numerator == 3 * length:
        return (im - re) * sine, (re + im) * -sine
    return re * cosine + im * sine, im * cosine - re * sine


def small_dft(values):
    length = len(values)
    if length == 1:
        return values
    even, odd = small_dft(values[0::2]), small_dft(values[1::2])
    odd = [times(value, k, length) for k, value in enumerate(odd)]
    return [(e[0] + o[0], e[1] + o[1]) for e, o in zip(even, odd)] + [
        (e[0] - o[0], e[1] - o[1]) for e, o in zip(even, odd)
    ]


def channelize_kernel(pieces, tile, z_ref, v_hbm, taps_ref, cos_ref, sin_ref, table_ref, *refs):
    count = len(pieces)
    outs, stages = refs[:count], refs[count : 2 * count]
    v_ref, filt, g_ref, in_sem, out_sem = refs[2 * count :]
    chunk = CHANNELS // CHUNKS
    spans = FRAMES + TAPS - 1
    rows = pl.ds(tile * TILE, TILE)
    for k in range(CHUNKS):
        for f in range(spans):
            lanes = pl.ds(f * CHANNELS + k * chunk, chunk)
            pltpu.make_async_copy(
                v_hbm.at[:, rows, lanes], v_ref.at[:, :, lanes], in_sem.at[k]
            ).start()

    for k in range(CHUNKS):
        lanes = pl.ds(0, spans * chunk)
        pltpu.make_async_copy(v_hbm.at[:, rows, lanes], v_ref.at[:, :, lanes], in_sem.at[k]).wait()

        @pl.loop(k * (chunk // LANES), (k + 1) * (chunk // LANES))
        def _(j):
            lane = pl.multiple_of(j * LANES, LANES)
            taps = [
                jnp.broadcast_to(taps_ref[p : p + 1, pl.ds(lane, LANES)], (TILE, LANES))
                for p in range(TAPS)
            ]
            for c in range(2):
                total = [None] * FRAMES
                for f in range(spans):
                    v = v_ref[c, :, pl.ds(f * CHANNELS + lane, LANES)].astype(jnp.float32)
                    for t in range(max(0, f - TAPS + 1), min(FRAMES, f + 1)):
                        term = taps[f - t] * v
                        total[t] = term if f == t else total[t] + term
                        if f - t == TAPS - 1:
                            filt[c, j, pl.ds(t, TILE, stride=FRAMES), :] = total[t]

    def turned_fft(s):
        rows = pl.ds(pl.multiple_of(s * FRAMES, FRAMES), FRAMES)
        first = []
        for j0 in range(4):
            part = small_dft([(filt[0, j, rows, :], filt[1, j, rows, :]) for j in range(j0, AVG, 4)])
            first.append([times(value, j0 * ka, AVG) for ka, value in enumerate(part)])
        turned = [None] * AVG
        for ka in range(8):
            last = small_dft([first[j0][ka] for j0 in range(4)])
            for kb in range(4):
                k = ka + 8 * kb
                re, im = last[kb]
                if k:
                    cosine, sine = cos_ref[k : k + 1, :], sin_ref[k : k + 1, :]
                    re, im = re * cosine + im * sine, im * cosine - re * sine
                turned[k] = jnp.concatenate([re, im], axis=1)
        return turned

    @pl.loop(0, TILE, unroll=4)
    def _(s):
        value = jnp.concatenate(turned_fft(s), axis=0)
        high = value.astype(jnp.bfloat16)
        low = (value - high.astype(jnp.float32)).astype(jnp.bfloat16)
        spectrum = lax.dot_general(
            table_ref[...],
            jnp.concatenate([high, low, high], axis=1),
            (((1,), (1,)), ((), ())),
            preferred_element_type=jnp.float32,
        )
        for c in range(2):
            for h in range(FINE // LANES):
                g_ref[2 * c + h, pl.ds(s, COARSE, stride=PITCH), :] = spectrum[
                    c * COARSE : (c + 1) * COARSE, h * LANES : (h + 1) * LANES
                ]

    copies = []
    for n, ((d, start, size, width), out, stage) in enumerate(zip(pieces, outs, stages)):
        base = (z_ref[0] ^ d) * width + start

        @pl.loop(0, size, unroll=min(8, size))
        def _(q):
            at = pl.ds((base + q) * PITCH, TILE)
            stage[q] = jnp.concatenate([g_ref[i, at, :] for i in range(4)], axis=1).astype(
                jnp.bfloat16
            )

        copies.append(pltpu.make_async_copy(stage, out, out_sem.at[n]))
        copies[-1].start()
    for copy in copies:
        copy.wait()


def channelize(voltages, fir_taps, tile, z, groups, cuts):
    samples = voltages.shape[2]
    cosine, sine = twiddles()
    table = dft_table()
    whole = lambda shape: pl.BlockSpec(shape, lambda i: (0,) * len(shape))
    pieces = [(d, start, count, COARSE // groups) for d, start, count in cuts]
    shapes = [(count, TILE, 2 * FINE) for _, _, count, _ in pieces]
    outs = pl.pallas_call(
        functools.partial(channelize_kernel, pieces, tile),
        grid=(1,),
        in_specs=[
            pl.BlockSpec(memory_space=pltpu.SMEM),
            pl.BlockSpec(memory_space=pl.ANY),
            whole(fir_taps.shape),
            whole(cosine.shape),
            whole(sine.shape),
            whole(table.shape),
        ],
        out_specs=[pl.BlockSpec(memory_space=pl.ANY)] * len(shapes),
        out_shape=[jax.ShapeDtypeStruct(shape, jnp.bfloat16) for shape in shapes],
        scratch_shapes=[pltpu.VMEM(shape, jnp.bfloat16) for shape in shapes]
        + [
            pltpu.VMEM((2, TILE, samples), jnp.bfloat16),
            pltpu.VMEM((2, CHANNELS // LANES, TILE * FRAMES, LANES), jnp.float32),
            pltpu.VMEM((4, COARSE * PITCH, LANES), jnp.float32),
            pltpu.SemaphoreType.DMA((CHUNKS,)),
            pltpu.SemaphoreType.DMA((len(shapes),)),
        ],
        compiler_params=pltpu.CompilerParams(vmem_limit_bytes=VMEM),
        cost_estimate=pl.CostEstimate(
            flops=2 * 10**9, bytes_accessed=8 * 10**6, transcendentals=0
        ),
        name="channelize",
    )(z, voltages, fir_taps, jnp.asarray(cosine), jnp.asarray(sine), jnp.asarray(table))
    return {(d, start): out for (d, start, _, _), out in zip(pieces, outs)}


def correlate_kernel(batch, places, at_ref, *refs):
    groups, (out_ref, mark_ref, right) = refs[: len(places)], refs[-3:]
    mark_ref[...] = jnp.zeros_like(mark_ref)
    scale = 1.0 / FINE
    pieces = [
        (ref.at[n], place) for ref, some in zip(groups, places) for n, place in enumerate(some)
    ]
    for q in range(batch):
        for ref, (_, col) in pieces:
            if col is not None:
                at = pl.multiple_of(at_ref[col], TILE)
                right[q, pl.ds(at, ref.shape[1]), :] = ref[q]
        rows = [(ref[q], row) for ref, (row, _) in pieces if row is not None]
        a, b = jnp.concatenate([value for value, _ in rows], axis=0), right[q]
        turned = jnp.concatenate([-b[:, FINE:], b[:, :FINE]], axis=1)
        parts = b.shape[0] // LANES
        for c, other in enumerate((b, turned)):
            product = scale * lax.dot_general(
                a, other, (((1,), (1,)), ((), ())), preferred_element_type=jnp.float32
            )
            start = 0
            for value, row in rows:
                size = value.shape[0]
                at = pl.multiple_of(at_ref[row] * parts, TILE * parts)
                for x in range(parts):
                    out_ref[c, q, pl.ds(at + x, size, stride=parts), :] = product[
                        start : start + size, x * LANES : (x + 1) * LANES
                    ]
                start += size


def correlate(result, mark, groups, start, count, coarse, row_count, col_count, batch):
    out_rows = row_count * col_count // LANES
    in_specs = [pl.BlockSpec(memory_space=pltpu.SMEM)]
    at, places = [], []
    for value, skip, wanted in groups:
        shape = (value.shape[0], batch) + value.shape[2:]
        in_specs.append(pl.BlockSpec(shape, lambda i, skip=skip // batch: (0, i + skip, 0, 0)))
        places.append([])
        for pair in wanted:
            numbered = []
            for place in pair:
                numbered.append(None if place is None else len(at))
                at += [] if place is None else [place]
            places[-1].append(numbered)
    operands = [jnp.stack(at)] + [group[0] for group in groups]
    aliases = {}
    if result is not None:
        aliases = {len(operands): 0}
        operands += [result, mark]
        in_specs += [pl.BlockSpec(memory_space=pl.ANY)] * 2
    return pl.pallas_call(
        functools.partial(correlate_kernel, batch, places),
        grid=(count // batch,),
        in_specs=in_specs,
        out_specs=[
            pl.BlockSpec((2, batch, out_rows, LANES), lambda i: (0, i + start // batch, 0, 0)),
            pl.BlockSpec((8, LANES), lambda i: (0, 0)),
        ],
        out_shape=[
            jax.ShapeDtypeStruct((2, coarse, out_rows, LANES), jnp.float32),
            jax.ShapeDtypeStruct((8, LANES), jnp.float32),
        ],
        scratch_shapes=[pltpu.VMEM((batch, col_count, 2 * FINE), jnp.bfloat16)],
        input_output_aliases=aliases,
        compiler_params=pltpu.CompilerParams(vmem_limit_bytes=VMEM),
        cost_estimate=pl.CostEstimate(
            flops=20 * count * row_count * col_count * FINE,
            bytes_accessed=8 * count * row_count * col_count,
            transcendentals=0,
        ),
        name="correlate",
    )(*operands)


def swap(value, axis, d):
    return lax.ppermute(value, axis, [(i, i ^ d) for i in range(lax.axis_size(axis))])


def after(values, earlier):
    if not earlier or not values:
        return list(values)
    return list(lax.optimization_barrier((tuple(values), tuple(earlier)))[0])


def shards(voltages, fir_taps):
    groups = lax.axis_size("freq")
    z, x, b = (lax.axis_index(name) for name in ("freq", "brow", "bcol"))
    streams = voltages.shape[1]
    block = streams * groups
    coarse = COARSE // groups
    known = []

    def note(value, parts):
        wanted = []
        for _, at, e in parts:
            row = None if e is None else (b ^ e) * block + at
            col = (x ^ 1) * block + at if e is None else x * block + at if e == 0 else None
            wanted.append((row, col))
        split = value.reshape((len(parts), -1) + value.shape[1:])
        known.append((split, parts[0][0], wanted))

    def fill(result, start, count, batch, mark=None):
        used = [
            (value, start - first, wanted)
            for value, first, wanted in known
            if first <= start < first + value.shape[1]
        ]
        return correlate(
            result, mark, used, start, count, coarse, 4 * block, 2 * block, batch
        )

    def join(pieces):
        return pieces[0][0] if len(pieces) == 1 else jnp.concatenate([p[0] for p in pieces], axis=0)

    def parts_of(pieces, e):
        return [(first, at, e) for _, parts in pieces for first, at in parts]

    freq_done, near_done = [], []

    def over_freq(pieces, earlier=()):
        values = after([piece[0] for piece, _ in pieces], freq_done + list(earlier))
        freq_done[:] = [swap(value, "freq", d) for value, (_, d) in zip(values, pieces)]
        return [(value, piece[1]) for value, (piece, _) in zip(freq_done, pieces)]

    def near(spread, inner, earlier=()):
        values = [join(spread)] if spread else []
        values += [join([piece for piece, _ in inner])] if inner else []
        values = after(values, near_done + list(earlier))
        near_done.clear()
        over_y = None
        if spread:
            value = values.pop(0)
            over_x, over_y = swap(value, "brow", 1), swap(value, "bcol", 2)
            near_done.extend([over_x, over_y])
            note(value, parts_of(spread, 0))
            note(over_x, parts_of(spread, None))
            note(over_y, parts_of(spread, 2))
            over_y = over_y, [part for _, parts in spread for part in parts]
        if inner:
            near_done.append(swap(values.pop(0), "bcol", 1))
            note(near_done[-1], [part for piece, e in inner for part in parts_of([piece], e ^ 1)])
        return over_y

    if streams == 2 * TILE and groups == 4:
        cut = coarse * 5 // 8

        def made(tile, cuts):
            local = channelize(voltages, fir_taps, tile, z[None], groups, cuts)
            return {
                (d, first): (local[d, first], [(first, (z ^ d) * streams + tile * TILE)])
                for d, first, _ in cuts
            }

        p = made(0, [(d, 0, coarse) for d in (2, 1, 3, 0)])
        own_a = p[0, 0]
        a2, a1 = over_freq([(p[2, 0], 2), (p[1, 0], 1)])
        y1 = near([own_a], [(own_a, 0)])
        both = [(d, first, count) for d in (2, 3) for first, count in ((0, cut), (cut, coarse - cut))]
        r = made(1, [(0, 0, coarse), (1, 0, coarse)] + both)
        own_b = r[0, 0]
        sent = list(freq_done)
        y2 = near([own_b], [(y1, 2)])
        a3, b1 = over_freq([(p[3, 0], 3), (r[1, 0], 1)], near_done)
        y3 = near([a1, a2], [(own_b, 0), (y2, 2), (a1, 0), (a2, 0)], sent)
        sent = freq_done + near_done
        b2, b3 = over_freq([(r[2, 0], 2), (r[3, 0], 3)], near_done)
        y4 = near([a3, b1], [(y3, 2), (a3, 0), (b1, 0)], sent)
        sent = freq_done + near_done
        c2, c3 = over_freq([(r[2, cut], 2), (r[3, cut], 3)], near_done)
        y5 = near([b2, b3], [(y4, 2)], sent)
        sent = freq_done + near_done
        near([], [(y5, 2), (b2, 0), (b3, 0)], sent)
        near_done.clear()
        y6 = near([c2, c3], [], sent)
        result, mark = fill(None, 0, cut, 4)
        y6 = after([y6[0]], [mark])[0], y6[1]
        near([], [(y6, 2), (c2, 0), (c3, 0)], [mark])
        result, _ = fill(result, cut, coarse - cut, 4, mark)
    else:
        padded = jnp.pad(voltages, ((0, 0), (0, -streams % TILE), (0, 0)))
        zero = jnp.zeros((1,), jnp.int32)
        cuts = [(d, 0, coarse) for d in range(groups)]
        local = [
            channelize(padded, fir_taps, tile, zero, groups, cuts)
            for tile in range(padded.shape[1] // TILE)
        ]
        local = jnp.concatenate(
            [jnp.concatenate([part[d, 0] for d in range(groups)], axis=0) for part in local], axis=1
        )[:, :streams]
        local = lax.all_to_all(local, "freq", 0, 1, tiled=True)
        own = local, [(0, jnp.int32(0))]
        over_y = near([own], [(own, 0)])
        near([], [(over_y, 2)])
        result, _ = fill(None, 0, coarse, 1)
    return result.reshape(2, coarse, 4 * block, 2, 1, block)


def solution(mesh):
    in_specs = (P(None, ("brow", "bcol", "freq"), None), P())
    out_specs = P(None, "freq", "brow", None, "bcol", None)
    return jax.shard_map(shards, mesh=mesh, in_specs=in_specs, out_specs=out_specs, check_vma=False)
```

```python
import functools
import math

import jax
import jax.numpy as jnp
import numpy as np
from jax import lax
from jax.experimental import pallas as pl
from jax.experimental.pallas import tpu as pltpu
from jax.sharding import PartitionSpec as P

CHANNELS = 4096
TAPS = 16
AVG = 32
FRAMES = 8
COARSE = CHANNELS // AVG
FINE = FRAMES * AVG
TILE = 16
LANES = 128
PITCH = TILE + 1
VMEM = 60 << 20
CHUNKS = 8


def dft_table():
    index = np.arange(COARSE)
    angle = 2.0 * math.pi * (index[:, None] * index[None, :] % COARSE) / COARSE
    cosine, sine = np.cos(angle) / 64.0, np.sin(angle) / 64.0
    table = np.block([[cosine, sine], [-sine, cosine]]).astype(np.float32)
    high = table.astype(jnp.bfloat16)
    low = (table - high.astype(np.float32)).astype(jnp.bfloat16)
    return np.concatenate([high, high, low], axis=1)


def twiddles():
    angle = 2.0 * math.pi * np.arange(AVG)[:, None] * np.arange(LANES)[None, :] / CHANNELS
    return np.cos(angle).astype(np.float32), np.sin(angle).astype(np.float32)


def times(value, numerator, length):
    re, im = value
    numerator %= length
    if numerator == 0:
        return re, im
    if 4 * numerator == length:
        return im, -re
    if 2 * numerator == length:
        return -re, -im
    if 4 * numerator == 3 * length:
        return -im, re
    cosine = math.cos(2.0 * math.pi * numerator / length)
    sine = math.sin(2.0 * math.pi * numerator / length)
    if 8 * numerator == length:
        return (re + im) * cosine, (im - re) * cosine
    if 8 * numerator == 3 * length:
        return (im - re) * sine, (re + im) * -sine
    return re * cosine + im * sine, im * cosine - re * sine


def small_dft(values):
    length = len(values)
    if length == 1:
        return values
    even, odd = small_dft(values[0::2]), small_dft(values[1::2])
    odd = [times(value, k, length) for k, value in enumerate(odd)]
    return [(e[0] + o[0], e[1] + o[1]) for e, o in zip(even, odd)] + [
        (e[0] - o[0], e[1] - o[1]) for e, o in zip(even, odd)
    ]


def channelize_kernel(pieces, tile, unroll, z_ref, v_hbm, taps_ref, cos_ref, sin_ref, table_ref, *refs):
    count = len(pieces)
    outs, stages = refs[:count], refs[count : 2 * count]
    v_ref, filt, g_ref, in_sem, out_sem = refs[2 * count :]
    chunk = CHANNELS // CHUNKS
    spans = FRAMES + TAPS - 1
    rows = pl.ds(tile * TILE, TILE)
    for k in range(CHUNKS):
        for f in range(spans):
            lanes = pl.ds(f * CHANNELS + k * chunk, chunk)
            pltpu.make_async_copy(
                v_hbm.at[:, rows, lanes], v_ref.at[:, :, lanes], in_sem.at[k]
            ).start()

    for k in range(CHUNKS):
        lanes = pl.ds(0, spans * chunk)
        pltpu.make_async_copy(v_hbm.at[:, rows, lanes], v_ref.at[:, :, lanes], in_sem.at[k]).wait()

        @pl.loop(k * (chunk // LANES), (k + 1) * (chunk // LANES))
        def _(j):
            lane = pl.multiple_of(j * LANES, LANES)
            taps = [
                jnp.broadcast_to(taps_ref[p : p + 1, pl.ds(lane, LANES)], (TILE, LANES))
                for p in range(TAPS)
            ]
            for c in range(2):
                total = [None] * FRAMES
                for f in range(spans):
                    v = v_ref[c, :, pl.ds(f * CHANNELS + lane, LANES)].astype(jnp.float32)
                    for t in range(max(0, f - TAPS + 1), min(FRAMES, f + 1)):
                        term = taps[f - t] * v
                        total[t] = term if f == t else total[t] + term
                        if f - t == TAPS - 1:
                            filt[c, j, pl.ds(t, TILE, stride=FRAMES), :] = total[t]

    def turned_fft(s):
        rows = pl.ds(pl.multiple_of(s * FRAMES, FRAMES), FRAMES)
        first = []
        for j0 in range(4):
            part = small_dft([(filt[0, j, rows, :], filt[1, j, rows, :]) for j in range(j0, AVG, 4)])
            first.append([times(value, j0 * ka, AVG) for ka, value in enumerate(part)])
        turned = [None] * AVG
        for ka in range(8):
            last = small_dft([first[j0][ka] for j0 in range(4)])
            for kb in range(4):
                k = ka + 8 * kb
                re, im = last[kb]
                if k:
                    cosine, sine = cos_ref[k : k + 1, :], sin_ref[k : k + 1, :]
                    re, im = re * cosine + im * sine, im * cosine - re * sine
                turned[k] = jnp.concatenate([re, im], axis=1)
        return turned

    @pl.loop(0, TILE, unroll=unroll)
    def _(s):
        value = jnp.concatenate(turned_fft(s), axis=0)
        high = value.astype(jnp.bfloat16)
        low = (value - high.astype(jnp.float32)).astype(jnp.bfloat16)
        spectrum = lax.dot_general(
            table_ref[...],
            jnp.concatenate([high, low, high], axis=1),
            (((1,), (1,)), ((), ())),
            preferred_element_type=jnp.float32,
        )
        for c in range(2):
            for h in range(FINE // LANES):
                g_ref[2 * c + h, pl.ds(s, COARSE, stride=PITCH), :] = spectrum[
                    c * COARSE : (c + 1) * COARSE, h * LANES : (h + 1) * LANES
                ]

    copies = []
    for n, ((d, start, size, width), out, stage) in enumerate(zip(pieces, outs, stages)):
        base = (z_ref[0] ^ d) * width + start

        @pl.loop(0, size, unroll=2)
        def _(q):
            at = pl.ds((base + q) * PITCH, TILE)
            stage[q] = jnp.concatenate([g_ref[i, at, :] for i in range(4)], axis=1).astype(
                jnp.bfloat16
            )

        copies.append(pltpu.make_async_copy(stage, out, out_sem.at[n]))
        copies[-1].start()
    for copy in copies:
        copy.wait()


def channelize(voltages, fir_taps, tile, z, groups, cuts):
    samples = voltages.shape[2]
    cosine, sine = twiddles()
    table = dft_table()
    whole = lambda shape: pl.BlockSpec(shape, lambda i: (0,) * len(shape))
    pieces = [(d, start, count, COARSE // groups) for d, start, count in cuts]
    shapes = [(count, TILE, 2 * FINE) for _, _, count, _ in pieces]
    outs = pl.pallas_call(
        functools.partial(channelize_kernel, pieces, tile, max(1, 2 - tile)),
        grid=(1,),
        in_specs=[
            pl.BlockSpec(memory_space=pltpu.SMEM),
            pl.BlockSpec(memory_space=pl.ANY),
            whole(fir_taps.shape),
            whole(cosine.shape),
            whole(sine.shape),
            whole(table.shape),
        ],
        out_specs=[pl.BlockSpec(memory_space=pl.ANY)] * len(shapes),
        out_shape=[jax.ShapeDtypeStruct(shape, jnp.bfloat16) for shape in shapes],
        scratch_shapes=[pltpu.VMEM(shape, jnp.bfloat16) for shape in shapes]
        + [
            pltpu.VMEM((2, TILE, samples), jnp.bfloat16),
            pltpu.VMEM((2, CHANNELS // LANES, TILE * FRAMES, LANES), jnp.float32),
            pltpu.VMEM((4, COARSE * PITCH, LANES), jnp.float32),
            pltpu.SemaphoreType.DMA((CHUNKS,)),
            pltpu.SemaphoreType.DMA((len(shapes),)),
        ],
        compiler_params=pltpu.CompilerParams(vmem_limit_bytes=VMEM),
        cost_estimate=pl.CostEstimate(
            flops=2 * 10**9, bytes_accessed=8 * 10**6, transcendentals=0
        ),
        name="channelize",
    )(z, voltages, fir_taps, jnp.asarray(cosine), jnp.asarray(sine), jnp.asarray(table))
    return {(d, start): out for (d, start, _, _), out in zip(pieces, outs)}


def correlate_kernel(batch, places, at_ref, *refs):
    groups, (out_ref, mark_ref, right) = refs[: len(places)], refs[-3:]
    mark_ref[...] = jnp.zeros_like(mark_ref)
    scale = 1.0 / FINE
    pieces = [
        (ref.at[n, 0], place) for ref, some in zip(groups, places) for n, place in enumerate(some)
    ]
    for q in range(batch):
        for ref, (_, col) in pieces:
            if col is not None:
                at = pl.multiple_of(at_ref[col], TILE)
                right[q, pl.ds(at, ref.shape[1]), :] = ref[q]
        rows = [(ref[q], row) for ref, (row, _) in pieces if row is not None]
        a, b = jnp.concatenate([value for value, _ in rows], axis=0), right[q]
        turned = jnp.concatenate([-b[:, FINE:], b[:, :FINE]], axis=1)
        parts = b.shape[0] // LANES
        for c, other in enumerate((b, turned)):
            product = scale * lax.dot_general(
                a, other, (((1,), (1,)), ((), ())), preferred_element_type=jnp.float32
            )
            start = 0
            for value, row in rows:
                size = value.shape[0]
                at = pl.multiple_of(at_ref[row] * parts, TILE * parts)
                for x in range(parts):
                    out_ref[c, q, pl.ds(at + x, size, stride=parts), :] = product[
                        start : start + size, x * LANES : (x + 1) * LANES
                    ]
                start += size


def correlate(result, mark, groups, start, count, coarse, row_count, col_count, batch):
    out_rows = row_count * col_count // LANES
    in_specs = [pl.BlockSpec(memory_space=pltpu.SMEM)]
    at, places = [], []
    for value, size, block, part, wanted in groups:
        shape = (size, 1, batch) + value.shape[3:]
        in_specs.append(
            pl.BlockSpec(shape, lambda i, block=block, part=part: (block, part, i, 0, 0))
        )
        places.append([])
        for pair in wanted:
            numbered = []
            for place in pair:
                numbered.append(None if place is None else len(at))
                at += [] if place is None else [place]
            places[-1].append(numbered)
    operands = [jnp.stack(at)] + [group[0] for group in groups]
    aliases = {}
    if result is not None:
        aliases = {len(operands): 0}
        operands += [result, mark]
        in_specs += [pl.BlockSpec(memory_space=pl.ANY)] * 2
    return pl.pallas_call(
        functools.partial(correlate_kernel, batch, places),
        grid=(count // batch,),
        in_specs=in_specs,
        out_specs=[
            pl.BlockSpec((2, batch, out_rows, LANES), lambda i: (0, i + start // batch, 0, 0)),
            pl.BlockSpec((8, LANES), lambda i: (0, 0)),
        ],
        out_shape=[
            jax.ShapeDtypeStruct((2, coarse, out_rows, LANES), jnp.float32),
            jax.ShapeDtypeStruct((8, LANES), jnp.float32),
        ],
        scratch_shapes=[pltpu.VMEM((batch, col_count, 2 * FINE), jnp.bfloat16)],
        input_output_aliases=aliases,
        compiler_params=pltpu.CompilerParams(vmem_limit_bytes=VMEM),
        cost_estimate=pl.CostEstimate(
            flops=20 * count * row_count * col_count * FINE,
            bytes_accessed=8 * count * row_count * col_count,
            transcendentals=0,
        ),
        name="correlate",
    )(*operands)


def swap(value, axis, d):
    return lax.ppermute(value, axis, [(i, i ^ d) for i in range(lax.axis_size(axis))])


def after(values, earlier):
    if not earlier or not values:
        return list(values)
    return list(lax.optimization_barrier((tuple(values), tuple(earlier)))[0])


def shards(voltages, fir_taps):
    groups = lax.axis_size("freq")
    z, x, b = (lax.axis_index(name) for name in ("freq", "brow", "bcol"))
    streams = voltages.shape[1]
    block = streams * groups
    coarse = COARSE // groups
    paired = streams == 2 * TILE and groups == 4
    unit = coarse // 2 if paired else coarse
    known = []

    def note(value, parts):
        offset, last = 0, None
        for units, at, e in parts:
            row = None if e is None else (b ^ e) * block + at
            col = (x ^ 1) * block + at if e is None else x * block + at if e == 0 else None
            if units != last:
                known.append((value, offset, units, []))
            known[-1][3].append((row, col))
            offset, last = offset + len(units), units

    def fill(result, which, batch, mark=None):
        used = []
        for value, offset, units, wanted in known:
            if which in units:
                split = value.reshape((-1, len(units), unit) + value.shape[1:])
                index = offset // len(units) // len(wanted)
                used.append((split, len(wanted), index, units.index(which), wanted))
        return correlate(
            result, mark, used, which * unit, unit, coarse, 4 * block, 2 * block, batch
        )

    def join(pieces):
        return pieces[0][0] if len(pieces) == 1 else jnp.concatenate([p[0] for p in pieces], axis=0)

    def parts_of(pieces, e):
        return [(units, at, e) for _, parts in pieces for units, at in parts]

    freq_done, near_done = [], []

    def over_freq(pieces, earlier=()):
        values = after([piece[0] for piece, _ in pieces], freq_done + list(earlier))
        freq_done[:] = [swap(value, "freq", d) for value, (_, d) in zip(values, pieces)]
        return [(value, piece[1]) for value, (piece, _) in zip(freq_done, pieces)]

    def near(spread, inner, earlier=()):
        values = [join(spread)] if spread else []
        values += [join([piece for piece, _ in inner])] if inner else []
        values = after(values, near_done + list(earlier))
        near_done.clear()
        over_y = None
        if spread:
            value = values.pop(0)
            over_x, over_y = swap(value, "brow", 1), swap(value, "bcol", 2)
            near_done.extend([over_x, over_y])
            note(value, parts_of(spread, 0))
            note(over_x, parts_of(spread, None))
            note(over_y, parts_of(spread, 2))
            over_y = over_y, [part for _, parts in spread for part in parts]
        if inner:
            near_done.append(swap(values.pop(0), "bcol", 1))
            note(near_done[-1], [part for piece, e in inner for part in parts_of([piece], e ^ 1)])
        return over_y

    if paired:

        def made(tile, cuts):
            local = channelize(voltages, fir_taps, tile, z[None], groups, cuts)
            return {
                (d, first): (
                    local[d, first],
                    [
                        (
                            (0, 1) if count == coarse else (first // unit,),
                            (z ^ d) * streams + tile * TILE,
                        )
                    ],
                )
                for d, first, count in cuts
            }

        p = made(0, [(d, 0, coarse) for d in (2, 1, 3, 0)])
        own_a = p[0, 0]
        a2, a1 = over_freq([(p[2, 0], 2), (p[1, 0], 1)])
        y1 = near([own_a], [(own_a, 0)])
        r = made(
            1, [(0, 0, coarse), (1, 0, coarse)] + [(d, at, unit) for d in (2, 3) for at in (0, unit)]
        )
        own_b = r[0, 0]
        a3, b1 = over_freq([(p[3, 0], 3), (r[1, 0], 1)])
        y2 = near([a1, a2], [(y1, 2), (a1, 0), (a2, 0)], [own_b[0]])
        sent = freq_done + near_done
        b2, b3 = over_freq([(r[2, 0], 2), (r[3, 0], 3)], near_done)
        y3 = near([a3, own_b], [(y2, 2), (a3, 0), (own_b, 0)], sent)
        sent = freq_done + near_done
        c2, c3 = over_freq([(r[2, unit], 2), (r[3, unit], 3)], near_done)
        y4 = near([b1, b2, b3], [(y3, 2), (b1, 0), (b2, 0), (b3, 0)], sent)
        y5 = near([c2, c3], [(y4, 2)], freq_done)
        result, mark = fill(None, 0, 4)
        y5 = after([y5[0]], [mark])[0], y5[1]
        near([], [(y5, 2), (c2, 0), (c3, 0)], [mark])
        result, _ = fill(result, 1, 4, mark)
    else:
        padded = jnp.pad(voltages, ((0, 0), (0, -streams % TILE), (0, 0)))
        zero = jnp.zeros((1,), jnp.int32)
        cuts = [(d, 0, coarse) for d in range(groups)]
        local = [
            channelize(padded, fir_taps, tile, zero, groups, cuts)
            for tile in range(padded.shape[1] // TILE)
        ]
        local = jnp.concatenate(
            [jnp.concatenate([part[d, 0] for d in range(groups)], axis=0) for part in local], axis=1
        )[:, :streams]
        local = lax.all_to_all(local, "freq", 0, 1, tiled=True)
        own = local, [((0,), jnp.int32(0))]
        over_y = near([own], [(own, 0)])
        near([], [(over_y, 2)])
        result, _ = fill(None, 0, 1)
    return result.reshape(2, coarse, 4 * block, 2, 1, block)


def solution(mesh):
    in_specs = (P(None, ("brow", "bcol", "freq"), None), P())
    out_specs = P(None, "freq", "brow", None, "bcol", None)
    return jax.shard_map(shards, mesh=mesh, in_specs=in_specs, out_specs=out_specs, check_vma=False)
```

```python
import functools
import math

import jax
import jax.numpy as jnp
import numpy as np
from jax import lax
from jax.experimental import pallas as pl
from jax.experimental.pallas import tpu as pltpu
from jax.sharding import PartitionSpec as P

CHANNELS = 4096
TAPS = 16
AVG = 32
FRAMES = 8
COARSE = CHANNELS // AVG
FINE = FRAMES * AVG
TILE = 16
LANES = 128
PITCH = TILE + 1
VMEM = 60 << 20
CHUNKS = 4


def dft_table():
    index = np.arange(COARSE)
    angle = 2.0 * math.pi * (index[:, None] * index[None, :] % COARSE) / COARSE
    cosine, sine = np.cos(angle) / 64.0, np.sin(angle) / 64.0
    table = np.block([[cosine, sine], [-sine, cosine]]).astype(np.float32)
    high = table.astype(jnp.bfloat16)
    low = (table - high.astype(np.float32)).astype(jnp.bfloat16)
    return np.concatenate([high, high, low], axis=1)


def twiddles():
    angle = 2.0 * math.pi * np.arange(AVG)[:, None] * np.arange(LANES)[None, :] / CHANNELS
    return np.cos(angle).astype(np.float32), np.sin(angle).astype(np.float32)


def times(value, numerator, length):
    re, im = value
    numerator %= length
    if numerator == 0:
        return re, im
    if 4 * numerator == length:
        return im, -re
    if 2 * numerator == length:
        return -re, -im
    if 4 * numerator == 3 * length:
        return -im, re
    cosine = math.cos(2.0 * math.pi * numerator / length)
    sine = math.sin(2.0 * math.pi * numerator / length)
    if 8 * numerator == length:
        return (re + im) * cosine, (im - re) * cosine
    if 8 * numerator == 3 * length:
        return (im - re) * sine, (re + im) * -sine
    return re * cosine + im * sine, im * cosine - re * sine


def small_dft(values):
    length = len(values)
    if length == 1:
        return values
    even, odd = small_dft(values[0::2]), small_dft(values[1::2])
    odd = [times(value, k, length) for k, value in enumerate(odd)]
    return [(e[0] + o[0], e[1] + o[1]) for e, o in zip(even, odd)] + [
        (e[0] - o[0], e[1] - o[1]) for e, o in zip(even, odd)
    ]


def channelize_kernel(pieces, tile, z_ref, v_hbm, taps_ref, cos_ref, sin_ref, table_ref, *refs):
    count = len(pieces)
    outs, stages = refs[:count], refs[count : 2 * count]
    v_ref, filt, g_ref, in_sem, out_sem = refs[2 * count :]
    chunk = CHANNELS // CHUNKS
    spans = FRAMES + TAPS - 1
    rows = pl.ds(tile * TILE, TILE)
    for k in range(CHUNKS):
        for f in range(spans):
            lanes = pl.ds(f * CHANNELS + k * chunk, chunk)
            pltpu.make_async_copy(
                v_hbm.at[:, rows, lanes], v_ref.at[:, :, lanes], in_sem.at[k]
            ).start()

    for k in range(CHUNKS):
        lanes = pl.ds(0, spans * chunk)
        pltpu.make_async_copy(v_hbm.at[:, rows, lanes], v_ref.at[:, :, lanes], in_sem.at[k]).wait()

        @pl.loop(k * (chunk // LANES), (k + 1) * (chunk // LANES))
        def _(j):
            lane = pl.multiple_of(j * LANES, LANES)
            taps = [
                jnp.broadcast_to(taps_ref[p : p + 1, pl.ds(lane, LANES)], (TILE, LANES))
                for p in range(TAPS)
            ]
            for c in range(2):
                total = [None] * FRAMES
                for f in range(spans):
                    v = v_ref[c, :, pl.ds(f * CHANNELS + lane, LANES)].astype(jnp.float32)
                    for t in range(max(0, f - TAPS + 1), min(FRAMES, f + 1)):
                        term = taps[f - t] * v
                        total[t] = term if f == t else total[t] + term
                        if f - t == TAPS - 1:
                            filt[c, j, pl.ds(t, TILE, stride=FRAMES), :] = total[t]

    def turned_fft(s):
        rows = pl.ds(pl.multiple_of(s * FRAMES, FRAMES), FRAMES)
        first = []
        for j0 in range(4):
            part = small_dft([(filt[0, j, rows, :], filt[1, j, rows, :]) for j in range(j0, AVG, 4)])
            first.append([times(value, j0 * ka, AVG) for ka, value in enumerate(part)])
        turned = [None] * AVG
        for ka in range(8):
            last = small_dft([first[j0][ka] for j0 in range(4)])
            for kb in range(4):
                k = ka + 8 * kb
                re, im = last[kb]
                if k:
                    cosine, sine = cos_ref[k : k + 1, :], sin_ref[k : k + 1, :]
                    re, im = re * cosine + im * sine, im * cosine - re * sine
                turned[k] = jnp.concatenate([re, im], axis=1)
        return turned

    @pl.loop(0, TILE, unroll=8)
    def _(s):
        value = jnp.concatenate(turned_fft(s), axis=0)
        high = value.astype(jnp.bfloat16)
        low = (value - high.astype(jnp.float32)).astype(jnp.bfloat16)
        spectrum = lax.dot_general(
            table_ref[...],
            jnp.concatenate([high, low, high], axis=1),
            (((1,), (1,)), ((), ())),
            preferred_element_type=jnp.float32,
        )
        for c in range(2):
            for h in range(FINE // LANES):
                g_ref[2 * c + h, pl.ds(s, COARSE, stride=PITCH), :] = spectrum[
                    c * COARSE : (c + 1) * COARSE, h * LANES : (h + 1) * LANES
                ]

    copies = []
    for n, ((d, start, size, width), out, stage) in enumerate(zip(pieces, outs, stages)):
        base = (z_ref[0] ^ d) * width + start

        @pl.loop(0, size, unroll=min(8, size))
        def _(q):
            at = pl.ds((base + q) * PITCH, TILE)
            stage[q] = jnp.concatenate([g_ref[i, at, :] for i in range(4)], axis=1).astype(
                jnp.bfloat16
            )

        copies.append(pltpu.make_async_copy(stage, out, out_sem.at[n]))
        copies[-1].start()
    for copy in copies:
        copy.wait()


def channelize(voltages, fir_taps, tile, z, groups, cuts):
    samples = voltages.shape[2]
    cosine, sine = twiddles()
    table = dft_table()
    whole = lambda shape: pl.BlockSpec(shape, lambda i: (0,) * len(shape))
    pieces = [(d, start, count, COARSE // groups) for d, start, count in cuts]
    shapes = [(count, TILE, 2 * FINE) for _, _, count, _ in pieces]
    outs = pl.pallas_call(
        functools.partial(channelize_kernel, pieces, tile),
        grid=(1,),
        in_specs=[
            pl.BlockSpec(memory_space=pltpu.SMEM),
            pl.BlockSpec(memory_space=pl.ANY),
            whole(fir_taps.shape),
            whole(cosine.shape),
            whole(sine.shape),
            whole(table.shape),
        ],
        out_specs=[pl.BlockSpec(memory_space=pl.ANY)] * len(shapes),
        out_shape=[jax.ShapeDtypeStruct(shape, jnp.bfloat16) for shape in shapes],
        scratch_shapes=[pltpu.VMEM(shape, jnp.bfloat16) for shape in shapes]
        + [
            pltpu.VMEM((2, TILE, samples), jnp.bfloat16),
            pltpu.VMEM((2, CHANNELS // LANES, TILE * FRAMES, LANES), jnp.float32),
            pltpu.VMEM((4, COARSE * PITCH, LANES), jnp.float32),
            pltpu.SemaphoreType.DMA((CHUNKS,)),
            pltpu.SemaphoreType.DMA((len(shapes),)),
        ],
        compiler_params=pltpu.CompilerParams(vmem_limit_bytes=VMEM),
        cost_estimate=pl.CostEstimate(
            flops=2 * 10**9, bytes_accessed=8 * 10**6, transcendentals=0
        ),
        name="channelize",
    )(z, voltages, fir_taps, jnp.asarray(cosine), jnp.asarray(sine), jnp.asarray(table))
    return {(d, start): out for (d, start, _, _), out in zip(pieces, outs)}


def correlate_kernel(batch, places, at_ref, *refs):
    groups, (out_ref, mark_ref, right) = refs[: len(places)], refs[-3:]
    mark_ref[...] = jnp.zeros_like(mark_ref)
    scale = 1.0 / FINE
    pieces = [
        (ref.at[n, 0], place) for ref, some in zip(groups, places) for n, place in enumerate(some)
    ]
    for q in range(batch):
        for ref, (_, col) in pieces:
            if col is not None:
                at = pl.multiple_of(at_ref[col], TILE)
                right[q, pl.ds(at, ref.shape[1]), :] = ref[q]
        rows = [(ref[q], row) for ref, (row, _) in pieces if row is not None]
        a, b = jnp.concatenate([value for value, _ in rows], axis=0), right[q]
        turned = jnp.concatenate([-b[:, FINE:], b[:, :FINE]], axis=1)
        parts = b.shape[0] // LANES
        for c, other in enumerate((b, turned)):
            product = scale * lax.dot_general(
                a, other, (((1,), (1,)), ((), ())), preferred_element_type=jnp.float32
            )
            start = 0
            for value, row in rows:
                size = value.shape[0]
                at = pl.multiple_of(at_ref[row] * parts, TILE * parts)
                for x in range(parts):
                    out_ref[c, q, pl.ds(at + x, size, stride=parts), :] = product[
                        start : start + size, x * LANES : (x + 1) * LANES
                    ]
                start += size


def correlate(result, mark, groups, start, count, coarse, row_count, col_count, batch, locate):
    out_rows = row_count * col_count // LANES
    in_specs = [pl.BlockSpec(memory_space=pltpu.SMEM)]
    at, places = [], []
    for value, size, block, part, wanted in groups:
        shape = (size, 1, batch) + value.shape[3:]
        in_specs.append(
            pl.BlockSpec(shape, lambda i, block=block, part=part: (block, part, i, 0, 0))
        )
        places.append([])
        for pair in wanted:
            numbered = []
            for place in pair:
                numbered.append(None if place is None else len(at))
                at += [] if place is None else [place]
            places[-1].append(numbered)
    operands = [locate(np.array(at, np.int32))] + [group[0] for group in groups]
    aliases = {}
    if result is not None:
        aliases = {len(operands): 0}
        operands += [result, mark]
        in_specs += [pl.BlockSpec(memory_space=pl.ANY)] * 2
    return pl.pallas_call(
        functools.partial(correlate_kernel, batch, places),
        grid=(count // batch,),
        in_specs=in_specs,
        out_specs=[
            pl.BlockSpec((2, batch, out_rows, LANES), lambda i: (0, i + start // batch, 0, 0)),
            pl.BlockSpec((8, LANES), lambda i: (0, 0)),
        ],
        out_shape=[
            jax.ShapeDtypeStruct((2, coarse, out_rows, LANES), jnp.float32),
            jax.ShapeDtypeStruct((8, LANES), jnp.float32),
        ],
        scratch_shapes=[pltpu.VMEM((batch, col_count, 2 * FINE), jnp.bfloat16)],
        input_output_aliases=aliases,
        compiler_params=pltpu.CompilerParams(vmem_limit_bytes=VMEM),
        cost_estimate=pl.CostEstimate(
            flops=20 * count * row_count * col_count * FINE,
            bytes_accessed=8 * count * row_count * col_count,
            transcendentals=0,
        ),
        name="correlate",
    )(*operands)


def swap(value, axis, d):
    return lax.ppermute(value, axis, [(i, i ^ d) for i in range(lax.axis_size(axis))])


def after(values, earlier):
    if not earlier or not values:
        return list(values)
    return list(lax.optimization_barrier((tuple(values), tuple(earlier)))[0])


def shards(voltages, fir_taps):
    groups = lax.axis_size("freq")
    z, x, b = (lax.axis_index(name) for name in ("freq", "brow", "bcol"))
    streams = voltages.shape[1]
    block = streams * groups
    coarse = COARSE // groups
    paired = streams == 2 * TILE and groups == 4
    unit = coarse // 2 if paired else coarse
    home = z if paired else jnp.int32(0)
    known = []

    def note(value, parts):
        offset, last = 0, None
        for units, at, e in parts:
            row = None if e is None else (1, e) + at
            col = (0, 1) + at if e is None else (0, 0) + at if e == 0 else None
            if units != last:
                known.append((value, offset, units, []))
            known[-1][3].append((row, col))
            offset, last = offset + len(units), units

    def locate(places):
        is_row, e, d, offset = places.T
        return ((b * is_row + x * (1 - is_row)) ^ e) * block + (home ^ d) * streams + offset

    def fill(result, which, batch, mark=None):
        used = []
        for value, offset, units, wanted in known:
            if which in units:
                split = value.reshape((-1, len(units), unit) + value.shape[1:])
                index = offset // len(units) // len(wanted)
                used.append((split, len(wanted), index, units.index(which), wanted))
        return correlate(
            result, mark, used, which * unit, unit, coarse, 4 * block, 2 * block, batch, locate
        )

    def join(pieces):
        return pieces[0][0] if len(pieces) == 1 else jnp.concatenate([p[0] for p in pieces], axis=0)

    def parts_of(pieces, e):
        return [(units, at, e) for _, parts in pieces for units, at in parts]

    freq_done, near_done = [], []

    def over_freq(pieces, earlier=()):
        values = after([piece[0] for piece, _ in pieces], freq_done + list(earlier))
        freq_done[:] = [swap(value, "freq", d) for value, (_, d) in zip(values, pieces)]
        return [(value, piece[1]) for value, (piece, _) in zip(freq_done, pieces)]

    def near(spread, inner, earlier=()):
        values = [join(spread)] if spread else []
        values += [join([piece for piece, _ in inner])] if inner else []
        values = after(values, near_done + list(earlier))
        near_done.clear()
        over_y = None
        if spread:
            value = values.pop(0)
            over_x, over_y = swap(value, "brow", 1), swap(value, "bcol", 2)
            near_done.extend([over_x, over_y])
            note(value, parts_of(spread, 0))
            note(over_x, parts_of(spread, None))
            note(over_y, parts_of(spread, 2))
            over_y = over_y, [part for _, parts in spread for part in parts]
        if inner:
            near_done.append(swap(values.pop(0), "bcol", 1))
            note(near_done[-1], [part for piece, e in inner for part in parts_of([piece], e ^ 1)])
        return over_y

    if paired:

        def made(tile, cuts):
            local = channelize(voltages, fir_taps, tile, z[None], groups, cuts)
            return {
                (d, first): (
                    local[d, first],
                    [
                        (
                            (0, 1) if count == coarse else (first // unit,),
                            (d, tile * TILE),
                        )
                    ],
                )
                for d, first, count in cuts
            }

        p = made(0, [(d, 0, coarse) for d in (2, 1, 3, 0)])
        own_a = p[0, 0]
        a2, a1 = over_freq([(p[2, 0], 2), (p[1, 0], 1)])
        y1 = near([own_a], [(own_a, 0)])
        r = made(
            1, [(0, 0, coarse), (1, 0, coarse)] + [(d, at, unit) for d in (2, 3) for at in (0, unit)]
        )
        own_b = r[0, 0]
        a3, b1 = over_freq([(p[3, 0], 3), (r[1, 0], 1)])
        y2 = near([a1, a2], [(y1, 2), (a1, 0), (a2, 0)], [own_b[0]])
        sent = freq_done + near_done
        b2, b3 = over_freq([(r[2, 0], 2), (r[3, 0], 3)], near_done)
        y3 = near([a3, own_b], [(y2, 2), (a3, 0), (own_b, 0)], sent)
        sent = freq_done + near_done
        c2, c3 = over_freq([(r[2, unit], 2), (r[3, unit], 3)], near_done)
        y4 = near([b1, b2, b3], [(y3, 2), (b1, 0), (b2, 0), (b3, 0)], sent)
        y5 = near([c2, c3], [(y4, 2)], freq_done)
        result, mark = fill(None, 0, 4)
        y5 = after([y5[0]], [mark])[0], y5[1]
        near([], [(y5, 2), (c2, 0), (c3, 0)], [mark])
        result, _ = fill(result, 1, 4, mark)
    else:
        padded = jnp.pad(voltages, ((0, 0), (0, -streams % TILE), (0, 0)))
        zero = jnp.zeros((1,), jnp.int32)
        cuts = [(d, 0, coarse) for d in range(groups)]
        local = [
            channelize(padded, fir_taps, tile, zero, groups, cuts)
            for tile in range(padded.shape[1] // TILE)
        ]
        local = jnp.concatenate(
            [jnp.concatenate([part[d, 0] for d in range(groups)], axis=0) for part in local], axis=1
        )[:, :streams]
        local = lax.all_to_all(local, "freq", 0, 1, tiled=True)
        own = local, [((0,), (0, 0))]
        over_y = near([own], [(own, 0)])
        near([], [(over_y, 2)])
        result, _ = fill(None, 0, 1)
    return result.reshape(2, coarse, 4 * block, 2, 1, block)


def solution(mesh):
    in_specs = (P(None, ("brow", "bcol", "freq"), None), P())
    out_specs = P(None, "freq", "brow", None, "bcol", None)
    return jax.shard_map(shards, mesh=mesh, in_specs=in_specs, out_specs=out_specs, check_vma=False)
```

```python
import functools
import math

import jax
import jax.numpy as jnp
import numpy as np
from jax import lax
from jax.experimental import pallas as pl
from jax.experimental.pallas import tpu as pltpu
from jax.sharding import PartitionSpec as P

CHANNELS = 4096
TAPS = 16
AVG = 32
FRAMES = 8
COARSE = CHANNELS // AVG
FINE = FRAMES * AVG
TILE = 16
LANES = 128
PITCH = TILE + 1
VMEM = 63 << 20
CHUNKS = 4


def dft_table():
    index = np.arange(COARSE)
    angle = 2.0 * math.pi * (index[:, None] * index[None, :] % COARSE) / COARSE
    cosine, sine = np.cos(angle) / 64.0, np.sin(angle) / 64.0
    table = np.block([[cosine, sine], [-sine, cosine]]).astype(np.float32)
    high = table.astype(jnp.bfloat16)
    low = (table - high.astype(np.float32)).astype(jnp.bfloat16)
    return np.concatenate([high, high, low], axis=1)


def twiddles():
    angle = 2.0 * math.pi * np.arange(AVG)[:, None] * np.arange(LANES)[None, :] / CHANNELS
    return np.cos(angle).astype(np.float32), np.sin(angle).astype(np.float32)


def times(value, numerator, length):
    re, im = value
    numerator %= length
    if numerator == 0:
        return re, im
    if 4 * numerator == length:
        return im, -re
    if 2 * numerator == length:
        return -re, -im
    if 4 * numerator == 3 * length:
        return -im, re
    cosine = math.cos(2.0 * math.pi * numerator / length)
    sine = math.sin(2.0 * math.pi * numerator / length)
    if 8 * numerator == length:
        return (re + im) * cosine, (im - re) * cosine
    if 8 * numerator == 3 * length:
        return (im - re) * sine, (re + im) * -sine
    return re * cosine + im * sine, im * cosine - re * sine


def small_dft(values):
    length = len(values)
    if length == 1:
        return values
    even, odd = small_dft(values[0::2]), small_dft(values[1::2])
    odd = [times(value, k, length) for k, value in enumerate(odd)]
    return [(e[0] + o[0], e[1] + o[1]) for e, o in zip(even, odd)] + [
        (e[0] - o[0], e[1] - o[1]) for e, o in zip(even, odd)
    ]


def channelize_kernel(pieces, tile, z_ref, v_hbm, taps_ref, cos_ref, sin_ref, table_ref, *refs):
    count = len(pieces)
    outs, stages = refs[:count], refs[count : 2 * count]
    v_ref, filt, g_ref, in_sem, out_sem = refs[2 * count :]
    chunk = CHANNELS // CHUNKS
    spans = FRAMES + TAPS - 1
    rows = pl.ds(tile * TILE, TILE)
    for k in range(CHUNKS):
        for f in range(spans):
            lanes = pl.ds(f * CHANNELS + k * chunk, chunk)
            pltpu.make_async_copy(
                v_hbm.at[:, rows, lanes], v_ref.at[:, :, lanes], in_sem.at[k]
            ).start()

    for k in range(CHUNKS):
        lanes = pl.ds(0, spans * chunk)
        pltpu.make_async_copy(v_hbm.at[:, rows, lanes], v_ref.at[:, :, lanes], in_sem.at[k]).wait()

        @pl.loop(k * (chunk // LANES), (k + 1) * (chunk // LANES))
        def _(j):
            lane = pl.multiple_of(j * LANES, LANES)
            taps = [
                jnp.broadcast_to(taps_ref[p : p + 1, pl.ds(lane, LANES)], (TILE, LANES))
                for p in range(TAPS)
            ]
            for c in range(2):
                total = [None] * FRAMES
                for f in range(spans):
                    v = v_ref[c, :, pl.ds(f * CHANNELS + lane, LANES)].astype(jnp.float32)
                    for t in range(max(0, f - TAPS + 1), min(FRAMES, f + 1)):
                        term = taps[f - t] * v
                        total[t] = term if f == t else total[t] + term
                        if f - t == TAPS - 1:
                            filt[c, j, pl.ds(t, TILE, stride=FRAMES), :] = total[t]

    def turned_fft(s):
        rows = pl.ds(pl.multiple_of(s * FRAMES, FRAMES), FRAMES)
        first = []
        for j0 in range(4):
            part = small_dft([(filt[0, j, rows, :], filt[1, j, rows, :]) for j in range(j0, AVG, 4)])
            first.append([times(value, j0 * ka, AVG) for ka, value in enumerate(part)])
        turned = [None] * AVG
        for ka in range(8):
            last = small_dft([first[j0][ka] for j0 in range(4)])
            for kb in range(4):
                k = ka + 8 * kb
                re, im = last[kb]
                if k:
                    cosine, sine = cos_ref[k : k + 1, :], sin_ref[k : k + 1, :]
                    re, im = re * cosine + im * sine, im * cosine - re * sine
                turned[k] = jnp.concatenate([re, im], axis=1)
        return turned

    @pl.loop(0, TILE, unroll=8)
    def _(s):
        value = jnp.concatenate(turned_fft(s), axis=0)
        high = value.astype(jnp.bfloat16)
        low = (value - high.astype(jnp.float32)).astype(jnp.bfloat16)
        spectrum = lax.dot_general(
            table_ref[...],
            jnp.concatenate([high, low, high], axis=1),
            (((1,), (1,)), ((), ())),
            preferred_element_type=jnp.float32,
        )
        for c in range(2):
            for h in range(FINE // LANES):
                g_ref[2 * c + h, pl.ds(s, COARSE, stride=PITCH), :] = spectrum[
                    c * COARSE : (c + 1) * COARSE, h * LANES : (h + 1) * LANES
                ]

    copies = []
    for n, ((d, start, size, width), out, stage) in enumerate(zip(pieces, outs, stages)):
        base = (z_ref[0] ^ d) * width + start

        @pl.loop(0, size, unroll=min(8, size))
        def _(q):
            at = pl.ds((base + q) * PITCH, TILE)
            stage[q] = jnp.concatenate([g_ref[i, at, :] for i in range(4)], axis=1).astype(
                jnp.bfloat16
            )

        copies.append(pltpu.make_async_copy(stage, out, out_sem.at[n]))
        copies[-1].start()
    for copy in copies:
        copy.wait()


def channelize(voltages, fir_taps, tile, z, groups, cuts):
    samples = voltages.shape[2]
    cosine, sine = twiddles()
    table = dft_table()
    whole = lambda shape: pl.BlockSpec(shape, lambda i: (0,) * len(shape))
    pieces = [(d, start, count, COARSE // groups) for d, start, count in cuts]
    shapes = [(count, TILE, 2 * FINE) for _, _, count, _ in pieces]
    outs = pl.pallas_call(
        functools.partial(channelize_kernel, pieces, tile),
        grid=(1,),
        in_specs=[
            pl.BlockSpec(memory_space=pltpu.SMEM),
            pl.BlockSpec(memory_space=pl.ANY),
            whole(fir_taps.shape),
            whole(cosine.shape),
            whole(sine.shape),
            whole(table.shape),
        ],
        out_specs=[pl.BlockSpec(memory_space=pl.ANY)] * len(shapes),
        out_shape=[jax.ShapeDtypeStruct(shape, jnp.bfloat16) for shape in shapes],
        scratch_shapes=[pltpu.VMEM(shape, jnp.bfloat16) for shape in shapes]
        + [
            pltpu.VMEM((2, TILE, samples), jnp.bfloat16),
            pltpu.VMEM((2, CHANNELS // LANES, TILE * FRAMES, LANES), jnp.float32),
            pltpu.VMEM((4, COARSE * PITCH, LANES), jnp.float32),
            pltpu.SemaphoreType.DMA((CHUNKS,)),
            pltpu.SemaphoreType.DMA((len(shapes),)),
        ],
        compiler_params=pltpu.CompilerParams(vmem_limit_bytes=VMEM),
        cost_estimate=pl.CostEstimate(
            flops=2 * 10**9, bytes_accessed=8 * 10**6, transcendentals=0
        ),
        name="channelize",
    )(z, voltages, fir_taps, jnp.asarray(cosine), jnp.asarray(sine), jnp.asarray(table))
    return {(d, start): out for (d, start, _, _), out in zip(pieces, outs)}


def correlate_kernel(batch, places, at_ref, *refs):
    groups, (out_ref, mark_ref, right) = refs[: len(places)], refs[-3:]
    mark_ref[...] = jnp.zeros_like(mark_ref)
    scale = 1.0 / FINE
    pieces = [
        (ref.at[n, 0], place) for ref, some in zip(groups, places) for n, place in enumerate(some)
    ]
    for q in range(batch):
        for ref, (_, col) in pieces:
            if col is not None:
                at = pl.multiple_of(at_ref[col], TILE)
                right[q, pl.ds(at, ref.shape[1]), :] = ref[q]
        rows = [(ref[q], row) for ref, (row, _) in pieces if row is not None]
        a, b = jnp.concatenate([value for value, _ in rows], axis=0), right[q]
        turned = jnp.concatenate([-b[:, FINE:], b[:, :FINE]], axis=1)
        parts = b.shape[0] // LANES
        for c, other in enumerate((b, turned)):
            product = scale * lax.dot_general(
                a, other, (((1,), (1,)), ((), ())), preferred_element_type=jnp.float32
            )
            start = 0
            for value, row in rows:
                size = value.shape[0]
                at = pl.multiple_of(at_ref[row] * parts, TILE * parts)
                for x in range(parts):
                    out_ref[c, q, pl.ds(at + x, size, stride=parts), :] = product[
                        start : start + size, x * LANES : (x + 1) * LANES
                    ]
                start += size


def correlate(result, mark, groups, start, count, coarse, row_count, col_count, batch, locate):
    out_rows = row_count * col_count // LANES
    in_specs = [pl.BlockSpec(memory_space=pltpu.SMEM)]
    at, places = [], []
    for value, size, block, part, wanted in groups:
        shape = (size, 1, batch) + value.shape[3:]
        in_specs.append(
            pl.BlockSpec(shape, lambda i, block=block, part=part: (block, part, i, 0, 0))
        )
        places.append([])
        for pair in wanted:
            numbered = []
            for place in pair:
                numbered.append(None if place is None else len(at))
                at += [] if place is None else [place]
            places[-1].append(numbered)
    operands = [locate(np.array(at, np.int32))] + [group[0] for group in groups]
    aliases = {}
    if result is not None:
        aliases = {len(operands): 0}
        operands += [result, mark]
        in_specs += [pl.BlockSpec(memory_space=pl.ANY)] * 2
    return pl.pallas_call(
        functools.partial(correlate_kernel, batch, places),
        grid=(count // batch,),
        in_specs=in_specs,
        out_specs=[
            pl.BlockSpec((2, batch, out_rows, LANES), lambda i: (0, i + start // batch, 0, 0)),
            pl.BlockSpec((8, LANES), lambda i: (0, 0)),
        ],
        out_shape=[
            jax.ShapeDtypeStruct((2, coarse, out_rows, LANES), jnp.float32),
            jax.ShapeDtypeStruct((8, LANES), jnp.float32),
        ],
        scratch_shapes=[pltpu.VMEM((batch, col_count, 2 * FINE), jnp.bfloat16)],
        input_output_aliases=aliases,
        compiler_params=pltpu.CompilerParams(vmem_limit_bytes=VMEM),
        cost_estimate=pl.CostEstimate(
            flops=20 * count * row_count * col_count * FINE,
            bytes_accessed=8 * count * row_count * col_count,
            transcendentals=0,
        ),
        name="correlate",
    )(*operands)


def swap(value, axis, d):
    return lax.ppermute(value, axis, [(i, i ^ d) for i in range(lax.axis_size(axis))])


def after(values, earlier):
    if not earlier or not values:
        return list(values)
    return list(lax.optimization_barrier((tuple(values), tuple(earlier)))[0])


def shards(voltages, fir_taps):
    groups = lax.axis_size("freq")
    z, x, b = (lax.axis_index(name) for name in ("freq", "brow", "bcol"))
    streams = voltages.shape[1]
    block = streams * groups
    coarse = COARSE // groups
    paired = streams == 2 * TILE and groups == 4
    unit = coarse // 2 if paired else coarse
    home = z if paired else jnp.int32(0)
    known = []

    def note(value, parts):
        offset, last = 0, None
        for units, at, e in parts:
            row = None if e is None else (1, e) + at
            col = (0, 1) + at if e is None else (0, 0) + at if e == 0 else None
            if units != last:
                known.append((value, offset, units, []))
            known[-1][3].append((row, col))
            offset, last = offset + len(units), units

    def locate(places):
        is_row, e, d, offset = places.T
        return ((b * is_row + x * (1 - is_row)) ^ e) * block + (home ^ d) * streams + offset

    def fill(result, which, batch, mark=None):
        used = []
        for value, offset, units, wanted in known:
            if which in units:
                split = value.reshape((-1, len(units), unit) + value.shape[1:])
                index = offset // len(units) // len(wanted)
                used.append((split, len(wanted), index, units.index(which), wanted))
        return correlate(
            result, mark, used, which * unit, unit, coarse, 4 * block, 2 * block, batch, locate
        )

    def join(pieces):
        return pieces[0][0] if len(pieces) == 1 else jnp.concatenate([p[0] for p in pieces], axis=0)

    def parts_of(pieces, e):
        return [(units, at, e) for _, parts in pieces for units, at in parts]

    freq_done, near_done = [], []

    def over_freq(pieces, earlier=()):
        values = after([piece[0] for piece, _ in pieces], freq_done + list(earlier))
        freq_done[:] = [swap(value, "freq", d) for value, (_, d) in zip(values, pieces)]
        return [(value, piece[1]) for value, (piece, _) in zip(freq_done, pieces)]

    def near(spread, inner, earlier=()):
        values = [join(spread)] if spread else []
        values += [join([piece for piece, _ in inner])] if inner else []
        values = after(values, near_done + list(earlier))
        near_done.clear()
        over_y = None
        if spread:
            value = values.pop(0)
            over_x, over_y = swap(value, "brow", 1), swap(value, "bcol", 2)
            near_done.extend([over_x, over_y])
            note(value, parts_of(spread, 0))
            note(over_x, parts_of(spread, None))
            note(over_y, parts_of(spread, 2))
            over_y = over_y, [part for _, parts in spread for part in parts]
        if inner:
            near_done.append(swap(values.pop(0), "bcol", 1))
            note(near_done[-1], [part for piece, e in inner for part in parts_of([piece], e ^ 1)])
        return over_y

    if paired:

        def made(tile, cuts):
            local = channelize(voltages, fir_taps, tile, z[None], groups, cuts)
            return {
                (d, first): (
                    local[d, first],
                    [
                        (
                            (0, 1) if count == coarse else (first // unit,),
                            (d, tile * TILE),
                        )
                    ],
                )
                for d, first, count in cuts
            }

        p = made(0, [(d, 0, coarse) for d in (2, 1, 3, 0)])
        own_a = p[0, 0]
        a2, a1 = over_freq([(p[2, 0], 2), (p[1, 0], 1)])
        y1 = near([own_a], [(own_a, 0)])
        r = made(
            1, [(0, 0, coarse), (1, 0, coarse)] + [(d, at, unit) for d in (2, 3) for at in (0, unit)]
        )
        own_b = r[0, 0]
        a3, b1 = over_freq([(p[3, 0], 3), (r[1, 0], 1)])
        y2 = near([a1, a2], [(y1, 2), (a1, 0), (a2, 0)], [own_b[0]])
        sent = freq_done + near_done
        b2, b3 = over_freq([(r[2, 0], 2), (r[3, 0], 3)], near_done)
        y3 = near([a3, own_b], [(y2, 2), (a3, 0), (own_b, 0)], sent)
        sent = freq_done + near_done
        c2, c3 = over_freq([(r[2, unit], 2), (r[3, unit], 3)], near_done)
        y4 = near([b1, b2, b3], [(y3, 2), (b1, 0), (b2, 0), (b3, 0)], sent)
        y5 = near([c2, c3], [(y4, 2)], freq_done)
        result, mark = fill(None, 0, 4)
        y5 = after([y5[0]], [mark])[0], y5[1]
        near([], [(y5, 2), (c2, 0), (c3, 0)], [mark])
        result, _ = fill(result, 1, 4, mark)
    else:
        padded = jnp.pad(voltages, ((0, 0), (0, -streams % TILE), (0, 0)))
        zero = jnp.zeros((1,), jnp.int32)
        cuts = [(d, 0, coarse) for d in range(groups)]
        local = [
            channelize(padded, fir_taps, tile, zero, groups, cuts)
            for tile in range(padded.shape[1] // TILE)
        ]
        local = jnp.concatenate(
            [jnp.concatenate([part[d, 0] for d in range(groups)], axis=0) for part in local], axis=1
        )[:, :streams]
        local = lax.all_to_all(local, "freq", 0, 1, tiled=True)
        own = local, [((0,), (0, 0))]
        over_y = near([own], [(own, 0)])
        near([], [(over_y, 2)])
        result, _ = fill(None, 0, 1)
    return result.reshape(2, coarse, 4 * block, 2, 1, block)


def solution(mesh):
    in_specs = (P(None, ("brow", "bcol", "freq"), None), P())
    out_specs = P(None, "freq", "brow", None, "bcol", None)
    return jax.shard_map(shards, mesh=mesh, in_specs=in_specs, out_specs=out_specs, check_vma=False)
```
